32 devices in a mesh: grp: 4 (over y, x), dp: 8 (over z, core).
Axes of the slice: x: 2, y: 2, z: 4, core: 2. Of those that a mesh axis runs over, the one named last changes fastest.
Arguments:
- tokens: bfloat16 [32, 1024, 1024], P(('grp', 'dp')), may hold values from -12 to 12
- cotangent: bfloat16 [32, 1024, 1024], P(('grp', 'dp')), may hold values from -6 to 6
- segment_ids: int32 [32, 1024], P(('grp', 'dp')), may hold values from 0 to 15, never falling along the last dimension, each value on 1 to 512 neighbouring positions
- in_weight: float32 [1024, 4384], P('grp'), may hold values from -0.1875 to 0.1875
- out_weight: float32 [2048, 1024], P('grp'), may hold values from -0.125 to 0.125
- filter_weight: float32 [4, 2304], P(None, 'grp'), may hold values from -3 to 3
- vectors: float32 [5472], P('grp'), may hold values from -7 to 3
- in_first: float32 [1024, 4384], P('grp'), may hold values from -512 to 512
- out_first: float32 [2048, 1024], P('grp'), may hold values from -1024 to 1024
- filter_first: float32 [4, 2304], P(None, 'grp'), may hold values from -320 to 320
- vector_first: float32 [5472], P('grp'), may hold values from -1024 to 1024
- in_second: float32 [1024, 4384], P('grp'), may hold values from 8192 to 32768
- out_second: float32 [2048, 1024], P('grp'), may hold values from 32768 to 131072
- filter_second: float32 [4, 2304], P(None, 'grp'), may hold values from 3276 to 13107
- vector_second: float32 [5472], P('grp'), may hold values from 32768 to 131072
Outputs:
- block_out: bfloat16 [32, 1024, 1024], P(('grp', 'dp'))
- token_grad: float32 [32, 1024, 1024], P(('grp', 'dp'))
- in_new: float32 [1024, 4384], P('grp')
- out_new: float32 [2048, 1024], P('grp')
- filter_new: float32 [4, 2304], P(None, 'grp')
- vectors_new: float32 [5472], P('grp')
- in_first_new: float32 [1024, 4384], P('grp')
- out_first_new: float32 [2048, 1024], P('grp')
- filter_first_new: float32 [4, 2304], P(None, 'grp')
- vector_first_new: float32 [5472], P('grp')
- in_second_new: float32 [1024, 4384], P('grp')
- out_second_new: float32 [2048, 1024], P('grp')
- filter_second_new: float32 [4, 2304], P(None, 'grp')
- vector_second_new: float32 [5472], P('grp')
The draws below stay inside these ranges and needn't reach their ends.
Inputs may be any that keep to these rules, and one draw needn't show every extreme that they name: `segment_ids`: along each row the ids never fall and every id appears; some document of each row has exactly 512 tokens.
All inputs are finite; a program needn't handle non-finite values.
Results may differ from the reference program's by a relative error of at most 0.012.
The reference program's roundings to bfloat16 on the way count: a program that leaves them out, or rounds other values in their place, can miss the bound.
Values may be sent and summed in bfloat16 or wider, within the bound.
A program may use at most 320 MiB of HBM per device.

```python
import math
import jax
import jax.numpy as jnp
import numpy as np
from jax import lax

D = 1024
H = 32
P_SIZE = 64
NSTATE = 128
KERNEL = 4
BLOCK = 256
DOCS = 16
STEP = 7
TOK_DEV = 1024
D_INNER = 2048
CONV_CH = 2304
PROJ = 4384
VEC = 5472
ROWS = 32
DEVICES = 32


def draw_vectors(key, part):
    key = jax.random.fold_in(key, 11)
    subkeys = jax.random.split(key, 6)
    pre_gain = jax.random.uniform(subkeys[0], (D,), jnp.float32, 0.5, 1.5)
    gate_gain = jax.random.uniform(subkeys[1], (D_INNER,), jnp.float32, 0.5, 1.5)
    filter_bias = jax.random.uniform(subkeys[2], (CONV_CH,), jnp.float32, -0.5, 0.5)
    step_init = jnp.exp(jax.random.uniform(subkeys[3], (H,), jnp.float32, math.log(0.001), math.log(0.1)))
    step_bias = step_init + jnp.log(-jnp.expm1(-step_init))
    decay_log = jnp.log(jax.random.uniform(subkeys[4], (H,), jnp.float32, 1.0, 16.0))
    skip_gain = jax.random.uniform(subkeys[5], (H,), jnp.float32, 0.5, 1.5)
    return jnp.concatenate([pre_gain, gate_gain, filter_bias, step_bias, decay_log, skip_gain])


def with_spikes(entries, stream_key, source, target, blocks, factor):
    def block_of(axis_at):
        return (jnp.arange(entries.shape[axis_at]) // (entries.shape[axis_at] // blocks)).reshape((-1,) + (1,) * (entries.ndim - 1 - axis_at))

    first = jax.random.permutation(stream_key, blocks)[block_of(target)]
    far = (block_of(target) + blocks // 2) % blocks
    return jnp.where((block_of(source) == first) | (block_of(source) == far), factor * entries, entries)


def shard_levels(key, dims, pieces, low, largest):
    def one(dim, shards_of):
        steps = jax.random.uniform(jax.random.fold_in(jax.random.fold_in(key, 6), dim), (shards_of,), jnp.float32, low / len(pieces), largest / len(pieces))
        return jnp.repeat(jnp.exp(steps), dims[dim] // shards_of).reshape((-1,) + (1,) * (len(dims) - dim - 1))

    gain = one(*pieces[0])
    for cut in pieces[1:]:
        gain = gain * one(*cut)
    return gain


def profile(amount, total, limit, skew):
    loads = [(1 << 20) // math.isqrt(grade ** skew) + 1 for grade in range(2, amount + 1)]
    surplus, counts = total - limit - (amount - 1), [1] * (amount - 1)
    while surplus > 0:
        candidates = [i for i in range(amount - 1) if counts[i] < limit]
        mass, remaining = sum([loads[i] for i in candidates]), surplus
        for i in candidates:
            extra = min(limit - counts[i], max(1, remaining * loads[i] // mass), surplus)
            counts[i] = counts[i] + extra
            surplus = surplus - extra
    return np.array([limit] + counts)


def uneven(stream_key, number_of, total, most, slope):
    if number_of == 2:
        one = jax.random.randint(stream_key, (), max(1, total - most), min(most, total - 1) + 1)
        return jnp.stack([one, total - one])
    sizes = jnp.asarray(profile(number_of, total, most, slope), jnp.int32)
    pairs = (number_of - 1) // 2
    giver, taker = sizes[1:1 + 2 * pairs:2], sizes[2:2 + 2 * pairs:2]
    room = jnp.minimum(giver - 1, most - taker)
    moved = jax.random.randint(jax.random.fold_in(stream_key, 1), (pairs,), 0, 1 << 20) % (room + 1)
    sizes = sizes.at[1:1 + 2 * pairs:2].set(giver - moved).at[2:2 + 2 * pairs:2].set(taker + moved)
    return sizes[jax.random.permutation(jax.random.fold_in(stream_key, 2), number_of)]


def noise(key, dims, scale, reach, cuts=(), kind=jnp.bfloat16):
    values = scale * jax.random.normal(key, dims, jnp.float32)
    if cuts:
        values = values * shard_levels(key, dims, cuts, -0.22, 0.18)
    return jnp.clip(values, -reach, reach).astype(kind)


def noise_with(rng, extent, width, most, cuts, heavy, kind=jnp.bfloat16):
    entries = width * jax.random.normal(rng, extent, jnp.float32)
    if cuts:
        entries = entries * shard_levels(rng, extent, cuts, -0.22, 0.18)
    return jnp.clip(with_spikes(entries, jax.random.fold_in(rng, 3), *heavy), -most, most).astype(kind)


def setup_inputs(seed: int = 0) -> dict:
    key_of = jax.random.split(jax.random.key(seed), 16)
    return {
        "tokens": noise_with(key_of[0], (ROWS, TOK_DEV, D), 1.0, 12.0, ((0, 32),), (0, 2, 32, 2.75)),
        "cotangent": noise(key_of[1], (ROWS, TOK_DEV, D), 1.0, 6.0, ((0, 32),)),
        "segment_ids": jax.vmap(lambda own: jnp.searchsorted(jnp.cumsum(uneven(own, DOCS, TOK_DEV, TOK_DEV // 2, 2)), jnp.arange(TOK_DEV), side="right"))(jax.random.split(key_of[2], ROWS)).reshape((ROWS, TOK_DEV)).astype(jnp.int32),
        "in_weight": noise(key_of[3], (D, PROJ), D ** -0.5, 0.1875, ((0, 4),), jnp.float32),
        "out_weight": noise(key_of[4], (D_INNER, D), D_INNER ** -0.5, 0.125, ((0, 4),), jnp.float32),
        "filter_weight": noise(key_of[5], (KERNEL, CONV_CH), KERNEL ** -0.5, 3.0, ((1, 4),), jnp.float32),
        "vectors": draw_vectors(jax.random.fold_in(key_of[15], 71), 0),
        "in_first": noise(key_of[7], (D, PROJ), ((TOK_DEV * DEVICES // 4) ** 0.5), 512.0, ((0, 4),), jnp.float32),
        "out_first": noise(key_of[8], (D_INNER, D), ((TOK_DEV * DEVICES) ** 0.5), 1024.0, ((0, 4),), jnp.float32),
        "filter_first": noise(key_of[9], (KERNEL, CONV_CH), ((TOK_DEV * DEVICES // 10) ** 0.5), 320.0, ((1, 4),), jnp.float32),
        "vector_first": noise(key_of[10], (VEC,), ((TOK_DEV * DEVICES) ** 0.5), 1024.0, ((0, 4),), jnp.float32),
        "in_second": jnp.clip(jnp.exp(math.log(32768.0) - 1.3862944 * jax.random.uniform(key_of[11], (D, PROJ), jnp.float32) ** shard_levels(key_of[11], (D, PROJ), ((0, 4),), -0.2, 0.2)), 8192.0, 32768.0),
        "out_second": jnp.clip(jnp.exp(math.log(131072.0) - 1.3862944 * jax.random.uniform(key_of[12], (D_INNER, D), jnp.float32) ** shard_levels(key_of[12], (D_INNER, D), ((0, 4),), -0.2, 0.2)), 32768.0, 131072.0),
        "filter_second": jnp.clip(jnp.exp(math.log(13107.0) - 1.3865233 * jax.random.uniform(key_of[13], (KERNEL, CONV_CH), jnp.float32) ** shard_levels(key_of[13], (KERNEL, CONV_CH), ((1, 4),), -0.2, 0.2)), 3276.0, 13107.0),
        "vector_second": jnp.clip(jnp.exp(math.log(131072.0) - 1.3862944 * jax.random.uniform(key_of[14], (VEC,), jnp.float32) ** shard_levels(key_of[14], (VEC,), ((0, 4),), -0.2, 0.2)), 32768.0, 131072.0),
    }


EPSILON = 1e-05
ADAM_EPSILON = 1e-08
BETA_FIRST = 0.5
BETA_SECOND = 0.5
WEIGHT_DECAY = 0.1

@jax.custom_vjp
def low(v):
    return lax.optimization_barrier(v.astype(jnp.bfloat16)).astype(jnp.float32)

@jax.custom_vjp
def low_back(v):
    return v

def low_keep(v):
    return (low(v), None)

def low_pass(kept, grad):
    return (grad,)

def back_keep(v):
    return (v, None)

def back_low(kept, grad):
    return (low(grad),)
low.defvjp(low_keep, low_pass)
low_back.defvjp(back_keep, back_low)

def state_scan(inputs, bmat, cmat, step_size, decay_rate, skip_gain, segment):
    highest = lax.Precision.HIGHEST
    length = inputs.shape[0]
    count = length // BLOCK
    x_blocks = inputs.reshape(count, BLOCK, H, P_SIZE)
    b_blocks = bmat.reshape(count, BLOCK, NSTATE)
    c_blocks = cmat.reshape(count, BLOCK, NSTATE)
    step_blocks = jnp.swapaxes(step_size.reshape(count, BLOCK, H), 1, 2)
    seg_blocks = segment.reshape(count, BLOCK)
    cumulative = jnp.cumsum(step_blocks * decay_rate[None, :, None], axis=2)
    positions = jnp.arange(BLOCK)
    same_mask = (seg_blocks[:, :, None] == seg_blocks[:, None, :]) & (positions[:, None] >= positions[None, :])
    same_mask = same_mask[:, None]
    differences = cumulative[:, :, :, None] - cumulative[:, :, None, :]
    decay_matrix = jnp.where(same_mask, jnp.exp(jnp.where(same_mask, differences, 0.0)), 0.0)
    scores = jnp.einsum('ctn,csn->cts', c_blocks, b_blocks, precision=highest)
    weights = scores[:, None] * decay_matrix * step_blocks[:, :, None, :]
    inner_part = jnp.einsum('chts,cshp->cthp', weights, x_blocks, precision=highest)
    last_cumsum = cumulative[:, :, -1:]
    tail_weight = jnp.exp(last_cumsum - cumulative) * step_blocks * (seg_blocks == seg_blocks[:, -1:]).astype(inputs.dtype)[:, None, :]
    weighted_x = x_blocks * jnp.swapaxes(tail_weight, 1, 2)[..., None]
    local_state = jnp.einsum('cshp,csn->chpn', weighted_x, b_blocks, precision=highest)
    block_ends = seg_blocks[:, -1]
    before_ends = jnp.concatenate([jnp.full((1,), -1, jnp.int32), block_ends[:-1]])
    keep_state = (block_ends == before_ends).astype(inputs.dtype)
    fade_rate = jnp.exp(last_cumsum[:, :, 0]) * keep_state[:, None]

    def advance(carried_state, block_item):
        fade_now, local_now = block_item
        return (fade_now[:, None, None] * carried_state + local_now, carried_state)
    start_state = jnp.zeros((H, P_SIZE, NSTATE), inputs.dtype)
    unused_state, entering = lax.scan(advance, start_state, (fade_rate, local_state))
    reach_mask = (seg_blocks == before_ends[:, None]).astype(inputs.dtype)
    carried_part = jnp.einsum('ctn,chpn->cthp', c_blocks, entering, precision=highest)
    carried_part = carried_part * (jnp.exp(jnp.swapaxes(cumulative, 1, 2)) * reach_mask[:, :, None])[..., None]
    result = inner_part + carried_part + skip_gain[None, None, :, None] * x_blocks
    return result.reshape(length, H, P_SIZE)

def mixer(projected, filter_taps, vector_vals, segment):
    length = projected.shape[0]
    gate_in = projected[:, :D_INNER]
    conv_in = projected[:, D_INNER:D_INNER + CONV_CH]
    step_raw = projected[:, D_INNER + CONV_CH:]
    first_end = D + D_INNER
    bias_end = first_end + CONV_CH
    padded = jnp.concatenate([jnp.zeros((KERNEL - 1, CONV_CH), projected.dtype), conv_in], 0)
    seg_padded = jnp.concatenate([jnp.full((KERNEL - 1,), -1, jnp.int32), segment])
    filtered = jnp.zeros((length, CONV_CH), projected.dtype) + vector_vals[first_end:bias_end]
    for offset in range(KERNEL):
        shifted = padded[KERNEL - 1 - offset:KERNEL - 1 - offset + length]
        same_doc = (seg_padded[KERNEL - 1 - offset:KERNEL - 1 - offset + length] == segment).astype(projected.dtype)
        filtered = filtered + shifted * same_doc[:, None] * filter_taps[offset]
    activated = jax.nn.silu(filtered)
    inputs = activated[:, :D_INNER].reshape(length, H, P_SIZE)
    bmat = activated[:, D_INNER:D_INNER + NSTATE]
    cmat = activated[:, D_INNER + NSTATE:]
    step_size = jax.nn.softplus(step_raw + vector_vals[bias_end:bias_end + H])
    decay_rate = -jnp.exp(vector_vals[bias_end + H:bias_end + 2 * H])
    skip_gain = vector_vals[bias_end + 2 * H:]
    scanned = state_scan(inputs, bmat, cmat, step_size, decay_rate, skip_gain, segment).reshape(length, D_INNER)
    gated = scanned * jax.nn.silu(gate_in)
    return gated * lax.rsqrt(lax.optimization_barrier(jnp.mean(gated * gated, -1, keepdims=True)) + EPSILON) * vector_vals[D:first_end]

def one_row(in_copy, out_copy, filter_copy, vector_copy, row_feats, row_seg):
    highest = lax.Precision.HIGHEST
    normed = row_feats * lax.rsqrt(lax.optimization_barrier(jnp.mean(row_feats * row_feats, -1, keepdims=True)) + EPSILON) * vector_copy[:D]
    projected = low_back(jnp.dot(low(normed), in_copy, precision=highest, preferred_element_type=jnp.float32))
    mixed = low(mixer(projected, filter_copy, vector_copy, row_seg))
    return row_feats + jnp.dot(mixed, out_copy, precision=highest, preferred_element_type=jnp.float32)

def adam_step(master, first, second, grad, rate):
    first_new = BETA_FIRST * first + (1.0 - BETA_FIRST) * grad
    second_new = BETA_SECOND * second + (1.0 - BETA_SECOND) * grad * grad
    first_fix = 1.0 - BETA_FIRST ** STEP
    second_fix = 1.0 - BETA_SECOND ** STEP
    master_new = master - rate * (first_new / first_fix / (jnp.sqrt(second_new / second_fix) + ADAM_EPSILON) + WEIGHT_DECAY * master)
    return (master_new, first_new, second_new)

def reference(tokens, cotangent, segment_ids, in_weight, out_weight, filter_weight, vectors, in_first, out_first, filter_first, vector_first, in_second, out_second, filter_second, vector_second):
    row_function = jax.checkpoint(one_row)

    def forward(in_master, out_master, filter_master, vector_master, features):
        in_copy = low(in_master)
        out_copy = low(out_master)
        filter_copy = low(filter_master)
        vector_copy = low(vector_master)

        def apply_row(row_pair):
            return row_function(in_copy, out_copy, filter_copy, vector_copy, row_pair[0], row_pair[1])
        return lax.map(apply_row, (features, segment_ids))
    outputs, pullback = jax.vjp(forward, in_weight, out_weight, filter_weight, vectors, tokens.astype(jnp.float32))
    grad_in, grad_out, grad_filter, grad_vectors, token_grad = pullback(cotangent.astype(jnp.float32))
    in_new, in_first_new, in_second_new = adam_step(in_weight, in_first, in_second, grad_in, 0.03)
    out_new, out_first_new, out_second_new = adam_step(out_weight, out_first, out_second, grad_out, 0.02)
    filter_new, filter_first_new, filter_second_new = adam_step(filter_weight, filter_first, filter_second, grad_filter, 0.3)
    vectors_new, vector_first_new, vector_second_new = adam_step(vectors, vector_first, vector_second, grad_vectors, 0.3)
    return (outputs.astype(jnp.bfloat16), token_grad, in_new, out_new, filter_new, vectors_new, in_first_new, out_first_new, filter_first_new, vector_first_new, in_second_new, out_second_new, filter_second_new, vector_second_new)
```

```python
import functools
import math

import jax
import jax.numpy as jnp
from jax import lax
from jax.experimental import pallas as pl
from jax.experimental.pallas import tpu as pltpu
from jax.sharding import PartitionSpec as P

D = 1024
H = 32
P_SIZE = 64
NSTATE = 128
KERNEL = 4
STEP = 7
D_INNER = 2048
CONV_CH = 2304
XBC = D_INNER + CONV_CH
LANES = 128
T = 256
W = 256
HPT = W // P_SIZE
NT = D_INNER // W
CT = CONV_CH // W
SMALL_COLS = 1408
CHUNK = 32
HEADS_AT = D + D_INNER + CONV_CH
VEC = HEADS_AT + 3 * H
VEC_PAD = 5504
STEP_AT = D_INNER + CONV_CH
ALL = STEP_AT + LANES
LOG2E = math.log2(math.e)

EPSILON = 1e-05
ADAM_EPSILON = 1e-08
BETA_FIRST = 0.5
BETA_SECOND = 0.5
WEIGHT_DECAY = 0.1

F32 = jnp.float32
BF16 = jnp.bfloat16
HIGHEST = lax.Precision.HIGHEST
VMEM_LIMIT = 58 * 1024 * 1024


def dot_nn(a, b):
    return lax.dot_general(a, b, (((1,), (0,)), ((), ())), preferred_element_type=F32)


def dot_nt(a, b):
    return lax.dot_general(a, b, (((1,), (1,)), ((), ())), preferred_element_type=F32)


def dot_tn(a, b):
    return lax.dot_general(a, b, (((0,), (0,)), ((), ())), preferred_element_type=F32)


def sigmoid(v):
    return 0.5 * jnp.tanh(0.5 * v) + 0.5


def rows8(v):
    return jnp.sum(v.reshape(v.shape[0] // 8, 8, v.shape[1]), axis=0)


def tile_of(i):
    return slice(i * W, (i + 1) * W)


def tile_at(i, width=W):
    return pl.ds(pl.multiple_of(i * width, width), width)


def whole(shape):
    zeros = (0,) * len(shape)
    return pl.BlockSpec(shape, lambda *_: zeros, pipeline_mode=pl.Buffered(1))


MESH = pl.DeviceIdType.MESH
HOPS = (("dp", 1), ("grp", 1), ("grp", 2), ("dp", 2), ("dp", 4))
CORE, ALONG_X, ALONG_Y, Z_NEAR, Z_FAR = range(5)


def bit(hop):
    name, size = HOPS[hop]
    return lax.rem(lax.div(lax.axis_index(name), size), 2)


def across(hop):
    name, size = HOPS[hop]
    return {name: lax.axis_index(name) + size * (1 - 2 * bit(hop))}


def greet(hops):
    barrier = pltpu.get_barrier_semaphore()
    for hop in hops:
        pl.semaphore_signal(barrier, inc=1, device_id=across(hop), device_id_type=MESH)
    pl.semaphore_wait(barrier, len(hops))


def rows_at(start, size):
    return pl.ds(pl.multiple_of(start, size), size)


def add_rows(out, a, b):
    out[...] = a[...] + b[...]


def reduce_chunk(src, cols, first_x, bufs, total, sends, recvs, index, local_sem):
    own, r1, r2, r3, r4, r0 = bufs
    rows = src.shape[2]
    half, quarter, eighth = rows // 2, rows // 4, rows // 8
    c, x, y, z1, z2 = (bit(hop) for hop in range(5))
    first, second = (ALONG_X, ALONG_Y) if first_x else (ALONG_Y, ALONG_X)
    base = c * half
    base1 = base + z1 * quarter
    base2 = base1 + z2 * eighth

    def copy(n, hop, a, b):
        return pltpu.make_async_remote_copy(
            src_ref=a, dst_ref=b, send_sem=sends.at[index, n], recv_sem=recvs.at[index, n],
            device_id=across(hop), device_id_type=MESH,
        )

    def pair(u):
        return own.at[:, u] if first_x else own.at[u]

    kept = bit(first)
    load = pltpu.make_async_copy(src.at[:, :, rows_at(base, half), cols], own, local_sem)
    here = [total.at[rows_at(base2, eighth)], total.at[rows_at(base1, quarter)], total.at[rows_at(base, half)]]
    copies = [
        copy(0, CORE, src.at[:, :, rows_at((1 - c) * half, half), cols], r0),
        copy(1, first, pair(1 - kept), r1),
        copy(2, second, r1.at[1 - bit(second)], r2),
        copy(3, Z_NEAR, r2.at[rows_at((1 - z1) * quarter, quarter)], r3),
        copy(4, Z_FAR, r3.at[rows_at((1 - z2) * eighth, eighth)], r4),
        copy(5, Z_FAR, here[0], here[0]),
        copy(6, Z_NEAR, here[1], here[1]),
        copy(7, CORE, here[2], here[2]),
    ]

    def begin():
        load.start()
        copies[0].start()

    def after_core():
        load.wait()
        copies[0].wait_recv()
        add_rows(own, own, r0)
        copies[1].start()

    def after_first():
        copies[1].wait_recv()
        add_rows(r1, r1, pair(kept))
        copies[2].start()

    def after_second():
        copies[2].wait_recv()
        add_rows(r2, r2, r1.at[bit(second)])
        copies[3].start()

    def after_near():
        copies[3].wait_recv()
        add_rows(r3, r3, r2.at[rows_at(z1 * quarter, quarter)])
        copies[4].start()

    def after_far():
        copies[4].wait_recv()
        add_rows(here[0], r4, r3.at[rows_at(z2 * eighth, eighth)])
        copies[5].start()

    def gather_far():
        copies[5].wait_recv()
        copies[6].start()

    def gather_near():
        copies[6].wait_recv()
        copies[7].start()

    def arrive():
        copies[7].wait_recv()

    def finish():
        for one in copies:
            one.wait_send()

    return (begin, after_core, after_first, after_second, after_near, after_far, gather_far, gather_near, arrive), finish


def reduce_buffers(rows, cols, count, dtype=BF16):
    half = rows // 2
    shapes = [
        (2, 2, half, cols), (2, 2, half, cols), (2, half, cols), (half, cols), (half // 2, cols), (half // 4, cols), (rows, cols),
    ]
    return [pltpu.VMEM((count, *shape), dtype) for shape in shapes]


BUFFERS = 7
STAGES = 9


def reduce_plan(src, starts, size, slots, pace, bufs, result, sems, base, x_first):
    local_sems, out_sems, sends, recvs = sems
    ticks, ends = [], []
    for n, (start, slot) in enumerate(zip(starts, slots)):
        index = base + n
        own, r0, r1, r2, r3, r4, total = (ref.at[n] for ref in bufs)
        cols = pl.ds(start, size)
        stages, finish = reduce_chunk(
            src, cols, x_first[n], (own, r1, r2, r3, r4, r0), total, sends, recvs, index, local_sems.at[index]
        )
        write = pltpu.make_async_copy(total, result.at[:, cols], out_sems.at[index])
        for later, stage in zip(pace, stages):
            ticks.append((slot + later, stage))
        ticks.append((slot + pace[-1], write.start))
        ends += [finish, write.wait]
    return ticks, ends


def small_plan(src, bufs, total, sems, slot, spacing):
    sends, recvs = sems
    r0, a1, r1, a2, r2, a3, r3, a4, r4 = bufs
    x, y = bit(ALONG_X), bit(ALONG_Y)

    def copy(n, hop, a, b):
        return pltpu.make_async_remote_copy(
            src_ref=a, dst_ref=b, send_sem=sends.at[n], recv_sem=recvs.at[n], device_id=across(hop), device_id_type=MESH
        )

    copies = [
        copy(0, CORE, src, r0),
        copy(1, ALONG_X, a1.at[:, 1 - x], r1),
        copy(2, ALONG_Y, a2.at[1 - y], r2),
        copy(3, Z_NEAR, a3, r3),
        copy(4, Z_FAR, a4, r4),
    ]

    def after(n, out, one, other):
        def stage():
            copies[n].wait_recv()
            out[...] = one[...] + other[...]
            if n < 4:
                copies[n + 1].start()

        return stage

    stages = [
        copies[0].start,
        after(0, a1, src, r0),
        after(1, a2, a1.at[:, x], r1),
        after(2, a3, a2.at[y], r2),
        after(3, a4, a3, r3),
        after(4, total, a4, r4),
    ]
    return [(slot + k * spacing, stage) for k, stage in enumerate(stages)], [one.wait_send for one in copies]


def small_buffers(rows, cols):
    shapes = [(2, 2, rows, cols), (2, 2, rows, cols), (2, rows, cols), (2, rows, cols)] + [(rows, cols)] * 5
    return [pltpu.VMEM(shape, F32) for shape in shapes]


def by_slot(ticks):
    slots = {}
    for slot, action in ticks:
        slots.setdefault(slot, []).append(action)
    return slots


def head_terms(sraw_ref, hv_ref):
    v = sraw_ref[...] + hv_ref[0:1, :]
    step = jnp.maximum(v, 0.0) + jnp.log1p(jnp.exp(-jnp.abs(v)))
    rate = -jnp.exp(hv_ref[1:2, :])
    return v, step, rate


def before(rows, cols):
    return lax.broadcasted_iota(jnp.int32, (rows, cols), 0), lax.broadcasted_iota(jnp.int32, (rows, cols), 1)


def cumulate(logdecay):
    t, s = before(T, T)
    lower = jnp.where(s <= t, 1.0, 0.0)
    return jnp.dot(lower, logdecay * LOG2E, precision=HIGHEST, preferred_element_type=F32)


def spread(cum, cum_b):
    for h in range(H):
        cum_b[h] = jnp.broadcast_to(cum[:, h : h + 1], (T, LANES))


def expand(values, fan, out):
    high = values.astype(BF16)
    low = (values - high.astype(F32)).astype(BF16)
    both = jnp.concatenate([high, low], axis=1)
    for c in range(0, D_INNER, 2 * W):
        out[:, c : c + 2 * W] = dot_nn(both, fan[:, c : c + 2 * W])


def set_fan(fan):
    for c in range(0, D_INNER, W):
        row, lane = before(2 * LANES, W)
        fan[:, c : c + W] = jnp.where(lax.shift_right_logical(lane + c, 6) == (row & (LANES - 1)), 1.0, 0.0).astype(BF16)


def put_diagonal(diag, r, tile):
    lane = lax.broadcasted_iota(jnp.int32, (tile.shape[0], LANES), 1)
    first = jnp.where(lane < P_SIZE, 1.0, 0.0).astype(BF16)
    second = jnp.where(lane < P_SIZE, 0.0, 1.0).astype(BF16)
    for k in range(HPT):
        at = LANES * (k // 2)
        part = tile[:, at : at + LANES]
        diag[k * T + r : k * T + r + tile.shape[0], at : at + LANES] = part * (first if k % 2 == 0 else second)


def from_start_last(cum_b, i):
    lane = lax.broadcasted_iota(jnp.int32, (1, LANES), 1)
    last = slice(T - 1, T)
    halves = [jnp.where(lane < P_SIZE, cum_b[HPT * i + 2 * k, last], cum_b[HPT * i + 2 * k + 1, last]) for k in range(2)]
    return jnp.exp2(jnp.concatenate(halves, axis=1))


def wide(m):
    return jnp.concatenate([m, m], axis=1)


def split_halves(values, high_ref, low_ref, rows):
    high = values.astype(BF16)
    high_ref[rows] = high
    low_ref[rows] = (values - high.astype(F32)).astype(BF16)


def head_sums(high_ref, low_ref, pick):
    return dot_nn(high_ref[...], pick) + dot_nn(low_ref[...], pick)


def set_pick(pick):
    for r in range(0, D_INNER, T):
        row, lane = before(T, LANES)
        pick[r : r + T] = jnp.where(lax.shift_right_logical(row + r, 6) == lane, 1.0, 0.0).astype(BF16)


def chunks(start=0, stop=T):
    return [slice(r, r + CHUNK) for r in range(start, stop, CHUNK)]


def scan_forward(block, act, sraw_ref, segb_ref, seg_ref, hv_ref, skip_ref, y_ref, st_ref, scratch):
    (
        state, cum_b, fan, wcat, cum_rows, xw_scr, carr_scr, diag, scores, prev_seg, step_f, from_start, to_end,
    ) = scratch
    tokens = rows_at(block * T, T)

    @pl.when(block == 0)
    def _():
        state[...] = jnp.zeros_like(state)
        wcat[...] = jnp.zeros_like(wcat)
        diag[...] = jnp.zeros_like(diag)
        prev_seg[...] = jnp.full(prev_seg.shape, -1.0, F32)
        set_fan(fan)

    _, step, rate = head_terms(sraw_ref.at[tokens], hv_ref)
    cum = cumulate(step * rate)
    cum_rows[...] = cum.T
    spread(cum, cum_b)
    bmat = act[tokens, D_INNER : D_INNER + NSTATE]
    cmat = act[tokens, D_INNER + NSTATE : CONV_CH]
    segb = segb_ref[tokens]
    t_at, s_at = before(T, T)
    valid = (wide(segb) == seg_ref[0:1, tokens].astype(F32)) & (s_at <= t_at)
    scores[...] = jnp.where(valid, dot_nt(cmat, bmat), 0.0).astype(BF16)
    prev = prev_seg[0:1]
    last_seg = segb[T - 1 : T]
    last = cum[T - 1 : T]
    expand(step, fan, step_f)
    expand(jnp.exp2(cum) * jnp.where(segb == prev, 1.0, 0.0), fan, from_start)
    expand(jnp.exp2(last - cum) * jnp.where(segb == last_seg, 1.0, 0.0), fan, to_end)
    keep = wide(jnp.where(last_seg == prev, 1.0, 0.0))
    prev_seg[0:1] = last_seg
    b_t = bmat.astype(F32).T.astype(BF16)
    st_ref[0] = state[...].astype(BF16)
    carr_scr[...] = dot_nn(cmat, st_ref[0])

    def group(i, _):
        cols = tile_at(i)
        for rows in chunks():
            here = pl.ds(pl.multiple_of(block * T + rows.start, CHUNK), CHUNK)
            x1 = (act[here, cols].astype(F32) * step_f[rows, cols]).astype(BF16)
            put_diagonal(diag, rows.start, x1)
            xw_scr[rows, cols] = (x1.astype(F32) * to_end[rows, cols]).astype(BF16)
        for k in range(HPT):
            row = cum_rows[pl.ds(HPT * i + k, 1), :]
            for rows in chunks():
                n = LANES if rows.start < LANES else T
                colb = cum_b[HPT * i + k, rows]
                colb = colb if n == LANES else wide(colb)
                decay = jnp.exp2(jnp.minimum(colb - row[:, :n], 0.0)).astype(BF16)
                wcat[rows, k * T : k * T + n] = scores[rows, :n] * decay
        y_ref[:, cols] = dot_nn(wcat[...], diag[...])
        skip = skip_ref[0:1, cols]
        for rows in chunks():
            here = pl.ds(pl.multiple_of(block * T + rows.start, CHUNK), CHUNK)
            y = y_ref[rows, cols] + carr_scr[rows, cols] * from_start[rows, cols]
            y_ref[rows, cols] = y + act[here, cols].astype(F32) * skip
        fade = from_start_last(cum_b, i) * keep
        for rows in chunks(0, NSTATE):
            state[rows, cols] = state[rows, cols] * fade
        return 0

    lax.fori_loop(0, NT, group, 0)
    state[...] += dot_nn(b_t, xw_scr[...])


def scan_scratch():
    return [
        pltpu.VMEM((NSTATE, D_INNER), F32),
        pltpu.VMEM((H, T, LANES), F32),
        pltpu.VMEM((2 * LANES, D_INNER), BF16),
        pltpu.VMEM((T, HPT * T), BF16),
        pltpu.VMEM((LANES, T), F32),
        pltpu.VMEM((T, D_INNER), BF16),
        pltpu.VMEM((T, D_INNER), F32),
        pltpu.VMEM((HPT * T, W), BF16),
        pltpu.VMEM((T, T), BF16),
        pltpu.VMEM((8, LANES), F32),
        pltpu.VMEM((T, D_INNER), F32),
        pltpu.VMEM((T, D_INNER), F32),
        pltpu.VMEM((T, D_INNER), F32),
    ]


def norm_rows(tok_ref, gain, nrm_ref):
    def body(i, _):
        rows = pl.ds(pl.multiple_of(i * CHUNK, CHUNK), CHUNK)
        tok = tok_ref[rows].astype(F32)
        rho = lax.rsqrt(jnp.sum(tok * tok, axis=1, keepdims=True) * (1.0 / D) + EPSILON)
        nrm_ref[rows] = (tok * rho * gain).astype(BF16)
        return 0

    lax.fori_loop(0, tok_ref.shape[0] // CHUNK, body, 0)


def segment_masks(seg_ref, segb_ref, pad, mask):
    length = segb_ref.shape[0]
    column = jnp.broadcast_to(seg_ref[...].astype(F32), (8, length)).T
    pad[0:8] = jnp.full((8, LANES), -1.0, F32)
    for r in range(0, length, T):
        rows = jnp.broadcast_to(column[r : r + T, 0:1], (T, LANES))
        segb_ref[r : r + T] = rows
        pad[8 + r : 8 + r + T] = rows
    for k in range(1, KERNEL):
        for r in range(0, length, T):
            mask[k - 1, r : r + T] = jnp.where(pad[8 + r - k : 8 + r - k + T] == segb_ref[r : r + T], 1.0, 0.0)


def unpack_small(slots, taps_ref, vec_ref, hv_ref, skip_ref):
    parts = slots.shape[0]
    taps_ref[...] = jnp.zeros_like(taps_ref)
    vec_ref[...] = jnp.zeros_like(vec_ref)
    hv_ref[...] = jnp.zeros_like(hv_ref)
    skip_ref[...] = jnp.zeros_like(skip_ref)
    n, m = CONV_CH // parts, VEC // parts
    for p in range(parts):
        taps_ref[0:KERNEL, n * p : n * (p + 1)] = slots[p, 0:KERNEL, 0:n].astype(BF16).astype(F32)
        vec_ref[0:1, m * p : m * (p + 1)] = slots[p, 8:9, 0:m].astype(BF16).astype(F32)
    for k in range(2):
        hv_ref[k : k + 1, 0:H] = vec_ref[0:1, HEADS_AT + k * H : HEADS_AT + (k + 1) * H]
    for h in range(H):
        at = HEADS_AT + 2 * H + h
        skip_ref[0:1, P_SIZE * h : P_SIZE * (h + 1)] = jnp.broadcast_to(vec_ref[0:1, at : at + 1], (1, P_SIZE))


def conv_tile(j, nrm_ref, w, taps_ref, vec_ref, mask, act_ref, dsilu_ref, cin_ref, pad):
    length = nrm_ref.shape[0]
    pad[0:8] = jnp.zeros((8, W), F32)
    cols = tile_at(j)
    taps = [taps_ref[k : k + 1, cols] for k in range(KERNEL)]
    bias = vec_ref[0:1, pl.ds(pl.multiple_of(D + D_INNER + j * W, W), W)]
    for top in range(0, length, T):
        pad[8 + top : 8 + top + T] = dot_nn(nrm_ref[top : top + T], w[:, cols])
        for r in range(top, top + T, CHUNK):
            here = pad[8 + r : 8 + r + CHUNK]
            cin_ref[r : r + CHUNK] = here.astype(BF16)
            total = bias + here * taps[0]
            for k in range(1, KERNEL):
                m = wide(mask[k - 1, r : r + CHUNK])
                total = total + pad[8 + r - k : 8 + r - k + CHUNK] * m * taps[k]
            sig = sigmoid(total)
            act = total * sig
            act_ref[r : r + CHUNK] = act.astype(BF16)
            dsilu_ref[r : r + CHUNK] = (sig + act * (1.0 - sig)).astype(BF16)


def weight_piece(src, src_cols, put, hop_sems, index, rows):
    sends, recvs = hop_sems
    half, quarter = rows // 2, rows // 4
    me = lax.axis_index("grp")
    x, y = bit(ALONG_X), bit(ALONG_Y)
    slot_x, slot_y, slot_d = 2 * y + 1 - x, 2 * (1 - y) + x, 2 * (1 - y) + 1 - x
    top = bit(CORE) * half

    def copy(n, a, b, hop):
        return pltpu.make_async_remote_copy(
            src_ref=a, dst_ref=b, send_sem=sends.at[index, n], recv_sem=recvs.at[index, n],
            device_id=across(hop), device_id_type=MESH,
        )

    def onward(n, slot, start, size, hop):
        return copy(n, put(slot * rows + start, size), put(slot * rows + start, size), hop)

    mine = src.at[rows_at(top, half), src_cols]
    copies = [
        copy(0, mine, put(me * rows + top, half), ALONG_X),
        copy(1, mine, put(me * rows + top, half), ALONG_Y),
        onward(2, slot_x, top, quarter, ALONG_Y),
        onward(3, slot_y, top + quarter, quarter, ALONG_X),
        onward(4, slot_x, top, half, CORE),
        onward(5, slot_y, top, half, CORE),
        onward(6, slot_d, top, quarter, CORE),
        onward(7, slot_d, top + quarter, quarter, CORE),
    ]

    def own():
        copies[0].start()
        copies[1].start()

    def pass_on():
        copies[0].wait_recv()
        copies[2].start()
        copies[1].wait_recv()
        copies[3].start()
        copies[4].start()
        copies[5].start()

    def corner():
        copies[2].wait_recv()
        copies[6].start()
        copies[3].wait_recv()
        copies[7].start()

    def arrive():
        for n in range(4, 8):
            copies[n].wait_recv()

    def finish():
        for one in copies:
            one.wait_send()

    return own, pass_on, corner, arrive, finish


def project_kernel(
    tok_ref, seg_ref, wt_ref, wo_ref, small_ref,
    act_ref, dsilu_ref, cin_ref, y_ref, st_ref, sraw_ref, nrm_ref, segb_ref, taps_ref, vec_ref, hv_ref, skip_ref,
    wg_full, wc_full, wo_full,
    wt_f32, wo_f32, stage_in, stage_out, conv_full, slots, pad, segpad, mask, act, *rest,
):
    *scan, local_sems, sends, recvs, small_sends, small_recvs = rest
    j = pl.program_id(0)
    me = lax.axis_index("grp")
    rows_in, rows_out = D // 4, D_INNER // 4
    load_conv = pltpu.make_async_copy(wt_ref.at[D_INNER:], wt_f32.at[D_INNER : D_INNER + CONV_CH + H], local_sems.at[0])
    load_gate = pltpu.make_async_copy(wt_ref.at[:D_INNER], wt_f32.at[:D_INNER], local_sems.at[1])
    load_out = pltpu.make_async_copy(wo_ref, wo_f32, local_sems.at[2])
    keep_conv = pltpu.make_async_copy(
        stage_in.at[:, D_INNER:], conv_full.at[rows_at(me * rows_in, rows_in)], local_sems.at[3]
    )
    keep_gate = pltpu.make_async_copy(
        stage_in.at[:, :D_INNER], wg_full.at[rows_at(me * rows_in, rows_in)], local_sems.at[4]
    )
    keep_out = pltpu.make_async_copy(stage_out, wo_full.at[rows_at(me * rows_out, rows_out)], local_sems.at[5])
    write_conv = pltpu.make_async_copy(conv_full, wc_full, local_sems.at[6])

    def small_copy(n, a, b, hop):
        return pltpu.make_async_remote_copy(
            src_ref=a, dst_ref=b, send_sem=small_sends.at[n], recv_sem=small_recvs.at[n],
            device_id=across(hop), device_id_type=MESH,
        )

    x, y = bit(ALONG_X), bit(ALONG_Y)
    slot_x, slot_y = 2 * y + 1 - x, 2 * (1 - y) + x
    smalls = [
        small_copy(0, small_ref, slots.at[me], ALONG_X),
        small_copy(1, small_ref, slots.at[me], ALONG_Y),
        small_copy(2, slots.at[slot_x, 0:8], slots.at[slot_x, 0:8], ALONG_Y),
        small_copy(3, slots.at[slot_y, 8:16], slots.at[slot_y, 8:16], ALONG_X),
    ]

    def conv_put(start, size):
        return lambda at, n: conv_full.at[rows_at(at, n), start : start + size]

    def gate_put(start, size):
        return lambda at, n: wg_full.at[rows_at(at, n), start : start + size]

    def out_put(start, size):
        return lambda at, n: wo_full.at[rows_at(at, n), start : start + size]

    sems = (sends, recvs)
    pieces = []
    for start, size in ((0, 768), (768, 768), (1536, 896)):
        pieces.append(weight_piece(
            stage_in, slice(D_INNER + start, D_INNER + start + size), conv_put(start, size), sems, len(pieces), rows_in))
    for start, size in ((0, 1024), (1024, 1024)):
        pieces.append(weight_piece(stage_in, slice(start, start + size), gate_put(start, size), sems, len(pieces), rows_in))
    for start, size in ((0, 512), (512, 512)):
        pieces.append(weight_piece(stage_out, slice(start, start + size), out_put(start, size), sems, len(pieces), rows_out))
    OWN, PASS, CORNER, ARRIVE, FINISH = range(5)

    def turn(start, count):
        def body(i, _):
            at = pl.ds(pl.multiple_of(start + i * LANES, LANES), LANES)
            stage_in[:, at] = wt_f32[at, :].T.astype(BF16)
            return 0

        lax.fori_loop(0, count, body, 0)

    @pl.when(j == 0)
    def _():
        load_conv.start()
        load_gate.start()
        load_out.start()
        wt_f32[STEP_AT + H : ALL] = jnp.zeros((LANES - H, wt_f32.shape[1]), F32)
        greet((CORE, ALONG_X, ALONG_Y))
        smalls[0].start()
        smalls[1].start()
        load_conv.wait()
        turn(D_INNER, 6)
        pieces[0][OWN]()
        smalls[0].wait_recv()
        smalls[2].start()
        smalls[1].wait_recv()
        smalls[3].start()
        slots[me] = small_ref[...]
        turn(D_INNER + 768, 6)
        pieces[1][OWN]()
        segment_masks(seg_ref, segb_ref, segpad, mask)
        pieces[0][PASS]()
        smalls[2].wait_recv()
        smalls[3].wait_recv()
        unpack_small(slots, taps_ref, vec_ref, hv_ref, skip_ref)
        turn(D_INNER + 1536, 7)
        keep_conv.start()
        pieces[0][CORNER]()
        pieces[2][OWN]()
        pieces[1][PASS]()
        norm_rows(tok_ref, vec_ref[0:1, :D], nrm_ref)
        keep_conv.wait()
        pieces[0][ARRIVE]()

    @pl.when(j == 1)
    def _():
        pieces[1][CORNER]()
        pieces[2][PASS]()
        load_gate.wait()
        turn(0, 16)
        keep_gate.start()
        pieces[3][OWN]()

    @pl.when(j == 3)
    def _():
        pieces[1][ARRIVE]()
        pieces[2][CORNER]()
        load_out.wait()

        def cast(i, _):
            at = pl.ds(pl.multiple_of(i * 32, 32), 32)
            stage_out[at] = wo_f32[at].astype(BF16)
            return 0

        lax.fori_loop(0, rows_out // 32, cast, 0)
        keep_out.start()
        pieces[4][OWN]()

    @pl.when(j == 4)
    def _():
        pieces[3][PASS]()

    @pl.when(j == 6)
    def _():
        pieces[2][ARRIVE]()
        write_conv.start()
        sraw_ref[...] = dot_nn(nrm_ref[...], conv_full[:, CONV_CH:])
        pieces[3][CORNER]()
        pieces[4][PASS]()
        pieces[5][OWN]()

    @pl.when(j == 8)
    def _():
        pieces[4][CORNER]()
        pieces[6][OWN]()

    @pl.when(j < CT)
    def _():
        conv_tile(j, nrm_ref, conv_full, taps_ref, vec_ref, mask, act_ref, dsilu_ref, cin_ref, pad)
        act[:, tile_at(j)] = act_ref[...]

    @pl.when(j == CT)
    def _():
        pieces[5][PASS]()

    @pl.when(j == CT + 1)
    def _():
        pieces[5][CORNER]()
        pieces[6][PASS]()

    @pl.when(j == CT + 2)
    def _():
        pieces[6][CORNER]()

    @pl.when(j >= CT)
    def _():
        scan_forward(j - CT, act, sraw_ref, segb_ref, seg_ref, hv_ref, skip_ref, y_ref, st_ref, scan)

    @pl.when(j == pl.num_programs(0) - 1)
    def _():
        for n in range(3, 7):
            pieces[n][ARRIVE]()
        for piece in pieces:
            piece[FINISH]()
        for one in smalls:
            one.wait_send()
        keep_gate.wait()
        keep_out.wait()
        write_conv.wait()


def plain_project_kernel(
    tok_ref, seg_ref, w_ref, slots,
    act_ref, dsilu_ref, cin_ref, y_ref, st_ref, sraw_ref, nrm_ref, segb_ref, taps_ref, vec_ref, hv_ref, skip_ref,
    pad, segpad, mask, act, *scan,
):
    j = pl.program_id(0)

    @pl.when(j == 0)
    def _():
        segment_masks(seg_ref, segb_ref, segpad, mask)
        unpack_small(slots, taps_ref, vec_ref, hv_ref, skip_ref)
        norm_rows(tok_ref, vec_ref[0:1, :D], nrm_ref)
        sraw_ref[...] = dot_nn(nrm_ref[...], w_ref[:, CONV_CH:])

    @pl.when(j < CT)
    def _():
        conv_tile(j, nrm_ref, w_ref, taps_ref, vec_ref, mask, act_ref, dsilu_ref, cin_ref, pad)
        act[:, tile_at(j)] = act_ref[...]

    @pl.when(j >= CT)
    def _():
        scan_forward(j - CT, act, sraw_ref, segb_ref, seg_ref, hv_ref, skip_ref, y_ref, st_ref, scan)


def project_outputs(length):
    col = lambda j: (0, jnp.minimum(j, CT - 1))
    fixed = lambda j: (0, 0)
    shapes = [((length, CONV_CH), BF16)] * 3 + [((length, D_INNER), F32), ((length // T, NSTATE, D_INNER), BF16)]
    specs = [pl.BlockSpec((length, W), col)] * 3 + [
        pl.BlockSpec((T, D_INNER), lambda j: (jnp.maximum(j - CT, 0), 0)),
        pl.BlockSpec((1, NSTATE, D_INNER), lambda j: (jnp.maximum(j - CT, 0), 0, 0)),
    ]
    for shape, dtype in (
        ((length, LANES), F32), ((length, D), BF16), ((length, LANES), F32), ((8, CONV_CH), F32), ((8, VEC_PAD), F32),
        ((8, LANES), F32), ((8, D_INNER), F32),
    ):
        shapes.append((shape, dtype))
        specs.append(pl.BlockSpec(shape, fixed))
    scratch = [
        pltpu.VMEM((8 + length, W), F32),
        pltpu.VMEM((8 + length, LANES), F32),
        pltpu.VMEM((KERNEL - 1, length, LANES), F32),
        pltpu.VMEM((length, CONV_CH), BF16),
        *scan_scratch(),
    ]
    return [jax.ShapeDtypeStruct(*one) for one in shapes], specs, scratch


def project_call(tok, seg, wt, wo, small):
    length = tok.shape[0]
    shapes, specs, scratch = project_outputs(length)
    hbm = pl.BlockSpec(memory_space=pl.ANY)
    shapes += [jax.ShapeDtypeStruct(shape, BF16) for shape in ((D, D_INNER), (D, CONV_CH + LANES), (D_INNER, D))]
    return pl.pallas_call(
        project_kernel,
        grid=(CT + length // T,),
        in_specs=[whole(tok.shape), whole(seg.shape), hbm, hbm, whole(small.shape)],
        out_specs=specs + [hbm] * 3,
        out_shape=shapes,
        scratch_shapes=[
            pltpu.VMEM((ALL, D // 4), F32),
            pltpu.VMEM((D_INNER // 4, D), F32),
            pltpu.VMEM((D // 4, ALL), BF16),
            pltpu.VMEM((D_INNER // 4, D), BF16),
            pltpu.VMEM((D, CONV_CH + LANES), BF16),
            pltpu.VMEM((4, *small.shape), F32),
            *scratch,
            pltpu.SemaphoreType.DMA((7,)),
            pltpu.SemaphoreType.DMA((7, 8)),
            pltpu.SemaphoreType.DMA((7, 8)),
            pltpu.SemaphoreType.DMA((4,)),
            pltpu.SemaphoreType.DMA((4,)),
        ],
        compiler_params=pltpu.CompilerParams(collective_id=0, has_side_effects=True, vmem_limit_bytes=VMEM_LIMIT),
        cost_estimate=pl.CostEstimate(flops=2 * length * D * CONV_CH, bytes_accessed=40 << 20, transcendentals=0),
    )(tok, seg, wt, wo, small)


def plain_project_call(tok, seg, w_conv, slots):
    length = tok.shape[0]
    shapes, specs, scratch = project_outputs(length)
    return pl.pallas_call(
        plain_project_kernel,
        grid=(CT + length // T,),
        in_specs=[whole(tok.shape), whole(seg.shape), whole(w_conv.shape), whole(slots.shape)],
        out_specs=specs,
        out_shape=shapes,
        scratch_shapes=scratch,
        compiler_params=pltpu.CompilerParams(vmem_limit_bytes=VMEM_LIMIT),
        cost_estimate=pl.CostEstimate(flops=2 * length * D * CONV_CH, bytes_accessed=20 << 20, transcendentals=0),
    )(tok, seg, w_conv, slots)


def fwd_kernel(
    xs_ref, y_ref, nrm_ref, tok_ref, cot_ref, wg_ref, wo_ref, vec_ref, skip_ref,
    out_ref, mixed_ref, gy_ref, gg_ref, rsum_ref, dgain_ref, dskip_ref,
    silu_scr, sig_scr, gated_scr, gm_scr, sums, rho_b, high, low, pick,
):
    block = pl.program_id(0)

    @pl.when(block == 0)
    def _():
        dgain_ref[...] = jnp.zeros_like(dgain_ref)
        dskip_ref[...] = jnp.zeros_like(dskip_ref)
        set_pick(pick)

    sums[...] = jnp.zeros_like(sums)

    def gate_product(i):
        cols = tile_of(i)
        silu_scr[:, cols] = dot_nn(nrm_ref[...], wg_ref[:, cols])

    gate_product(0)
    for i in range(NT):
        if i + 1 < NT:
            gate_product(i + 1)
        cols = tile_of(i)
        for rows in chunks():
            gate = silu_scr[rows, cols]
            sig = sigmoid(gate)
            silu = gate * sig
            sig_scr[rows, cols] = sig
            silu_scr[rows, cols] = silu
            gated = y_ref[rows, cols] * silu
            gated_scr[rows, cols] = gated
            g2 = gated * gated
            sums[rows] += g2[:, :LANES] + g2[:, LANES:]

    def mixed_product(i):
        cols = tile_of(i)
        gm_scr[:, cols] = dot_nt(cot_ref[...], wo_ref[cols, :])

    mixed_product(0)
    mean2 = jnp.sum(sums[...], axis=1, keepdims=True) * (1.0 / D_INNER)
    rho_b[...] = jnp.broadcast_to(lax.rsqrt(mean2 + EPSILON), (T, LANES))
    sums[...] = jnp.zeros_like(sums)

    for i in range(NT):
        if i + 1 < NT:
            mixed_product(i + 1)
        cols = tile_of(i)
        gain = vec_ref[0:1, D + i * W : D + (i + 1) * W]
        total = jnp.zeros((8, W), F32)
        for rows in chunks():
            gated = gated_scr[rows, cols]
            unit = gated * wide(rho_b[rows])
            mixed_ref[rows, cols] = (unit * gain).astype(BF16)
            gm = gm_scr[rows, cols]
            total = total + rows8(gm * unit)
            e = gm * gain
            gm_scr[rows, cols] = e
            eg = e * gated
            sums[rows] += eg[:, :LANES] + eg[:, LANES:]
        dgain_ref[:, cols] += total

    rho = rho_b[...]
    inner = jnp.sum(sums[...], axis=1, keepdims=True) * (1.0 / D_INNER)
    sums[...] = inner * rho * rho * rho
    rsum_ref[...] = jnp.zeros_like(rsum_ref)

    def out_product(j):
        cols = tile_of(j)
        branch = dot_nn(mixed_ref[...], wo_ref[:, cols])
        out_ref[:, cols] = (tok_ref[:, cols].astype(F32) + branch).astype(BF16)

    for i in range(NT):
        if i % 2 == 0:
            out_product(i // 2)
        cols = tile_of(i)
        skip = skip_ref[0:1, cols]
        total = jnp.zeros((8, W), F32)
        p = i % 2
        for rows in chunks():
            sig = sig_scr[rows, cols]
            silu = silu_scr[rows, cols]
            y = y_ref[rows, cols]
            grad_gated = wide(rho_b[rows]) * gm_scr[rows, cols] - gated_scr[rows, cols] * wide(sums[rows])
            gg_ref[rows, cols] = (grad_gated * y * (sig + silu * (1.0 - sig))).astype(BF16)
            gy = (grad_gated * silu).astype(BF16)
            gy_ref[rows, cols] = gy
            gy = gy.astype(F32)
            xs = xs_ref[rows, cols].astype(F32)
            total = total + rows8(gy * xs)
            split_halves(gy * (y - xs * skip), high.at[p], low.at[p], rows)
        dskip_ref[:, cols] += total
        rsum_ref[...] += head_sums(high.at[p], low.at[p], pick[cols, :])


def fwd_call(xs_bc, y, nrm, tok, cot, wg, wo, vec, skip):
    length = nrm.shape[0]
    blocks = length // T
    tokens = lambda b: (b, 0)
    fixed = lambda b: (0, 0)
    wide_block = pl.BlockSpec((T, D_INNER), tokens)
    return pl.pallas_call(
        fwd_kernel,
        grid=(blocks,),
        in_specs=[
            wide_block,
            wide_block,
            pl.BlockSpec((T, D), tokens),
            pl.BlockSpec((T, D), tokens),
            pl.BlockSpec((T, D), tokens),
            whole(wg.shape),
            whole(wo.shape),
            whole(vec.shape),
            whole(skip.shape),
        ],
        out_specs=[
            pl.BlockSpec((T, D), tokens),
            wide_block,
            wide_block,
            wide_block,
            pl.BlockSpec((T, LANES), tokens),
            pl.BlockSpec((8, D_INNER), fixed),
            pl.BlockSpec((8, D_INNER), fixed),
        ],
        out_shape=[
            jax.ShapeDtypeStruct((length, D), BF16),
            jax.ShapeDtypeStruct((length, D_INNER), BF16),
            jax.ShapeDtypeStruct((length, D_INNER), BF16),
            jax.ShapeDtypeStruct((length, D_INNER), BF16),
            jax.ShapeDtypeStruct((length, LANES), F32),
            jax.ShapeDtypeStruct((8, D_INNER), F32),
            jax.ShapeDtypeStruct((8, D_INNER), F32),
        ],
        scratch_shapes=[
            pltpu.VMEM((T, D_INNER), F32),
            pltpu.VMEM((T, D_INNER), F32),
            pltpu.VMEM((T, D_INNER), F32),
            pltpu.VMEM((T, D_INNER), F32),
            pltpu.VMEM((T, LANES), F32),
            pltpu.VMEM((T, LANES), F32),
            pltpu.VMEM((2, T, W), BF16),
            pltpu.VMEM((2, T, W), BF16),
            pltpu.VMEM((D_INNER, LANES), BF16),
        ],
        compiler_params=pltpu.CompilerParams(vmem_limit_bytes=VMEM_LIMIT),
        cost_estimate=pl.CostEstimate(flops=2 * length * D * D_INNER * 3, bytes_accessed=40 << 20, transcendentals=0),
    )(xs_bc, y, nrm, tok, cot, wg, wo, vec, skip)


def bwd_kernel(remote, *refs):
    if remote:
        ticks, ends, refs = gate_out_plan(refs)
        slots = by_slot(ticks)
    (
        xs_ref, bc_ref, sraw_ref, segb_ref, seg_ref, prev_ref, gy_ref, st_ref, rsum_ref, dsilu_ref, cin_ref,
        hv_ref, skip_ref, taps_ref,
        gc_ref, dtaps_ref, dhv_ref,
        gstate, cum_b, fan, wcat, cum_rows, gf, gscore, gyw_scr, xw_scr, back_scr, through, diag_x, diag_y, gw_scr, gx_scr,
        scores, x1_scr, high, low, high_s, pick, segpad, mask, inner_ref, outer_ref, step_f, from_start, to_end,
    ) = refs
    turn = pl.program_id(0)
    last_turn = pl.num_programs(0) - 1

    @pl.when(turn == 0)
    def _():
        gstate[...] = jnp.zeros_like(gstate)
        wcat[...] = jnp.zeros_like(wcat)
        diag_x[...] = jnp.zeros_like(diag_x)
        diag_y[...] = jnp.zeros_like(diag_y)
        dtaps_ref[...] = jnp.zeros_like(dtaps_ref)
        dhv_ref[...] = jnp.zeros_like(dhv_ref)
        gf[T : T + 8] = jnp.zeros((8, CONV_CH), F32)
        segpad[T : T + 8] = jnp.full((8, LANES), -1.0, F32)
        set_pick(pick)
        set_fan(fan)
        if remote:
            greet(range(5))

    @pl.when(turn > 0)
    def _():
        gf[T : T + 8] = gf[0:8]
        segpad[T : T + 8] = segpad[0:8]

    segb = segb_ref[...]
    segpad[0:T] = segb
    for k in range(1, KERNEL):
        mask[k - 1] = jnp.where(segpad[k : k + T] == segb, 1.0, 0.0)
    v, step, rate = head_terms(sraw_ref, hv_ref)
    logdecay = step * rate
    cum = cumulate(logdecay)
    cum_rows[...] = cum.T
    spread(cum, cum_b)
    bmat = bc_ref[:, :NSTATE]
    cmat = bc_ref[:, NSTATE:]
    s_at, t_at = before(T, T)
    same = wide(segb) == seg_ref[...].astype(F32)
    valid = same & (s_at <= t_at)
    scores[...] = jnp.where(valid, dot_nt(bmat, cmat), 0.0).astype(BF16)
    prev = jnp.where(turn == last_turn, -1.0, prev_ref[7:8])
    last_seg = segb[T - 1 : T]
    last = cum[T - 1 : T]
    expand(step, fan, step_f)
    expand(jnp.exp2(cum) * jnp.where(segb == prev, 1.0, 0.0), fan, from_start)
    expand(jnp.exp2(last - cum) * jnp.where(segb == last_seg, 1.0, 0.0), fan, to_end)
    keep = wide(jnp.where(last_seg == prev, 1.0, 0.0))
    c_t = cmat.astype(F32).T.astype(BF16)
    gst_b = gstate[...].astype(BF16)
    back_scr[...] = dot_nn(bmat, gst_b)
    gscore[...] = jnp.zeros_like(gscore)
    inner_ref[...] = jnp.zeros_like(inner_ref)
    outer_ref[...] = jnp.zeros_like(outer_ref)

    def spread_out(i, p):
        cols = tile_at(i)
        for rows in chunks():
            x1 = (xs_ref[rows, cols].astype(F32) * step_f[rows, cols]).astype(BF16)
            x1_scr[p, rows] = x1
            put_diagonal(diag_x.at[p], rows.start, x1)
            gy = gy_ref[rows, cols]
            put_diagonal(diag_y.at[p], rows.start, gy)
            xw_scr[rows, cols] = (x1.astype(F32) * to_end[rows, cols]).astype(BF16)
            gyw_scr[rows, cols] = (gy.astype(F32) * from_start[rows, cols]).astype(BF16)

    def pair_product(i, p):
        gw_scr[p] = dot_nt(diag_x[p], gy_ref[:, tile_at(i)])

    def decays(i, p):
        for rows in chunks():
            start = 0 if rows.start < LANES else LANES
            total = gscore[rows, start:]
            score = scores[rows, start:]
            for k in range(HPT):
                row = cum_rows[pl.ds(HPT * i + k, 1), :]
                colb = cum_b[HPT * i + k, rows]
                colb = colb if start else wide(colb)
                decay = jnp.exp2(jnp.minimum(row[:, start:] - colb, 0.0))
                wcat[p, rows, k * T + start : (k + 1) * T] = score * decay.astype(BF16)
                total = total + gw_scr[p, k * T + rows.start : k * T + rows.stop, start:] * decay
            gscore[rows, start:] = total

    def grad_product(p):
        gx_scr[p] = dot_nn(wcat[p], diag_y[p])

    def collect(i, p):
        cols = tile_at(i)
        skip = skip_ref[0:1, cols]
        for rows in chunks():
            gx1 = gx_scr[p, rows]
            x1 = x1_scr[p, rows].astype(F32)
            from_state = back_scr[rows, cols] * to_end[rows, cols]
            split_halves(x1 * gx1, high.at[p], low.at[p], rows)
            high_s[p, rows] = (x1 * from_state).astype(BF16)
            gx = (gx1 + from_state) * step_f[rows, cols] + gy_ref[rows, cols].astype(F32) * skip
            gf[rows, cols] = gx * dsilu_ref[rows, cols].astype(F32)
        fade = from_start_last(cum_b, i) * keep
        total = jnp.zeros((8, W), F32)
        for rows in chunks(0, NSTATE):
            gst = gstate[rows, cols] * fade
            gstate[rows, cols] = gst
            total = total + rows8(gst * st_ref[0, rows, cols].astype(F32))
        through[:, cols] = total

    def head_product(i, p):
        pick_i = pick[tile_at(i), :]
        inner_ref[...] += head_sums(high.at[p], low.at[p], pick_i)
        outer_ref[...] += dot_nn(high_s[p], pick_i)

    def two_groups(n, _):
        a, b = 2 * n, 2 * n + 1
        spread_out(a, 0)
        pair_product(a, 0)
        spread_out(b, 1)
        pair_product(b, 1)
        decays(a, 0)
        grad_product(0)
        decays(b, 1)
        grad_product(1)
        collect(a, 0)
        head_product(a, 0)
        collect(b, 1)
        head_product(b, 1)
        if remote:
            for slot, actions in slots.items():

                @pl.when(turn * NT + a == slot - slot % 2)
                def _():
                    for action in actions:
                        action()

        return 0

    lax.fori_loop(0, NT // 2, two_groups, 0)
    gyw = gyw_scr[...]
    gstate[...] += dot_nn(c_t, gyw)
    gsc = jnp.where(valid, gscore[...], 0.0)
    g_b = dot_nn(gsc.astype(BF16), cmat) + dot_nt(xw_scr[...], gst_b)
    g_c = dot_nn(gsc.T.astype(BF16), bmat) + dot_nt(gyw, st_ref[0])
    tail_cols = slice(D_INNER, CONV_CH)
    gf[0:T, tail_cols] = jnp.concatenate([g_b, g_c], axis=1) * dsilu_ref[:, tail_cols].astype(F32)

    inner_sum, outer_sum = inner_ref[...], outer_ref[...]
    after = jnp.where(valid, 1.0, 0.0)
    ahead = jnp.where(same & (s_at > t_at), 1.0, 0.0)
    flow = through[...]
    flow_high = flow.astype(BF16)
    flow_low = (flow - flow_high.astype(F32)).astype(BF16)
    over = jnp.sum(dot_nn(flow_high, pick[...]) + dot_nn(flow_low, pick[...]), axis=0, keepdims=True)
    gl = jnp.dot(after, rsum_ref[...] - inner_sum, precision=HIGHEST, preferred_element_type=F32)
    gl = gl + jnp.dot(ahead, outer_sum, precision=HIGHEST, preferred_element_type=F32) + over
    grad_step = (inner_sum + outer_sum) / jnp.maximum(step, 1e-37) + gl * rate
    lane = lax.broadcasted_iota(jnp.int32, (T, LANES), 1)
    g_sraw = jnp.where(lane < H, grad_step * sigmoid(v), 0.0)
    gc_ref[:, CONV_CH:] = g_sraw.astype(BF16)
    dhv_ref[0:8] += rows8(g_sraw)
    dhv_ref[8:16] += rows8(gl * logdecay)

    def conv_group(j, _):
        cols = tile_at(j)
        taps = [taps_ref[k : k + 1, cols] for k in range(KERNEL)]
        totals = [jnp.zeros((8, W), F32) for _ in range(KERNEL + 1)]
        for rows in chunks():
            here = gf[rows, cols]
            cin = cin_ref[rows, cols].astype(F32)
            totals[KERNEL] = totals[KERNEL] + rows8(here)
            totals[0] = totals[0] + rows8(cin * here)
            total = here * taps[0]
            for k in range(1, KERNEL):
                u = gf[rows.start + k : rows.stop + k, cols] * wide(mask[k - 1, rows])
                total = total + u * taps[k]
                totals[k] = totals[k] + rows8(cin * u)
            gc_ref[rows, cols] = total.astype(BF16)
        for k in range(KERNEL + 1):
            dtaps_ref[8 * k : 8 * k + 8, cols] += totals[k]
        return 0

    lax.fori_loop(0, CT, conv_group, 0)

    if remote:

        @pl.when(turn == last_turn)
        def _():
            for end in ends:
                end()


OUT_CHUNKS, GATE_CHUNKS = 4, 4
OUT_COLS, GATE_COLS = D // OUT_CHUNKS, D_INNER // GATE_CHUNKS
BWD_PACE = (0, 4, 8, 10, 12, 14, 16, 18, 20)
BWD_SLOTS = (0, 1, 3, 4, 6, 7, 9, 11)
TOKEN_PACE = (0, 2, 4, 6, 7, 8, 9, 10, 11)


def gate_out_plan(refs):
    ins, outs, scratch = 14, 3, 28
    head, rest = refs[:ins], refs[ins:]
    (grad_out, grad_gate), rest = rest[:2], rest[2:]
    mid, rest = rest[:outs], rest[outs:]
    (out_total, gate_total), rest = rest[:2], rest[2:]
    tail, rest = rest[:scratch], rest[scratch:]
    out_bufs, gate_bufs, sems = rest[:BUFFERS], rest[BUFFERS : 2 * BUFFERS], rest[2 * BUFFERS :]
    out_starts = [OUT_COLS * n for n in range(OUT_CHUNKS)]
    gate_starts = [GATE_COLS * n for n in range(GATE_CHUNKS)]
    ticks, ends = reduce_plan(
        grad_out, out_starts, OUT_COLS, BWD_SLOTS[0::2], BWD_PACE, out_bufs, out_total, sems, 0, [True] * OUT_CHUNKS
    )
    more, more_ends = reduce_plan(
        grad_gate, gate_starts, GATE_COLS, BWD_SLOTS[1::2], BWD_PACE, gate_bufs, gate_total, sems, OUT_CHUNKS,
        [False] * GATE_CHUNKS,
    )
    return ticks + more, ends + more_ends, (*head, *mid, *tail)


def reduce_sems(count):
    return [
        pltpu.SemaphoreType.DMA((count,)),
        pltpu.SemaphoreType.DMA((count,)),
        pltpu.SemaphoreType.DMA((count, 8)),
        pltpu.SemaphoreType.DMA((count, 8)),
    ]


def bwd_call(xs_bc, sraw, segb, seg, gy, states, rsum, dsilu, cin, hv, skip, taps, grad_out=None, grad_gate=None):
    remote = grad_out is not None
    hbm = pl.BlockSpec(memory_space=pl.ANY)
    length = gy.shape[0]
    blocks = length // T
    tokens = lambda b: (blocks - 1 - b, 0)
    third = lambda b: (blocks - 1 - b, 0, 0)
    fixed = lambda b: (0, 0)
    return pl.pallas_call(
        functools.partial(bwd_kernel, remote),
        grid=(blocks,),
        in_specs=[
            pl.BlockSpec((T, D_INNER), tokens),
            pl.BlockSpec((T, 2 * NSTATE), lambda b: (blocks - 1 - b, D_INNER // (2 * NSTATE))),
            pl.BlockSpec((T, LANES), tokens),
            pl.BlockSpec((T, LANES), tokens),
            pl.BlockSpec((1, T), lambda b: (0, blocks - 1 - b)),
            pl.BlockSpec((8, LANES), lambda b: (jnp.maximum((blocks - 1 - b) * (T // 8) - 1, 0), 0)),
            pl.BlockSpec((T, D_INNER), tokens),
            pl.BlockSpec((1, NSTATE, D_INNER), third),
            pl.BlockSpec((T, LANES), tokens),
            pl.BlockSpec((T, CONV_CH), tokens),
            pl.BlockSpec((T, CONV_CH), tokens),
            whole(hv.shape),
            whole(skip.shape),
            whole(taps.shape),
            *([hbm] * 2 if remote else []),
        ],
        out_specs=[
            pl.BlockSpec((T, CONV_CH + LANES), tokens),
            pl.BlockSpec((8 * (KERNEL + 1), CONV_CH), fixed),
            pl.BlockSpec((16, LANES), fixed),
            *([hbm] * 2 if remote else []),
        ],
        out_shape=[
            jax.ShapeDtypeStruct((length, CONV_CH + LANES), BF16),
            jax.ShapeDtypeStruct((8 * (KERNEL + 1), CONV_CH), F32),
            jax.ShapeDtypeStruct((16, LANES), F32),
            *([jax.ShapeDtypeStruct(g.shape[2:], BF16) for g in (grad_out, grad_gate)] if remote else []),
        ],
        scratch_shapes=[
            pltpu.VMEM((NSTATE, D_INNER), F32),
            pltpu.VMEM((H, T, LANES), F32),
            pltpu.VMEM((2 * LANES, D_INNER), BF16),
            pltpu.VMEM((2, T, HPT * T), BF16),
            pltpu.VMEM((LANES, T), F32),
            pltpu.VMEM((T + 8, CONV_CH), F32),
            pltpu.VMEM((T, T), F32),
            pltpu.VMEM((T, D_INNER), BF16),
            pltpu.VMEM((T, D_INNER), BF16),
            pltpu.VMEM((T, D_INNER), F32),
            pltpu.VMEM((8, D_INNER), F32),
            pltpu.VMEM((2, HPT * T, W), BF16),
            pltpu.VMEM((2, HPT * T, W), BF16),
            pltpu.VMEM((2, HPT * T, T), F32),
            pltpu.VMEM((2, T, W), F32),
            pltpu.VMEM((T, T), BF16),
            pltpu.VMEM((2, T, W), BF16),
            pltpu.VMEM((2, T, W), BF16),
            pltpu.VMEM((2, T, W), BF16),
            pltpu.VMEM((2, T, W), BF16),
            pltpu.VMEM((D_INNER, LANES), BF16),
            pltpu.VMEM((T + 8, LANES), F32),
            pltpu.VMEM((KERNEL - 1, T, LANES), F32),
            pltpu.VMEM((T, LANES), F32),
            pltpu.VMEM((T, LANES), F32),
            pltpu.VMEM((T, D_INNER), F32),
            pltpu.VMEM((T, D_INNER), F32),
            pltpu.VMEM((T, D_INNER), F32),
            *(
                reduce_buffers(grad_out.shape[2], OUT_COLS, OUT_CHUNKS)
                + reduce_buffers(grad_gate.shape[2], GATE_COLS, GATE_CHUNKS)
                + reduce_sems(OUT_CHUNKS + GATE_CHUNKS)
                if remote
                else []
            ),
        ],
        compiler_params=pltpu.CompilerParams(
            vmem_limit_bytes=VMEM_LIMIT, **(dict(collective_id=1, has_side_effects=True) if remote else {})
        ),
        cost_estimate=pl.CostEstimate(flops=2 * length * D * D_INNER * 4, bytes_accessed=30 << 20, transcendentals=0),
    )(xs_bc, xs_bc, sraw, segb, seg, segb, gy, states, rsum, dsilu, cin, hv, skip, taps, *((grad_out, grad_gate) if remote else ()))


CONV_COLS = 2 * W
CONV_CHUNKS = (CONV_CH + LANES) // CONV_COLS
CONV_DONE = CONV_CHUNKS * CONV_COLS
CONV_LEFT = CONV_CH + LANES - CONV_DONE


def token_kernel(remote, *refs):
    (gg_ref, gc_ref, wg_hbm, wc_hbm, tok_ref, cot_ref, vec_ref, taps_sum, vec_sum), refs = refs[:9], refs[9:]
    if remote:
        grad_conv, refs = refs[0], refs[1:]
        (tg_ref, small_total, conv_total), refs = refs[:3], refs[3:]
    else:
        (tg_ref, small_total), refs = refs[:2], refs[2:]
    (wg, wc, grad, dpre, small, load_sems), refs = refs[:6], refs[6:]
    turn = pl.program_id(0)
    last_turn = pl.num_programs(0) - 1
    loads = [
        pltpu.make_async_copy(wg_hbm, wg, load_sems.at[0]),
        pltpu.make_async_copy(wc_hbm, wc, load_sems.at[1]),
    ]
    pieces = D // CONV_COLS
    slots = {}
    if remote:
        conv_bufs, step_bufs, refs = refs[:BUFFERS], refs[BUFFERS : 2 * BUFFERS], refs[2 * BUFFERS :]
        small_bufs, refs = refs[:9], refs[9:]
        sems, small_sems = refs[:4], refs[4:]
        starts = [CONV_COLS * n for n in range(CONV_CHUNKS)]
        ticks, ends = reduce_plan(
            grad_conv, starts, CONV_COLS, range(CONV_CHUNKS), TOKEN_PACE, conv_bufs, conv_total, sems, 0,
            [n % 2 == 0 for n in range(CONV_CHUNKS)],
        )
        more, more_ends = reduce_plan(
            grad_conv, [CONV_DONE], CONV_LEFT, [CONV_CHUNKS], TOKEN_PACE, step_bufs, conv_total, sems, CONV_CHUNKS,
            [True],
        )
        done = 4 * pieces
        last, last_ends = small_plan(small, small_bufs, small_total, small_sems, done, 1)
        slots = by_slot(ticks + more + last)
        ends = ends + more_ends + last_ends

    @pl.when(turn == 0)
    def _():
        for load in loads:
            load.start()
        dpre[...] = jnp.zeros_like(dpre)
        if remote:
            greet(range(5))
            for action in slots.pop(0):
                action()
        for load in loads:
            load.wait()

    def piece(q, _):
        rows = tile_at(q, CONV_COLS)
        grad[:, rows] = dot_nt(gg_ref[...], wg[rows, :]) + dot_nt(gc_ref[...], wc[rows, :])
        for slot, actions in slots.items():
            if slot < 4 * pieces:

                @pl.when(turn * pieces + q == slot)
                def _():
                    for action in actions:
                        action()

        return 0

    lax.fori_loop(0, pieces, piece, 0)
    gain = vec_ref[0:1, :D]
    total = jnp.zeros((8, D), F32)
    step = 16
    for r in range(0, T, step):
        rows = slice(r, r + step)
        tok = tok_ref[rows].astype(F32)
        rho = lax.rsqrt(jnp.sum(tok * tok, axis=1, keepdims=True) * (1.0 / D) + EPSILON)
        unit = tok * rho
        g = grad[rows]
        total = total + rows8(g * unit)
        e = g * gain
        mean = jnp.sum(e * unit, axis=1, keepdims=True) * (1.0 / D)
        tg_ref[rows] = cot_ref[rows].astype(F32) + rho * (e - unit * mean)
    dpre[...] += total

    @pl.when(turn == last_turn)
    def _():
        vec_sum_all = vec_sum[0:1, :]
        pre = jnp.sum(dpre[...], axis=0, keepdims=True)
        vec_all = jnp.concatenate([pre, vec_sum_all[:, D:]], axis=1)
        parts = small.shape[0] * small.shape[1] if remote else small.shape[0]
        n, m = CONV_CH // parts, VEC // parts
        small[...] = jnp.zeros_like(small)
        for p in range(parts):
            at = (p // 2, p % 2) if remote else (p,)
            small[(*at, slice(0, KERNEL), slice(0, n))] = taps_sum[0:KERNEL, n * p : n * (p + 1)]
            small[(*at, slice(8, 9), slice(0, m))] = vec_all[:, m * p : m * (p + 1)]
        if remote:
            for slot in sorted(slots):
                if slot >= 4 * pieces:
                    for action in slots[slot]:
                        action()
            for end in ends:
                end()
        else:
            small_total[...] = small[...]


def token_call(gg, gc, wg, wc, tok, cot, vec, taps_sum, vec_sum, parts, grad_conv=None):
    remote = grad_conv is not None
    length = tok.shape[0]
    tokens = lambda b: (b, 0)
    hbm = pl.BlockSpec(memory_space=pl.ANY)
    small = (2, 2, 16, SMALL_COLS) if remote else (parts, 16, SMALL_COLS)
    small_out = small[2:] if remote else small
    zeros = (0,) * len(small_out)
    return pl.pallas_call(
        functools.partial(token_kernel, remote),
        grid=(length // T,),
        in_specs=[
            pl.BlockSpec((T, D_INNER), tokens),
            pl.BlockSpec((T, CONV_CH + LANES), tokens),
            hbm,
            hbm,
            pl.BlockSpec((T, D), tokens),
            pl.BlockSpec((T, D), tokens),
            whole(vec.shape),
            whole(taps_sum.shape),
            whole(vec_sum.shape),
            *([hbm] if remote else []),
        ],
        out_specs=[
            pl.BlockSpec((T, D), tokens),
            pl.BlockSpec(small_out, lambda b: zeros),
            *([hbm] if remote else []),
        ],
        out_shape=[
            jax.ShapeDtypeStruct((length, D), F32),
            jax.ShapeDtypeStruct(small_out, F32),
            *([jax.ShapeDtypeStruct(grad_conv.shape[2:], BF16)] if remote else []),
        ],
        scratch_shapes=[
            pltpu.VMEM(wg.shape, BF16),
            pltpu.VMEM(wc.shape, BF16),
            pltpu.VMEM((T, D), F32),
            pltpu.VMEM((8, D), F32),
            pltpu.VMEM(small, F32),
            pltpu.SemaphoreType.DMA((2,)),
            *(
                reduce_buffers(grad_conv.shape[2], CONV_COLS, CONV_CHUNKS)
                + reduce_buffers(grad_conv.shape[2], CONV_LEFT, 1)
                + small_buffers(16, SMALL_COLS)
                + reduce_sems(CONV_CHUNKS + 1)
                + [pltpu.SemaphoreType.DMA((5,)), pltpu.SemaphoreType.DMA((5,))]
                if remote
                else []
            ),
        ],
        compiler_params=pltpu.CompilerParams(
            vmem_limit_bytes=VMEM_LIMIT, **(dict(collective_id=2, has_side_effects=True) if remote else {})
        ),
        cost_estimate=pl.CostEstimate(flops=2 * length * D * 4480, bytes_accessed=22 << 20, transcendentals=0),
    )(gg, gc, wg, wc, tok, cot, vec, taps_sum, vec_sum, *((grad_conv,) if remote else ()))


def adam_step(master, first, second, grad, rate):
    first_new = BETA_FIRST * first + (1.0 - BETA_FIRST) * grad
    second_new = BETA_SECOND * second + (1.0 - BETA_SECOND) * grad * grad
    first_fix = 1.0 - BETA_FIRST**STEP
    second_fix = 1.0 - BETA_SECOND**STEP
    master_new = master - rate * (
        first_new / first_fix / (jnp.sqrt(second_new / second_fix) + ADAM_EPSILON) + WEIGHT_DECAY * master
    )
    return (master_new, first_new, second_new)


def adam_rows(rate, grad, refs, rows):
    ins, outs = refs
    for ref, value in zip(outs, adam_step(*(r[rows] for r in ins), grad, rate)):
        ref[rows] = value


def adam_turned_kernel(rate, tiles, first_ref, second_ref, *refs):
    j = pl.program_id(0)
    for which, grad_ref in enumerate((first_ref, second_ref)):

        @pl.when((j >= tiles) == bool(which))
        def _():
            for r in range(0, 2 * W, LANES):
                rows = slice(r, r + LANES)
                adam_rows(rate, grad_ref[:, rows].astype(F32).T, (refs[:3], refs[3:]), rows)


def adam_kernel(rate, grad_ref, *refs):
    for r in range(0, refs[0].shape[0], 32):
        rows = slice(r, r + 32)
        adam_rows(rate, grad_ref[rows].astype(F32), (refs[:3], refs[3:]), rows)


def adam_call(grads, master, first, second, rate):
    rows, cols = master.shape
    if len(grads) == 2:
        tile = 2 * W
        tiles = grads[0].shape[1] // tile
        kernel = functools.partial(adam_turned_kernel, rate, tiles)
        grad_specs = [
            pl.BlockSpec((cols, tile), lambda j: (0, jnp.minimum(j, tiles - 1))),
            pl.BlockSpec((cols, tile), lambda j: (0, jnp.maximum(j - tiles, 0))),
        ]
    else:
        tile = rows // 4
        kernel = functools.partial(adam_kernel, rate)
        grad_specs = [pl.BlockSpec((tile, cols), lambda j: (j, 0))]
    down = pl.BlockSpec((tile, cols), lambda j: (j, 0))
    return pl.pallas_call(
        kernel,
        grid=(-(-rows // tile),),
        in_specs=[*grad_specs, down, down, down],
        out_specs=[down] * 3,
        out_shape=[jax.ShapeDtypeStruct((rows, cols), F32)] * 3,
        compiler_params=pltpu.CompilerParams(vmem_limit_bytes=VMEM_LIMIT),
        cost_estimate=pl.CostEstimate(flops=0, bytes_accessed=26 * rows * cols, transcendentals=0),
    )(*grads, master, first, second)


def owners(grad, parts, remote):
    return grad.reshape(*((2, 2) if remote else (parts,)), -1, grad.shape[1])


def row_pass(projected, tok, cot, seg, wg, wc, wo, parts, remote):
    act, dsilu, cin, y, states, sraw, nrm, segb, taps, vec, hv, skip = projected
    block_out, mixed, gy, gg, rsum, dgain, dskip = fwd_call(act, y, nrm, tok, cot, wg, wo, vec, skip)
    grad_out = owners(dot_tn(mixed, cot).astype(BF16), parts, remote)
    grad_gate = owners(dot_tn(nrm, gg).astype(BF16), parts, remote)
    gc, dtaps, dhv, *totals = bwd_call(
        act, sraw, segb, seg, gy, states, rsum, dsilu, cin, hv, skip, taps, *((grad_out, grad_gate) if remote else ())
    )
    grad_conv = owners(dot_tn(nrm, gc).astype(BF16), parts, remote)
    dtaps = dtaps.reshape(KERNEL + 1, 8, CONV_CH).sum(1)
    dhv = dhv.reshape(2, 8, LANES).sum(1)
    vec_sum = jnp.concatenate(
        [
            jnp.zeros((D,), F32),
            dgain.sum(0),
            dtaps[KERNEL],
            dhv[0, :H],
            dhv[1, :H],
            dskip.sum(0).reshape(H, P_SIZE).sum(1),
            jnp.zeros((VEC_PAD - VEC,), F32),
        ]
    )[None]
    token_grad, small, *conv_total = token_call(
        gg, gc, wg, wc, tok, cot, vec, dtaps, vec_sum, parts, *((grad_conv,) if remote else ())
    )
    if remote:
        out_total, gate_total = totals
        return block_out, token_grad, gate_total, conv_total[0], out_total, small
    return block_out, token_grad, grad_gate, grad_conv, grad_out, small


def local(
    tokens, cotangent, segment_ids, in_weight, out_weight, filter_weight, vectors,
    in_first, out_first, filter_first, vector_first, in_second, out_second, filter_second, vector_second,
):
    remote = lax.axis_size("grp") == 4 and lax.axis_size("dp") == 8
    parts = D // in_weight.shape[0]
    vec_size = vectors.size
    in_turned = in_weight.T
    small = jnp.pad(filter_weight, ((0, 12), (0, SMALL_COLS - filter_weight.shape[1])))
    small = small.at[8, :vec_size].set(vectors)
    tok, cot = tokens[0], cotangent[0]
    if remote:
        *projected, wg, wc, wo = project_call(tok, segment_ids, in_turned, out_weight, small)
    else:
        in_full = lax.all_gather(in_weight.astype(BF16), "grp", axis=0, tiled=True)
        wo = lax.all_gather(out_weight.astype(BF16), "grp", axis=0, tiled=True)
        slots = lax.all_gather(small, "grp")
        wg = in_full[:, :D_INNER]
        wc = jnp.pad(in_full[:, D_INNER:], ((0, 0), (0, LANES - H)))
        projected = plain_project_call(tok, segment_ids, wc, slots)
    block_out, token_grad, *grads = row_pass(projected, tok, cot, segment_ids, wg, wc, wo, parts, remote)
    if not remote:
        grads = [lax.psum(lax.psum_scatter(g, "grp", scatter_dimension=0, tiled=False), "dp") for g in grads]
    gate_total, conv_total, out_total, small_total = grads
    in_new = [a.T for a in adam_call((gate_total, conv_total), in_turned, in_first.T, in_second.T, 0.03)]
    out_new = adam_call((out_total,), out_weight, out_first, out_second, 0.02)
    filter_new = adam_step(
        filter_weight, filter_first, filter_second, small_total[:KERNEL, : filter_weight.shape[1]], 0.3
    )
    vector_new = adam_step(vectors, vector_first, vector_second, small_total[8, :vec_size], 0.3)
    results = (in_new, out_new, filter_new, vector_new)
    return (block_out[None], token_grad[None], *(r[n] for n in range(3) for r in results))


def solution(mesh):
    rows = P(("grp", "dp"), None, None)
    shards = (P("grp", None), P("grp", None), P(None, "grp"), P("grp"))
    in_specs = (rows, rows, P(("grp", "dp"), None)) + shards * 3
    out_specs = (rows, rows) + shards * 3
    return jax.shard_map(local, mesh=mesh, in_specs=in_specs, out_specs=out_specs, check_vma=False)
```

```python
import functools
import math

import jax
import jax.numpy as jnp
from jax import lax
from jax.experimental import pallas as pl
from jax.experimental.pallas import tpu as pltpu
from jax.sharding import PartitionSpec as P

D = 1024
H = 32
P_SIZE = 64
NSTATE = 128
KERNEL = 4
STEP = 7
D_INNER = 2048
CONV_CH = 2304
XBC = D_INNER + CONV_CH
LANES = 128
T = 256
W = 256
HPT = W // P_SIZE
NT = D_INNER // W
CT = CONV_CH // W
SMALL_COLS = 1408
CHUNK = 32
HEADS_AT = D + D_INNER + CONV_CH
VEC = HEADS_AT + 3 * H
VEC_PAD = 5504
STEP_AT = D_INNER + CONV_CH
ALL = STEP_AT + LANES
LOG2E = math.log2(math.e)

EPSILON = 1e-05
ADAM_EPSILON = 1e-08
BETA_FIRST = 0.5
BETA_SECOND = 0.5
WEIGHT_DECAY = 0.1

F32 = jnp.float32
BF16 = jnp.bfloat16
HIGHEST = lax.Precision.HIGHEST
VMEM_LIMIT = 58 * 1024 * 1024


def dot_nn(a, b):
    return lax.dot_general(a, b, (((1,), (0,)), ((), ())), preferred_element_type=F32)


def dot_nt(a, b):
    return lax.dot_general(a, b, (((1,), (1,)), ((), ())), preferred_element_type=F32)


def dot_tn(a, b):
    return lax.dot_general(a, b, (((0,), (0,)), ((), ())), preferred_element_type=F32)


def sigmoid(v):
    return 0.5 * jnp.tanh(0.5 * v) + 0.5


def rows8(v):
    return jnp.sum(v.reshape(v.shape[0] // 8, 8, v.shape[1]), axis=0)


def tile_of(i):
    return slice(i * W, (i + 1) * W)


def tile_at(i, width=W):
    return pl.ds(pl.multiple_of(i * width, width), width)


def whole(shape):
    zeros = (0,) * len(shape)
    return pl.BlockSpec(shape, lambda *_: zeros, pipeline_mode=pl.Buffered(1))


MESH = pl.DeviceIdType.MESH
HOPS = (("dp", 1), ("grp", 1), ("grp", 2), ("dp", 2), ("dp", 4))
CORE, ALONG_X, ALONG_Y, Z_NEAR, Z_FAR = range(5)


def bit(hop):
    name, size = HOPS[hop]
    return lax.rem(lax.div(lax.axis_index(name), size), 2)


def across(hop):
    name, size = HOPS[hop]
    return {name: lax.axis_index(name) + size * (1 - 2 * bit(hop))}


def greet(hops):
    barrier = pltpu.get_barrier_semaphore()
    for hop in hops:
        pl.semaphore_signal(barrier, inc=1, device_id=across(hop), device_id_type=MESH)
    pl.semaphore_wait(barrier, len(hops))


class Transfer:
    def __init__(self, hop, src, dst, send, recv, ways):
        rows = src.shape[-2]
        lead = (slice(None),) * (len(src.shape) - 2)
        parts = [(*lead, pl.ds(i * rows // ways, rows // ways)) for i in range(ways)]

        def copy(a, b):
            return pltpu.make_async_remote_copy(
                src_ref=a, dst_ref=b, send_sem=send, recv_sem=recv, device_id=across(hop), device_id_type=MESH
            )

        self.parts = [copy(src.at[at], dst.at[at]) for at in parts] if ways > 1 else [copy(src, dst)]
        self.whole = copy(src, dst)

    def start(self):
        for part in self.parts:
            part.start()

    def wait_recv(self):
        self.whole.wait_recv()

    def wait_send(self):
        self.whole.wait_send()


def rows_at(start, size):
    return pl.ds(pl.multiple_of(start, size), size)


def add_rows(out, a, b):
    out[...] = a[...] + b[...]


def reduce_chunk(src, cols, first_x, bufs, total, sends, recvs, index, local_sem):
    own, r1, r2, r3, r4, r0 = bufs
    rows = src.shape[2]
    half, quarter, eighth = rows // 2, rows // 4, rows // 8
    c, x, y, z1, z2 = (bit(hop) for hop in range(5))
    first, second = (ALONG_X, ALONG_Y) if first_x else (ALONG_Y, ALONG_X)
    base = c * half
    base1 = base + z1 * quarter
    base2 = base1 + z2 * eighth

    def copy(n, hop, a, b, ways=1):
        return Transfer(hop, a, b, sends.at[index, n], recvs.at[index, n], ways)

    def pair(u):
        return own.at[:, u] if first_x else own.at[u]

    kept = bit(first)
    load = pltpu.make_async_copy(src.at[:, :, rows_at(base, half), cols], own, local_sem)
    here = [total.at[rows_at(base2, eighth)], total.at[rows_at(base1, quarter)], total.at[rows_at(base, half)]]
    copies = [
        copy(0, CORE, src.at[:, :, rows_at((1 - c) * half, half), cols], r0, 4),
        copy(1, first, pair(1 - kept), r1, 4),
        copy(2, second, r1.at[1 - bit(second)], r2, 4),
        copy(3, Z_NEAR, r2.at[rows_at((1 - z1) * quarter, quarter)], r3, 2),
        copy(4, Z_FAR, r3.at[rows_at((1 - z2) * eighth, eighth)], r4),
        copy(5, Z_FAR, here[0], here[0]),
        copy(6, Z_NEAR, here[1], here[1], 2),
        copy(7, CORE, here[2], here[2], 2),
    ]

    def begin():
        load.start()
        copies[0].start()

    def after_core():
        load.wait()
        copies[0].wait_recv()
        add_rows(own, own, r0)
        copies[1].start()

    def after_first():
        copies[1].wait_recv()
        add_rows(r1, r1, pair(kept))
        copies[2].start()

    def after_second():
        copies[2].wait_recv()
        add_rows(r2, r2, r1.at[bit(second)])
        copies[3].start()

    def after_near():
        copies[3].wait_recv()
        add_rows(r3, r3, r2.at[rows_at(z1 * quarter, quarter)])
        copies[4].start()

    def after_far():
        copies[4].wait_recv()
        add_rows(here[0], r4, r3.at[rows_at(z2 * eighth, eighth)])
        copies[5].start()

    def gather_far():
        copies[5].wait_recv()
        copies[6].start()

    def gather_near():
        copies[6].wait_recv()
        copies[7].start()

    def arrive():
        copies[7].wait_recv()

    def finish():
        for one in copies:
            one.wait_send()

    return (begin, after_core, after_first, after_second, after_near, after_far, gather_far, gather_near, arrive), finish


def reduce_buffers(rows, cols, count, dtype=BF16):
    half = rows // 2
    shapes = [
        (2, 2, half, cols), (2, 2, half, cols), (2, half, cols), (half, cols), (half // 2, cols), (half // 4, cols), (rows, cols),
    ]
    return [pltpu.VMEM((count, *shape), dtype) for shape in shapes]


BUFFERS = 7
STAGES = 9


def reduce_plan(src, starts, size, slots, pace, bufs, result, sems, base, x_first):
    local_sems, out_sems, sends, recvs = sems
    ticks, ends = [], []
    for n, (start, slot) in enumerate(zip(starts, slots)):
        index = base + n
        own, r0, r1, r2, r3, r4, total = (ref.at[n] for ref in bufs)
        cols = pl.ds(start, size)
        stages, finish = reduce_chunk(
            src, cols, x_first[n], (own, r1, r2, r3, r4, r0), total, sends, recvs, index, local_sems.at[index]
        )
        write = pltpu.make_async_copy(total, result.at[:, cols], out_sems.at[index])
        for later, stage in zip(pace, stages):
            ticks.append((slot + later, stage))
        ticks.append((slot + pace[-1], write.start))
        ends += [finish, write.wait]
    return ticks, ends


def small_plan(src, bufs, total, sems, slot, spacing):
    sends, recvs = sems
    r0, a1, r1, a2, r2, a3, r3, a4, r4 = bufs
    x, y = bit(ALONG_X), bit(ALONG_Y)

    def copy(n, hop, a, b):
        return pltpu.make_async_remote_copy(
            src_ref=a, dst_ref=b, send_sem=sends.at[n], recv_sem=recvs.at[n], device_id=across(hop), device_id_type=MESH
        )

    copies = [
        copy(0, CORE, src, r0),
        copy(1, ALONG_X, a1.at[:, 1 - x], r1),
        copy(2, ALONG_Y, a2.at[1 - y], r2),
        copy(3, Z_NEAR, a3, r3),
        copy(4, Z_FAR, a4, r4),
    ]

    def after(n, out, one, other):
        def stage():
            copies[n].wait_recv()
            out[...] = one[...] + other[...]
            if n < 4:
                copies[n + 1].start()

        return stage

    stages = [
        copies[0].start,
        after(0, a1, src, r0),
        after(1, a2, a1.at[:, x], r1),
        after(2, a3, a2.at[y], r2),
        after(3, a4, a3, r3),
        after(4, total, a4, r4),
    ]
    return [(slot + k * spacing, stage) for k, stage in enumerate(stages)], [one.wait_send for one in copies]


def small_buffers(rows, cols):
    shapes = [(2, 2, rows, cols), (2, 2, rows, cols), (2, rows, cols), (2, rows, cols)] + [(rows, cols)] * 5
    return [pltpu.VMEM(shape, F32) for shape in shapes]


def by_slot(ticks):
    slots = {}
    for slot, action in ticks:
        slots.setdefault(slot, []).append(action)
    return slots


def head_terms(sraw_ref, hv_ref):
    v = sraw_ref[...] + hv_ref[0:1, :]
    step = jnp.maximum(v, 0.0) + jnp.log1p(jnp.exp(-jnp.abs(v)))
    rate = -jnp.exp(hv_ref[1:2, :])
    return v, step, rate


def before(rows, cols):
    return lax.broadcasted_iota(jnp.int32, (rows, cols), 0), lax.broadcasted_iota(jnp.int32, (rows, cols), 1)


def cumulate(logdecay):
    t, s = before(T, T)
    lower = jnp.where(s <= t, 1.0, 0.0)
    return jnp.dot(lower, logdecay * LOG2E, precision=HIGHEST, preferred_element_type=F32)


def spread(cum, cum_b):
    for h in range(H):
        cum_b[h] = jnp.broadcast_to(cum[:, h : h + 1], (T, LANES))


def expand(values, fan, out):
    high = values.astype(BF16)
    low = (values - high.astype(F32)).astype(BF16)
    both = jnp.concatenate([high, low], axis=1)
    for c in range(0, D_INNER, 2 * W):
        out[:, c : c + 2 * W] = dot_nn(both, fan[:, c : c + 2 * W])


def set_fan(fan):
    for c in range(0, D_INNER, W):
        row, lane = before(2 * LANES, W)
        fan[:, c : c + W] = jnp.where(lax.shift_right_logical(lane + c, 6) == (row & (LANES - 1)), 1.0, 0.0).astype(BF16)


def put_diagonal(diag, r, tile):
    lane = lax.broadcasted_iota(jnp.int32, (tile.shape[0], LANES), 1)
    first = jnp.where(lane < P_SIZE, 1.0, 0.0).astype(BF16)
    second = jnp.where(lane < P_SIZE, 0.0, 1.0).astype(BF16)
    for k in range(HPT):
        at = LANES * (k // 2)
        part = tile[:, at : at + LANES]
        diag[k * T + r : k * T + r + tile.shape[0], at : at + LANES] = part * (first if k % 2 == 0 else second)


def from_start_last(cum_b, i):
    lane = lax.broadcasted_iota(jnp.int32, (1, LANES), 1)
    last = slice(T - 1, T)
    halves = [jnp.where(lane < P_SIZE, cum_b[HPT * i + 2 * k, last], cum_b[HPT * i + 2 * k + 1, last]) for k in range(2)]
    return jnp.exp2(jnp.concatenate(halves, axis=1))


def wide(m):
    return jnp.concatenate([m, m], axis=1)


def split_halves(values, high_ref, low_ref, rows):
    high = values.astype(BF16)
    high_ref[rows] = high
    low_ref[rows] = (values - high.astype(F32)).astype(BF16)


def head_sums(high_ref, low_ref, pick):
    return dot_nn(high_ref[...], pick) + dot_nn(low_ref[...], pick)


def set_pick(pick):
    for r in range(0, D_INNER, T):
        row, lane = before(T, LANES)
        pick[r : r + T] = jnp.where(lax.shift_right_logical(row + r, 6) == lane, 1.0, 0.0).astype(BF16)


def chunks(start=0, stop=T):
    return [slice(r, r + CHUNK) for r in range(start, stop, CHUNK)]


def scan_forward(block, act, sraw_ref, segb_ref, seg_ref, hv_ref, skip_ref, y_ref, st_ref, scratch):
    (
        state, cum_b, fan, wcat, cum_rows, xw_scr, carr_scr, diag, scores, prev_seg, step_f, from_start, to_end,
    ) = scratch
    tokens = rows_at(block * T, T)

    @pl.when(block == 0)
    def _():
        state[...] = jnp.zeros_like(state)
        wcat[...] = jnp.zeros_like(wcat)
        diag[...] = jnp.zeros_like(diag)
        prev_seg[...] = jnp.full(prev_seg.shape, -1.0, F32)
        set_fan(fan)

    _, step, rate = head_terms(sraw_ref.at[tokens], hv_ref)
    cum = cumulate(step * rate)
    cum_rows[...] = cum.T
    spread(cum, cum_b)
    bmat = act[tokens, D_INNER : D_INNER + NSTATE]
    cmat = act[tokens, D_INNER + NSTATE : CONV_CH]
    segb = segb_ref[tokens]
    t_at, s_at = before(T, T)
    valid = (wide(segb) == seg_ref[0:1, tokens].astype(F32)) & (s_at <= t_at)
    scores[...] = jnp.where(valid, dot_nt(cmat, bmat), 0.0).astype(BF16)
    prev = prev_seg[0:1]
    last_seg = segb[T - 1 : T]
    last = cum[T - 1 : T]
    expand(step, fan, step_f)
    expand(jnp.exp2(cum) * jnp.where(segb == prev, 1.0, 0.0), fan, from_start)
    expand(jnp.exp2(last - cum) * jnp.where(segb == last_seg, 1.0, 0.0), fan, to_end)
    keep = wide(jnp.where(last_seg == prev, 1.0, 0.0))
    prev_seg[0:1] = last_seg
    b_t = bmat.astype(F32).T.astype(BF16)
    st_ref[0] = state[...].astype(BF16)
    carr_scr[...] = dot_nn(cmat, st_ref[0])

    def here(rows):
        return pl.ds(pl.multiple_of(block * T + rows.start, CHUNK), CHUNK)

    def prepare(i, p):
        cols = tile_of(i)
        for rows in chunks():
            x1 = (act[here(rows), cols].astype(F32) * step_f[rows, cols]).astype(BF16)
            put_diagonal(diag.at[p], rows.start, x1)
            xw_scr[rows, cols] = (x1.astype(F32) * to_end[rows, cols]).astype(BF16)
        for k in range(HPT):
            row = cum_rows[HPT * i + k : HPT * i + k + 1, :]
            for rows in chunks():
                n = LANES if rows.start < LANES else T
                colb = cum_b[HPT * i + k, rows]
                colb = colb if n == LANES else wide(colb)
                decay = jnp.exp2(jnp.minimum(colb - row[:, :n], 0.0)).astype(BF16)
                wcat[p, rows, k * T : k * T + n] = scores[rows, :n] * decay

    prepare(0, 0)
    for i in range(NT):
        cols = tile_of(i)
        y_ref[:, cols] = dot_nn(wcat[i % 2], diag[i % 2])
        if i + 1 < NT:
            prepare(i + 1, (i + 1) % 2)
        skip = skip_ref[0:1, cols]
        for rows in chunks():
            y = y_ref[rows, cols] + carr_scr[rows, cols] * from_start[rows, cols]
            y_ref[rows, cols] = y + act[here(rows), cols].astype(F32) * skip
        fade = from_start_last(cum_b, i) * keep
        for rows in chunks(0, NSTATE):
            state[rows, cols] = state[rows, cols] * fade
    state[...] += dot_nn(b_t, xw_scr[...])


def scan_scratch():
    return [
        pltpu.VMEM((NSTATE, D_INNER), F32),
        pltpu.VMEM((H, T, LANES), F32),
        pltpu.VMEM((2 * LANES, D_INNER), BF16),
        pltpu.VMEM((2, T, HPT * T), BF16),
        pltpu.VMEM((LANES, T), F32),
        pltpu.VMEM((T, D_INNER), BF16),
        pltpu.VMEM((T, D_INNER), F32),
        pltpu.VMEM((2, HPT * T, W), BF16),
        pltpu.VMEM((T, T), BF16),
        pltpu.VMEM((8, LANES), F32),
        pltpu.VMEM((T, D_INNER), F32),
        pltpu.VMEM((T, D_INNER), F32),
        pltpu.VMEM((T, D_INNER), F32),
    ]


def norm_rows(tok_ref, gain, nrm_ref):
    def body(i, _):
        rows = pl.ds(pl.multiple_of(i * CHUNK, CHUNK), CHUNK)
        tok = tok_ref[rows].astype(F32)
        rho = lax.rsqrt(jnp.sum(tok * tok, axis=1, keepdims=True) * (1.0 / D) + EPSILON)
        nrm_ref[rows] = (tok * rho * gain).astype(BF16)
        return 0

    lax.fori_loop(0, tok_ref.shape[0] // CHUNK, body, 0)


def segment_masks(seg_ref, segb_ref, pad, mask):
    length = segb_ref.shape[0]
    column = jnp.broadcast_to(seg_ref[...].astype(F32), (8, length)).T
    pad[0:8] = jnp.full((8, LANES), -1.0, F32)
    for r in range(0, length, T):
        rows = jnp.broadcast_to(column[r : r + T, 0:1], (T, LANES))
        segb_ref[r : r + T] = rows
        pad[8 + r : 8 + r + T] = rows
    for k in range(1, KERNEL):
        for r in range(0, length, T):
            mask[k - 1, r : r + T] = jnp.where(pad[8 + r - k : 8 + r - k + T] == segb_ref[r : r + T], 1.0, 0.0)


def unpack_small(slots, taps_ref, vec_ref, hv_ref, skip_ref):
    parts = slots.shape[0]
    taps_ref[...] = jnp.zeros_like(taps_ref)
    vec_ref[...] = jnp.zeros_like(vec_ref)
    hv_ref[...] = jnp.zeros_like(hv_ref)
    skip_ref[...] = jnp.zeros_like(skip_ref)
    n, m = CONV_CH // parts, VEC // parts
    for p in range(parts):
        taps_ref[0:KERNEL, n * p : n * (p + 1)] = slots[p, 0:KERNEL, 0:n].astype(BF16).astype(F32)
        vec_ref[0:1, m * p : m * (p + 1)] = slots[p, 8:9, 0:m].astype(BF16).astype(F32)
    for k in range(2):
        hv_ref[k : k + 1, 0:H] = vec_ref[0:1, HEADS_AT + k * H : HEADS_AT + (k + 1) * H]
    for h in range(H):
        at = HEADS_AT + 2 * H + h
        skip_ref[0:1, P_SIZE * h : P_SIZE * (h + 1)] = jnp.broadcast_to(vec_ref[0:1, at : at + 1], (1, P_SIZE))


def conv_tile(j, nrm_ref, w, taps_ref, vec_ref, mask, act_ref, dsilu_ref, cin_ref, pad):
    length = nrm_ref.shape[0]
    pad[0:8] = jnp.zeros((8, W), F32)
    cols = tile_at(j)
    taps = [taps_ref[k : k + 1, cols] for k in range(KERNEL)]
    bias = vec_ref[0:1, pl.ds(pl.multiple_of(D + D_INNER + j * W, W), W)]
    def product(top):
        pad[8 + top : 8 + top + T] = dot_nn(nrm_ref[top : top + T], w[:, cols])

    product(0)
    for top in range(0, length, T):
        if top + T < length:
            product(top + T)
        for r in range(top, top + T, CHUNK):
            here = pad[8 + r : 8 + r + CHUNK]
            cin_ref[r : r + CHUNK] = here.astype(BF16)
            total = bias + here * taps[0]
            for k in range(1, KERNEL):
                m = wide(mask[k - 1, r : r + CHUNK])
                total = total + pad[8 + r - k : 8 + r - k + CHUNK] * m * taps[k]
            sig = sigmoid(total)
            act = total * sig
            act_ref[r : r + CHUNK] = act.astype(BF16)
            dsilu_ref[r : r + CHUNK] = (sig + act * (1.0 - sig)).astype(BF16)


def weight_piece(src, src_cols, put, hop_sems, index, rows):
    sends, recvs = hop_sems
    half, quarter = rows // 2, rows // 4
    me = lax.axis_index("grp")
    x, y = bit(ALONG_X), bit(ALONG_Y)
    slot_x, slot_y, slot_d = 2 * y + 1 - x, 2 * (1 - y) + x, 2 * (1 - y) + 1 - x
    top = bit(CORE) * half

    def copy(n, a, b, hop):
        return Transfer(hop, a, b, sends.at[index, n], recvs.at[index, n], 2)

    def onward(n, slot, start, size, hop):
        return copy(n, put(slot * rows + start, size), put(slot * rows + start, size), hop)

    mine = src.at[rows_at(top, half), src_cols]
    copies = [
        copy(0, mine, put(me * rows + top, half), ALONG_X),
        copy(1, mine, put(me * rows + top, half), ALONG_Y),
        onward(2, slot_x, top, quarter, ALONG_Y),
        onward(3, slot_y, top + quarter, quarter, ALONG_X),
        onward(4, slot_x, top, half, CORE),
        onward(5, slot_y, top, half, CORE),
        onward(6, slot_d, top, quarter, CORE),
        onward(7, slot_d, top + quarter, quarter, CORE),
    ]

    def own():
        copies[0].start()
        copies[1].start()

    def pass_on():
        copies[0].wait_recv()
        copies[2].start()
        copies[1].wait_recv()
        copies[3].start()
        copies[4].start()
        copies[5].start()

    def corner():
        copies[2].wait_recv()
        copies[6].start()
        copies[3].wait_recv()
        copies[7].start()

    def arrive():
        for n in range(4, 8):
            copies[n].wait_recv()

    def finish():
        for one in copies:
            one.wait_send()

    return own, pass_on, corner, arrive, finish


def project_kernel(
    tok_ref, seg_ref, wt_ref, wo_ref, small_ref,
    act_ref, dsilu_ref, cin_ref, y_ref, st_ref, sraw_ref, nrm_ref, segb_ref, taps_ref, vec_ref, hv_ref, skip_ref,
    wg_full, wc_full, wo_full,
    wt_f32, wo_f32, stage_in, stage_out, conv_full, slots, pad, segpad, mask, act, *rest,
):
    *scan, local_sems, sends, recvs, small_sends, small_recvs = rest
    j = pl.program_id(0)
    me = lax.axis_index("grp")
    rows_in, rows_out = D // 4, D_INNER // 4
    load_conv = pltpu.make_async_copy(wt_ref.at[D_INNER:], wt_f32.at[D_INNER : D_INNER + CONV_CH + H], local_sems.at[0])
    load_gate = pltpu.make_async_copy(wt_ref.at[:D_INNER], wt_f32.at[:D_INNER], local_sems.at[1])
    load_out = pltpu.make_async_copy(wo_ref, wo_f32, local_sems.at[2])
    keep_conv = pltpu.make_async_copy(
        stage_in.at[:, D_INNER:], conv_full.at[rows_at(me * rows_in, rows_in)], local_sems.at[3]
    )
    keep_gate = pltpu.make_async_copy(
        stage_in.at[:, :D_INNER], wg_full.at[rows_at(me * rows_in, rows_in)], local_sems.at[4]
    )
    keep_out = pltpu.make_async_copy(stage_out, wo_full.at[rows_at(me * rows_out, rows_out)], local_sems.at[5])
    write_conv = pltpu.make_async_copy(conv_full, wc_full, local_sems.at[6])

    def small_copy(n, a, b, hop):
        return pltpu.make_async_remote_copy(
            src_ref=a, dst_ref=b, send_sem=small_sends.at[n], recv_sem=small_recvs.at[n],
            device_id=across(hop), device_id_type=MESH,
        )

    x, y = bit(ALONG_X), bit(ALONG_Y)
    slot_x, slot_y = 2 * y + 1 - x, 2 * (1 - y) + x
    smalls = [
        small_copy(0, small_ref, slots.at[me], ALONG_X),
        small_copy(1, small_ref, slots.at[me], ALONG_Y),
        small_copy(2, slots.at[slot_x, 0:8], slots.at[slot_x, 0:8], ALONG_Y),
        small_copy(3, slots.at[slot_y, 8:16], slots.at[slot_y, 8:16], ALONG_X),
    ]

    def conv_put(start, size):
        return lambda at, n: conv_full.at[rows_at(at, n), start : start + size]

    def gate_put(start, size):
        return lambda at, n: wg_full.at[rows_at(at, n), start : start + size]

    def out_put(start, size):
        return lambda at, n: wo_full.at[rows_at(at, n), start : start + size]

    sems = (sends, recvs)
    pieces = []
    for start, size in ((0, 768), (768, 768), (1536, 896)):
        pieces.append(weight_piece(
            stage_in, slice(D_INNER + start, D_INNER + start + size), conv_put(start, size), sems, len(pieces), rows_in))
    for start, size in ((0, 1024), (1024, 1024)):
        pieces.append(weight_piece(stage_in, slice(start, start + size), gate_put(start, size), sems, len(pieces), rows_in))
    for start, size in ((0, 512), (512, 512)):
        pieces.append(weight_piece(stage_out, slice(start, start + size), out_put(start, size), sems, len(pieces), rows_out))
    OWN, PASS, CORNER, ARRIVE, FINISH = range(5)

    def turn(start, count):
        def body(i, _):
            at = pl.ds(pl.multiple_of(start + i * LANES, LANES), LANES)
            stage_in[:, at] = wt_f32[at, :].T.astype(BF16)
            return 0

        lax.fori_loop(0, count, body, 0)

    @pl.when(j == 0)
    def _():
        load_conv.start()
        load_gate.start()
        load_out.start()
        wt_f32[STEP_AT + H : ALL] = jnp.zeros((LANES - H, wt_f32.shape[1]), F32)
        greet((CORE, ALONG_X, ALONG_Y))
        smalls[0].start()
        smalls[1].start()
        load_conv.wait()
        turn(D_INNER, 6)
        pieces[0][OWN]()
        smalls[0].wait_recv()
        smalls[2].start()
        smalls[1].wait_recv()
        smalls[3].start()
        slots[me] = small_ref[...]
        turn(D_INNER + 768, 6)
        pieces[1][OWN]()
        segment_masks(seg_ref, segb_ref, segpad, mask)
        pieces[0][PASS]()
        smalls[2].wait_recv()
        smalls[3].wait_recv()
        unpack_small(slots, taps_ref, vec_ref, hv_ref, skip_ref)
        turn(D_INNER + 1536, 7)
        keep_conv.start()
        pieces[0][CORNER]()
        pieces[2][OWN]()
        pieces[1][PASS]()
        norm_rows(tok_ref, vec_ref[0:1, :D], nrm_ref)
        keep_conv.wait()
        pieces[0][ARRIVE]()

    @pl.when(j == 1)
    def _():
        pieces[1][CORNER]()
        pieces[2][PASS]()
        load_gate.wait()
        turn(0, 16)
        keep_gate.start()
        pieces[3][OWN]()

    @pl.when(j == 3)
    def _():
        pieces[1][ARRIVE]()
        pieces[2][CORNER]()
        load_out.wait()

        def cast(i, _):
            at = pl.ds(pl.multiple_of(i * 32, 32), 32)
            stage_out[at] = wo_f32[at].astype(BF16)
            return 0

        lax.fori_loop(0, rows_out // 32, cast, 0)
        keep_out.start()
        pieces[4][OWN]()

    @pl.when(j == 4)
    def _():
        pieces[3][PASS]()

    @pl.when(j == 6)
    def _():
        pieces[2][ARRIVE]()
        write_conv.start()
        sraw_ref[...] = dot_nn(nrm_ref[...], conv_full[:, CONV_CH:])
        pieces[3][CORNER]()
        pieces[4][PASS]()
        pieces[5][OWN]()

    @pl.when(j == 8)
    def _():
        pieces[4][CORNER]()
        pieces[6][OWN]()

    @pl.when(j < CT)
    def _():
        conv_tile(j, nrm_ref, conv_full, taps_ref, vec_ref, mask, act_ref, dsilu_ref, cin_ref, pad)
        act[:, tile_at(j)] = act_ref[...]

    @pl.when(j == CT)
    def _():
        pieces[5][PASS]()

    @pl.when(j == CT + 1)
    def _():
        pieces[5][CORNER]()
        pieces[6][PASS]()

    @pl.when(j == CT + 2)
    def _():
        pieces[6][CORNER]()

    @pl.when(j >= CT)
    def _():
        scan_forward(j - CT, act, sraw_ref, segb_ref, seg_ref, hv_ref, skip_ref, y_ref, st_ref, scan)

    @pl.when(j == pl.num_programs(0) - 1)
    def _():
        for n in range(3, 7):
            pieces[n][ARRIVE]()
        for piece in pieces:
            piece[FINISH]()
        for one in smalls:
            one.wait_send()
        keep_gate.wait()
        keep_out.wait()
        write_conv.wait()


def plain_project_kernel(
    tok_ref, seg_ref, w_ref, slots,
    act_ref, dsilu_ref, cin_ref, y_ref, st_ref, sraw_ref, nrm_ref, segb_ref, taps_ref, vec_ref, hv_ref, skip_ref,
    pad, segpad, mask, act, *scan,
):
    j = pl.program_id(0)

    @pl.when(j == 0)
    def _():
        segment_masks(seg_ref, segb_ref, segpad, mask)
        unpack_small(slots, taps_ref, vec_ref, hv_ref, skip_ref)
        norm_rows(tok_ref, vec_ref[0:1, :D], nrm_ref)
        sraw_ref[...] = dot_nn(nrm_ref[...], w_ref[:, CONV_CH:])

    @pl.when(j < CT)
    def _():
        conv_tile(j, nrm_ref, w_ref, taps_ref, vec_ref, mask, act_ref, dsilu_ref, cin_ref, pad)
        act[:, tile_at(j)] = act_ref[...]

    @pl.when(j >= CT)
    def _():
        scan_forward(j - CT, act, sraw_ref, segb_ref, seg_ref, hv_ref, skip_ref, y_ref, st_ref, scan)


def project_outputs(length):
    col = lambda j: (0, jnp.minimum(j, CT - 1))
    fixed = lambda j: (0, 0)
    shapes = [((length, CONV_CH), BF16)] * 3 + [((length, D_INNER), F32), ((length // T, NSTATE, D_INNER), BF16)]
    specs = [pl.BlockSpec((length, W), col)] * 3 + [
        pl.BlockSpec((T, D_INNER), lambda j: (jnp.maximum(j - CT, 0), 0)),
        pl.BlockSpec((1, NSTATE, D_INNER), lambda j: (jnp.maximum(j - CT, 0), 0, 0)),
    ]
    for shape, dtype in (
        ((length, LANES), F32), ((length, D), BF16), ((length, LANES), F32), ((8, CONV_CH), F32), ((8, VEC_PAD), F32),
        ((8, LANES), F32), ((8, D_INNER), F32),
    ):
        shapes.append((shape, dtype))
        specs.append(pl.BlockSpec(shape, fixed))
    scratch = [
        pltpu.VMEM((8 + length, W), F32),
        pltpu.VMEM((8 + length, LANES), F32),
        pltpu.VMEM((KERNEL - 1, length, LANES), F32),
        pltpu.VMEM((length, CONV_CH), BF16),
        *scan_scratch(),
    ]
    return [jax.ShapeDtypeStruct(*one) for one in shapes], specs, scratch


def project_call(tok, seg, wt, wo, small):
    length = tok.shape[0]
    shapes, specs, scratch = project_outputs(length)
    hbm = pl.BlockSpec(memory_space=pl.ANY)
    shapes += [jax.ShapeDtypeStruct(shape, BF16) for shape in ((D, D_INNER), (D, CONV_CH + LANES), (D_INNER, D))]
    return pl.pallas_call(
        project_kernel,
        grid=(CT + length // T,),
        in_specs=[whole(tok.shape), whole(seg.shape), hbm, hbm, whole(small.shape)],
        out_specs=specs + [hbm] * 3,
        out_shape=shapes,
        scratch_shapes=[
            pltpu.VMEM((ALL, D // 4), F32),
            pltpu.VMEM((D_INNER // 4, D), F32),
            pltpu.VMEM((D // 4, ALL), BF16),
            pltpu.VMEM((D_INNER // 4, D), BF16),
            pltpu.VMEM((D, CONV_CH + LANES), BF16),
            pltpu.VMEM((4, *small.shape), F32),
            *scratch,
            pltpu.SemaphoreType.DMA((7,)),
            pltpu.SemaphoreType.DMA((7, 8)),
            pltpu.SemaphoreType.DMA((7, 8)),
            pltpu.SemaphoreType.DMA((4,)),
            pltpu.SemaphoreType.DMA((4,)),
        ],
        compiler_params=pltpu.CompilerParams(collective_id=0, has_side_effects=True, vmem_limit_bytes=VMEM_LIMIT),
        cost_estimate=pl.CostEstimate(flops=2 * length * D * CONV_CH, bytes_accessed=40 << 20, transcendentals=0),
    )(tok, seg, wt, wo, small)


def plain_project_call(tok, seg, w_conv, slots):
    length = tok.shape[0]
    shapes, specs, scratch = project_outputs(length)
    return pl.pallas_call(
        plain_project_kernel,
        grid=(CT + length // T,),
        in_specs=[whole(tok.shape), whole(seg.shape), whole(w_conv.shape), whole(slots.shape)],
        out_specs=specs,
        out_shape=shapes,
        scratch_shapes=scratch,
        compiler_params=pltpu.CompilerParams(vmem_limit_bytes=VMEM_LIMIT),
        cost_estimate=pl.CostEstimate(flops=2 * length * D * CONV_CH, bytes_accessed=20 << 20, transcendentals=0),
    )(tok, seg, w_conv, slots)


def fwd_kernel(
    xs_ref, y_ref, nrm_ref, tok_ref, cot_ref, wg_ref, wo_ref, vec_ref, skip_ref,
    out_ref, mixed_ref, gy_ref, gg_ref, rsum_ref, dgain_ref, dskip_ref,
    silu_scr, sig_scr, gated_scr, gm_scr, sums, rho_b, high, low, pick,
):
    block = pl.program_id(0)

    @pl.when(block == 0)
    def _():
        dgain_ref[...] = jnp.zeros_like(dgain_ref)
        dskip_ref[...] = jnp.zeros_like(dskip_ref)
        set_pick(pick)

    sums[...] = jnp.zeros_like(sums)

    def gate_product(i):
        cols = tile_of(i)
        silu_scr[:, cols] = dot_nn(nrm_ref[...], wg_ref[:, cols])

    gate_product(0)
    for i in range(NT):
        if i + 1 < NT:
            gate_product(i + 1)
        cols = tile_of(i)
        for rows in chunks():
            gate = silu_scr[rows, cols]
            sig = sigmoid(gate)
            silu = gate * sig
            sig_scr[rows, cols] = sig
            silu_scr[rows, cols] = silu
            gated = y_ref[rows, cols] * silu
            gated_scr[rows, cols] = gated
            g2 = gated * gated
            sums[rows] += g2[:, :LANES] + g2[:, LANES:]

    def mixed_product(i):
        cols = tile_of(i)
        gm_scr[:, cols] = dot_nt(cot_ref[...], wo_ref[cols, :])

    mixed_product(0)
    mean2 = jnp.sum(sums[...], axis=1, keepdims=True) * (1.0 / D_INNER)
    rho_b[...] = jnp.broadcast_to(lax.rsqrt(mean2 + EPSILON), (T, LANES))
    sums[...] = jnp.zeros_like(sums)

    for i in range(NT):
        if i + 1 < NT:
            mixed_product(i + 1)
        cols = tile_of(i)
        gain = vec_ref[0:1, D + i * W : D + (i + 1) * W]
        total = jnp.zeros((8, W), F32)
        for rows in chunks():
            gated = gated_scr[rows, cols]
            unit = gated * wide(rho_b[rows])
            mixed_ref[rows, cols] = (unit * gain).astype(BF16)
            gm = gm_scr[rows, cols]
            total = total + rows8(gm * unit)
            e = gm * gain
            gm_scr[rows, cols] = e
            eg = e * gated
            sums[rows] += eg[:, :LANES] + eg[:, LANES:]
        dgain_ref[:, cols] += total

    rho = rho_b[...]
    inner = jnp.sum(sums[...], axis=1, keepdims=True) * (1.0 / D_INNER)
    sums[...] = inner * rho * rho * rho
    rsum_ref[...] = jnp.zeros_like(rsum_ref)

    def out_product(j):
        cols = tile_of(j)
        branch = dot_nn(mixed_ref[...], wo_ref[:, cols])
        out_ref[:, cols] = (tok_ref[:, cols].astype(F32) + branch).astype(BF16)

    for i in range(NT):
        if i % 2 == 0:
            out_product(i // 2)
        cols = tile_of(i)
        skip = skip_ref[0:1, cols]
        total = jnp.zeros((8, W), F32)
        p = i % 2
        for rows in chunks():
            sig = sig_scr[rows, cols]
            silu = silu_scr[rows, cols]
            y = y_ref[rows, cols]
            grad_gated = wide(rho_b[rows]) * gm_scr[rows, cols] - gated_scr[rows, cols] * wide(sums[rows])
            gg_ref[rows, cols] = (grad_gated * y * (sig + silu * (1.0 - sig))).astype(BF16)
            gy = (grad_gated * silu).astype(BF16)
            gy_ref[rows, cols] = gy
            gy = gy.astype(F32)
            xs = xs_ref[rows, cols].astype(F32)
            total = total + rows8(gy * xs)
            split_halves(gy * (y - xs * skip), high.at[p], low.at[p], rows)
        dskip_ref[:, cols] += total
        rsum_ref[...] += head_sums(high.at[p], low.at[p], pick[cols, :])


def fwd_call(xs_bc, y, nrm, tok, cot, wg, wo, vec, skip):
    length = nrm.shape[0]
    blocks = length // T
    tokens = lambda b: (b, 0)
    fixed = lambda b: (0, 0)
    wide_block = pl.BlockSpec((T, D_INNER), tokens)
    return pl.pallas_call(
        fwd_kernel,
        grid=(blocks,),
        in_specs=[
            wide_block,
            wide_block,
            pl.BlockSpec((T, D), tokens),
            pl.BlockSpec((T, D), tokens),
            pl.BlockSpec((T, D), tokens),
            whole(wg.shape),
            whole(wo.shape),
            whole(vec.shape),
            whole(skip.shape),
        ],
        out_specs=[
            pl.BlockSpec((T, D), tokens),
            wide_block,
            wide_block,
            wide_block,
            pl.BlockSpec((T, LANES), tokens),
            pl.BlockSpec((8, D_INNER), fixed),
            pl.BlockSpec((8, D_INNER), fixed),
        ],
        out_shape=[
            jax.ShapeDtypeStruct((length, D), BF16),
            jax.ShapeDtypeStruct((length, D_INNER), BF16),
            jax.ShapeDtypeStruct((length, D_INNER), BF16),
            jax.ShapeDtypeStruct((length, D_INNER), BF16),
            jax.ShapeDtypeStruct((length, LANES), F32),
            jax.ShapeDtypeStruct((8, D_INNER), F32),
            jax.ShapeDtypeStruct((8, D_INNER), F32),
        ],
        scratch_shapes=[
            pltpu.VMEM((T, D_INNER), F32),
            pltpu.VMEM((T, D_INNER), F32),
            pltpu.VMEM((T, D_INNER), F32),
            pltpu.VMEM((T, D_INNER), F32),
            pltpu.VMEM((T, LANES), F32),
            pltpu.VMEM((T, LANES), F32),
            pltpu.VMEM((2, T, W), BF16),
            pltpu.VMEM((2, T, W), BF16),
            pltpu.VMEM((D_INNER, LANES), BF16),
        ],
        compiler_params=pltpu.CompilerParams(vmem_limit_bytes=VMEM_LIMIT),
        cost_estimate=pl.CostEstimate(flops=2 * length * D * D_INNER * 3, bytes_accessed=40 << 20, transcendentals=0),
    )(xs_bc, y, nrm, tok, cot, wg, wo, vec, skip)


def bwd_kernel(remote, *refs):
    if remote:
        ticks, ends, refs = gate_out_plan(refs)
        slots = by_slot(ticks)
    (
        xs_ref, bc_ref, sraw_ref, segb_ref, seg_ref, prev_ref, gy_ref, st_ref, rsum_ref, dsilu_ref, cin_ref,
        hv_ref, skip_ref, taps_ref,
        gc_ref, dtaps_ref, dhv_ref,
        gstate, cum_b, fan, wcat, cum_rows, gf, gscore, gyw_scr, xw_scr, back_scr, through, diag_x, diag_y, gw_scr, gx_scr,
        scores, x1_scr, high, low, high_s, pick, segpad, mask, inner_ref, outer_ref, step_f, from_start, to_end,
    ) = refs
    turn = pl.program_id(0)
    last_turn = pl.num_programs(0) - 1

    @pl.when(turn == 0)
    def _():
        gstate[...] = jnp.zeros_like(gstate)
        wcat[...] = jnp.zeros_like(wcat)
        diag_x[...] = jnp.zeros_like(diag_x)
        diag_y[...] = jnp.zeros_like(diag_y)
        dtaps_ref[...] = jnp.zeros_like(dtaps_ref)
        dhv_ref[...] = jnp.zeros_like(dhv_ref)
        gf[T : T + 8] = jnp.zeros((8, CONV_CH), F32)
        segpad[T : T + 8] = jnp.full((8, LANES), -1.0, F32)
        set_pick(pick)
        set_fan(fan)
        if remote:
            greet(range(5))

    @pl.when(turn > 0)
    def _():
        gf[T : T + 8] = gf[0:8]
        segpad[T : T + 8] = segpad[0:8]

    segb = segb_ref[...]
    segpad[0:T] = segb
    for k in range(1, KERNEL):
        mask[k - 1] = jnp.where(segpad[k : k + T] == segb, 1.0, 0.0)
    v, step, rate = head_terms(sraw_ref, hv_ref)
    logdecay = step * rate
    cum = cumulate(logdecay)
    cum_rows[...] = cum.T
    spread(cum, cum_b)
    bmat = bc_ref[:, :NSTATE]
    cmat = bc_ref[:, NSTATE:]
    s_at, t_at = before(T, T)
    same = wide(segb) == seg_ref[...].astype(F32)
    valid = same & (s_at <= t_at)
    scores[...] = jnp.where(valid, dot_nt(bmat, cmat), 0.0).astype(BF16)
    prev = jnp.where(turn == last_turn, -1.0, prev_ref[7:8])
    last_seg = segb[T - 1 : T]
    last = cum[T - 1 : T]
    expand(step, fan, step_f)
    expand(jnp.exp2(cum) * jnp.where(segb == prev, 1.0, 0.0), fan, from_start)
    expand(jnp.exp2(last - cum) * jnp.where(segb == last_seg, 1.0, 0.0), fan, to_end)
    keep = wide(jnp.where(last_seg == prev, 1.0, 0.0))
    c_t = cmat.astype(F32).T.astype(BF16)
    gst_b = gstate[...].astype(BF16)
    back_scr[...] = dot_nn(bmat, gst_b)
    gscore[...] = jnp.zeros_like(gscore)
    inner_ref[...] = jnp.zeros_like(inner_ref)
    outer_ref[...] = jnp.zeros_like(outer_ref)

    def spread_out(i, p):
        cols = tile_at(i)
        for rows in chunks():
            x1 = (xs_ref[rows, cols].astype(F32) * step_f[rows, cols]).astype(BF16)
            x1_scr[p, rows] = x1
            put_diagonal(diag_x.at[p], rows.start, x1)
            gy = gy_ref[rows, cols]
            put_diagonal(diag_y.at[p], rows.start, gy)
            xw_scr[rows, cols] = (x1.astype(F32) * to_end[rows, cols]).astype(BF16)
            gyw_scr[rows, cols] = (gy.astype(F32) * from_start[rows, cols]).astype(BF16)

    def pair_product(i, p):
        gw_scr[p] = dot_nt(diag_x[p], gy_ref[:, tile_at(i)])

    def decays(i, p):
        for rows in chunks():
            start = 0 if rows.start < LANES else LANES
            total = gscore[rows, start:]
            score = scores[rows, start:]
            for k in range(HPT):
                row = cum_rows[pl.ds(HPT * i + k, 1), :]
                colb = cum_b[HPT * i + k, rows]
                colb = colb if start else wide(colb)
                decay = jnp.exp2(jnp.minimum(row[:, start:] - colb, 0.0))
                wcat[p, rows, k * T + start : (k + 1) * T] = score * decay.astype(BF16)
                total = total + gw_scr[p, k * T + rows.start : k * T + rows.stop, start:] * decay
            gscore[rows, start:] = total

    def grad_product(p):
        gx_scr[p] = dot_nn(wcat[p], diag_y[p])

    def collect(i, p):
        cols = tile_at(i)
        skip = skip_ref[0:1, cols]
        for rows in chunks():
            gx1 = gx_scr[p, rows]
            x1 = x1_scr[p, rows].astype(F32)
            from_state = back_scr[rows, cols] * to_end[rows, cols]
            split_halves(x1 * gx1, high.at[p], low.at[p], rows)
            high_s[p, rows] = (x1 * from_state).astype(BF16)
            gx = (gx1 + from_state) * step_f[rows, cols] + gy_ref[rows, cols].astype(F32) * skip
            gf[rows, cols] = gx * dsilu_ref[rows, cols].astype(F32)
        fade = from_start_last(cum_b, i) * keep
        total = jnp.zeros((8, W), F32)
        for rows in chunks(0, NSTATE):
            gst = gstate[rows, cols] * fade
            gstate[rows, cols] = gst
            total = total + rows8(gst * st_ref[0, rows, cols].astype(F32))
        through[:, cols] = total

    def head_product(i, p):
        pick_i = pick[tile_at(i), :]
        inner_ref[...] += head_sums(high.at[p], low.at[p], pick_i)
        outer_ref[...] += dot_nn(high_s[p], pick_i)

    def two_groups(n, _):
        a, b = 2 * n, 2 * n + 1
        spread_out(a, 0)
        pair_product(a, 0)
        spread_out(b, 1)
        pair_product(b, 1)
        decays(a, 0)
        grad_product(0)
        decays(b, 1)
        grad_product(1)
        collect(a, 0)
        head_product(a, 0)
        collect(b, 1)
        head_product(b, 1)
        if remote:
            for slot, actions in slots.items():

                @pl.when(turn * NT + a == slot - slot % 2)
                def _():
                    for action in actions:
                        action()

        return 0

    lax.fori_loop(0, NT // 2, two_groups, 0)
    gyw = gyw_scr[...]
    gstate[...] += dot_nn(c_t, gyw)
    gsc = jnp.where(valid, gscore[...], 0.0)
    g_b = dot_nn(gsc.astype(BF16), cmat) + dot_nt(xw_scr[...], gst_b)
    g_c = dot_nn(gsc.T.astype(BF16), bmat) + dot_nt(gyw, st_ref[0])
    tail_cols = slice(D_INNER, CONV_CH)
    gf[0:T, tail_cols] = jnp.concatenate([g_b, g_c], axis=1) * dsilu_ref[:, tail_cols].astype(F32)

    inner_sum, outer_sum = inner_ref[...], outer_ref[...]
    after = jnp.where(valid, 1.0, 0.0)
    ahead = jnp.where(same & (s_at > t_at), 1.0, 0.0)
    flow = through[...]
    flow_high = flow.astype(BF16)
    flow_low = (flow - flow_high.astype(F32)).astype(BF16)
    over = jnp.sum(dot_nn(flow_high, pick[...]) + dot_nn(flow_low, pick[...]), axis=0, keepdims=True)
    gl = jnp.dot(after, rsum_ref[...] - inner_sum, precision=HIGHEST, preferred_element_type=F32)
    gl = gl + jnp.dot(ahead, outer_sum, precision=HIGHEST, preferred_element_type=F32) + over
    grad_step = (inner_sum + outer_sum) / jnp.maximum(step, 1e-37) + gl * rate
    lane = lax.broadcasted_iota(jnp.int32, (T, LANES), 1)
    g_sraw = jnp.where(lane < H, grad_step * sigmoid(v), 0.0)
    gc_ref[:, CONV_CH:] = g_sraw.astype(BF16)
    dhv_ref[0:8] += rows8(g_sraw)
    dhv_ref[8:16] += rows8(gl * logdecay)

    def conv_group(j, _):
        cols = tile_at(j)
        taps = [taps_ref[k : k + 1, cols] for k in range(KERNEL)]
        totals = [jnp.zeros((8, W), F32) for _ in range(KERNEL + 1)]
        for rows in chunks():
            here = gf[rows, cols]
            cin = cin_ref[rows, cols].astype(F32)
            totals[KERNEL] = totals[KERNEL] + rows8(here)
            totals[0] = totals[0] + rows8(cin * here)
            total = here * taps[0]
            for k in range(1, KERNEL):
                u = gf[rows.start + k : rows.stop + k, cols] * wide(mask[k - 1, rows])
                total = total + u * taps[k]
                totals[k] = totals[k] + rows8(cin * u)
            gc_ref[rows, cols] = total.astype(BF16)
        for k in range(KERNEL + 1):
            dtaps_ref[8 * k : 8 * k + 8, cols] += totals[k]
        return 0

    lax.fori_loop(0, CT, conv_group, 0)

    if remote:

        @pl.when(turn == last_turn)
        def _():
            for end in ends:
                end()


OUT_CHUNKS, GATE_CHUNKS = 4, 4
OUT_COLS, GATE_COLS = D // OUT_CHUNKS, D_INNER // GATE_CHUNKS
BWD_PACE = (0, 4, 8, 10, 12, 14, 16, 18, 20)
BWD_SLOTS = (0, 1, 3, 4, 6, 7, 9, 11)
TOKEN_PACE = (0, 2, 4, 6, 7, 8, 9, 10, 11)


def gate_out_plan(refs):
    ins, outs, scratch = 14, 3, 28
    head, rest = refs[:ins], refs[ins:]
    (grad_out, grad_gate), rest = rest[:2], rest[2:]
    mid, rest = rest[:outs], rest[outs:]
    (out_total, gate_total), rest = rest[:2], rest[2:]
    tail, rest = rest[:scratch], rest[scratch:]
    out_bufs, gate_bufs, sems = rest[:BUFFERS], rest[BUFFERS : 2 * BUFFERS], rest[2 * BUFFERS :]
    out_starts = [OUT_COLS * n for n in range(OUT_CHUNKS)]
    gate_starts = [GATE_COLS * n for n in range(GATE_CHUNKS)]
    ticks, ends = reduce_plan(
        grad_out, out_starts, OUT_COLS, BWD_SLOTS[0::2], BWD_PACE, out_bufs, out_total, sems, 0, [True] * OUT_CHUNKS
    )
    more, more_ends = reduce_plan(
        grad_gate, gate_starts, GATE_COLS, BWD_SLOTS[1::2], BWD_PACE, gate_bufs, gate_total, sems, OUT_CHUNKS,
        [False] * GATE_CHUNKS,
    )
    return ticks + more, ends + more_ends, (*head, *mid, *tail)


def reduce_sems(count):
    return [
        pltpu.SemaphoreType.DMA((count,)),
        pltpu.SemaphoreType.DMA((count,)),
        pltpu.SemaphoreType.DMA((count, 8)),
        pltpu.SemaphoreType.DMA((count, 8)),
    ]


def bwd_call(xs_bc, sraw, segb, seg, gy, states, rsum, dsilu, cin, hv, skip, taps, grad_out=None, grad_gate=None):
    remote = grad_out is not None
    hbm = pl.BlockSpec(memory_space=pl.ANY)
    length = gy.shape[0]
    blocks = length // T
    tokens = lambda b: (blocks - 1 - b, 0)
    third = lambda b: (blocks - 1 - b, 0, 0)
    fixed = lambda b: (0, 0)
    return pl.pallas_call(
        functools.partial(bwd_kernel, remote),
        grid=(blocks,),
        in_specs=[
            pl.BlockSpec((T, D_INNER), tokens),
            pl.BlockSpec((T, 2 * NSTATE), lambda b: (blocks - 1 - b, D_INNER // (2 * NSTATE))),
            pl.BlockSpec((T, LANES), tokens),
            pl.BlockSpec((T, LANES), tokens),
            pl.BlockSpec((1, T), lambda b: (0, blocks - 1 - b)),
            pl.BlockSpec((8, LANES), lambda b: (jnp.maximum((blocks - 1 - b) * (T // 8) - 1, 0), 0)),
            pl.BlockSpec((T, D_INNER), tokens),
            pl.BlockSpec((1, NSTATE, D_INNER), third),
            pl.BlockSpec((T, LANES), tokens),
            pl.BlockSpec((T, CONV_CH), tokens),
            pl.BlockSpec((T, CONV_CH), tokens),
            whole(hv.shape),
            whole(skip.shape),
            whole(taps.shape),
            *([hbm] * 2 if remote else []),
        ],
        out_specs=[
            pl.BlockSpec((T, CONV_CH + LANES), tokens),
            pl.BlockSpec((8 * (KERNEL + 1), CONV_CH), fixed),
            pl.BlockSpec((16, LANES), fixed),
            *([hbm] * 2 if remote else []),
        ],
        out_shape=[
            jax.ShapeDtypeStruct((length, CONV_CH + LANES), BF16),
            jax.ShapeDtypeStruct((8 * (KERNEL + 1), CONV_CH), F32),
            jax.ShapeDtypeStruct((16, LANES), F32),
            *([jax.ShapeDtypeStruct(g.shape[2:], BF16) for g in (grad_out, grad_gate)] if remote else []),
        ],
        scratch_shapes=[
            pltpu.VMEM((NSTATE, D_INNER), F32),
            pltpu.VMEM((H, T, LANES), F32),
            pltpu.VMEM((2 * LANES, D_INNER), BF16),
            pltpu.VMEM((2, T, HPT * T), BF16),
            pltpu.VMEM((LANES, T), F32),
            pltpu.VMEM((T + 8, CONV_CH), F32),
            pltpu.VMEM((T, T), F32),
            pltpu.VMEM((T, D_INNER), BF16),
            pltpu.VMEM((T, D_INNER), BF16),
            pltpu.VMEM((T, D_INNER), F32),
            pltpu.VMEM((8, D_INNER), F32),
            pltpu.VMEM((2, HPT * T, W), BF16),
            pltpu.VMEM((2, HPT * T, W), BF16),
            pltpu.VMEM((2, HPT * T, T), F32),
            pltpu.VMEM((2, T, W), F32),
            pltpu.VMEM((T, T), BF16),
            pltpu.VMEM((2, T, W), BF16),
            pltpu.VMEM((2, T, W), BF16),
            pltpu.VMEM((2, T, W), BF16),
            pltpu.VMEM((2, T, W), BF16),
            pltpu.VMEM((D_INNER, LANES), BF16),
            pltpu.VMEM((T + 8, LANES), F32),
            pltpu.VMEM((KERNEL - 1, T, LANES), F32),
            pltpu.VMEM((T, LANES), F32),
            pltpu.VMEM((T, LANES), F32),
            pltpu.VMEM((T, D_INNER), F32),
            pltpu.VMEM((T, D_INNER), F32),
            pltpu.VMEM((T, D_INNER), F32),
            *(
                reduce_buffers(grad_out.shape[2], OUT_COLS, OUT_CHUNKS)
                + reduce_buffers(grad_gate.shape[2], GATE_COLS, GATE_CHUNKS)
                + reduce_sems(OUT_CHUNKS + GATE_CHUNKS)
                if remote
                else []
            ),
        ],
        compiler_params=pltpu.CompilerParams(
            vmem_limit_bytes=VMEM_LIMIT, **(dict(collective_id=1, has_side_effects=True) if remote else {})
        ),
        cost_estimate=pl.CostEstimate(flops=2 * length * D * D_INNER * 4, bytes_accessed=30 << 20, transcendentals=0),
    )(xs_bc, xs_bc, sraw, segb, seg, segb, gy, states, rsum, dsilu, cin, hv, skip, taps, *((grad_out, grad_gate) if remote else ()))


CONV_COLS = 2 * W
CONV_CHUNKS = (CONV_CH + LANES) // CONV_COLS
CONV_DONE = CONV_CHUNKS * CONV_COLS
CONV_LEFT = CONV_CH + LANES - CONV_DONE


def token_kernel(remote, *refs):
    (gg_ref, gc_ref, wg_hbm, wc_hbm, tok_ref, cot_ref, vec_ref, taps_sum, vec_sum), refs = refs[:9], refs[9:]
    if remote:
        grad_conv, refs = refs[0], refs[1:]
        (tg_ref, small_total, conv_total), refs = refs[:3], refs[3:]
    else:
        (tg_ref, small_total), refs = refs[:2], refs[2:]
    (wg, wc, grad, dpre, small, load_sems), refs = refs[:6], refs[6:]
    turn = pl.program_id(0)
    last_turn = pl.num_programs(0) - 1
    loads = [
        pltpu.make_async_copy(wg_hbm, wg, load_sems.at[0]),
        pltpu.make_async_copy(wc_hbm, wc, load_sems.at[1]),
    ]
    pieces = D // CONV_COLS
    slots = {}
    if remote:
        conv_bufs, step_bufs, refs = refs[:BUFFERS], refs[BUFFERS : 2 * BUFFERS], refs[2 * BUFFERS :]
        small_bufs, refs = refs[:9], refs[9:]
        sems, small_sems = refs[:4], refs[4:]
        starts = [CONV_COLS * n for n in range(CONV_CHUNKS)]
        ticks, ends = reduce_plan(
            grad_conv, starts, CONV_COLS, range(CONV_CHUNKS), TOKEN_PACE, conv_bufs, conv_total, sems, 0,
            [n % 2 == 0 for n in range(CONV_CHUNKS)],
        )
        more, more_ends = reduce_plan(
            grad_conv, [CONV_DONE], CONV_LEFT, [CONV_CHUNKS], TOKEN_PACE, step_bufs, conv_total, sems, CONV_CHUNKS,
            [True],
        )
        done = 4 * pieces
        last, last_ends = small_plan(small, small_bufs, small_total, small_sems, done, 1)
        slots = by_slot(ticks + more + last)
        ends = ends + more_ends + last_ends

    @pl.when(turn == 0)
    def _():
        for load in loads:
            load.start()
        dpre[...] = jnp.zeros_like(dpre)
        if remote:
            greet(range(5))
            for action in slots.pop(0):
                action()
        for load in loads:
            load.wait()

    def piece(q, _):
        rows = tile_at(q, CONV_COLS)
        grad[:, rows] = dot_nt(gg_ref[...], wg[rows, :]) + dot_nt(gc_ref[...], wc[rows, :])
        for slot, actions in slots.items():
            if slot < 4 * pieces:

                @pl.when(turn * pieces + q == slot)
                def _():
                    for action in actions:
                        action()

        return 0

    lax.fori_loop(0, pieces, piece, 0)
    gain = vec_ref[0:1, :D]
    total = jnp.zeros((8, D), F32)
    step = 16
    for r in range(0, T, step):
        rows = slice(r, r + step)
        tok = tok_ref[rows].astype(F32)
        rho = lax.rsqrt(jnp.sum(tok * tok, axis=1, keepdims=True) * (1.0 / D) + EPSILON)
        unit = tok * rho
        g = grad[rows]
        total = total + rows8(g * unit)
        e = g * gain
        mean = jnp.sum(e * unit, axis=1, keepdims=True) * (1.0 / D)
        tg_ref[rows] = cot_ref[rows].astype(F32) + rho * (e - unit * mean)
    dpre[...] += total

    @pl.when(turn == last_turn)
    def _():
        vec_sum_all = vec_sum[0:1, :]
        pre = jnp.sum(dpre[...], axis=0, keepdims=True)
        vec_all = jnp.concatenate([pre, vec_sum_all[:, D:]], axis=1)
        parts = small.shape[0] * small.shape[1] if remote else small.shape[0]
        n, m = CONV_CH // parts, VEC // parts
        small[...] = jnp.zeros_like(small)
        for p in range(parts):
            at = (p // 2, p % 2) if remote else (p,)
            small[(*at, slice(0, KERNEL), slice(0, n))] = taps_sum[0:KERNEL, n * p : n * (p + 1)]
            small[(*at, slice(8, 9), slice(0, m))] = vec_all[:, m * p : m * (p + 1)]
        if remote:
            for slot in sorted(slots):
                if slot >= 4 * pieces:
                    for action in slots[slot]:
                        action()
            for end in ends:
                end()
        else:
            small_total[...] = small[...]


def token_call(gg, gc, wg, wc, tok, cot, vec, taps_sum, vec_sum, parts, grad_conv=None):
    remote = grad_conv is not None
    length = tok.shape[0]
    tokens = lambda b: (b, 0)
    hbm = pl.BlockSpec(memory_space=pl.ANY)
    small = (2, 2, 16, SMALL_COLS) if remote else (parts, 16, SMALL_COLS)
    small_out = small[2:] if remote else small
    zeros = (0,) * len(small_out)
    return pl.pallas_call(
        functools.partial(token_kernel, remote),
        grid=(length // T,),
        in_specs=[
            pl.BlockSpec((T, D_INNER), tokens),
            pl.BlockSpec((T, CONV_CH + LANES), tokens),
            hbm,
            hbm,
            pl.BlockSpec((T, D), tokens),
            pl.BlockSpec((T, D), tokens),
            whole(vec.shape),
            whole(taps_sum.shape),
            whole(vec_sum.shape),
            *([hbm] if remote else []),
        ],
        out_specs=[
            pl.BlockSpec((T, D), tokens),
            pl.BlockSpec(small_out, lambda b: zeros),
            *([hbm] if remote else []),
        ],
        out_shape=[
            jax.ShapeDtypeStruct((length, D), F32),
            jax.ShapeDtypeStruct(small_out, F32),
            *([jax.ShapeDtypeStruct(grad_conv.shape[2:], BF16)] if remote else []),
        ],
        scratch_shapes=[
            pltpu.VMEM(wg.shape, BF16),
            pltpu.VMEM(wc.shape, BF16),
            pltpu.VMEM((T, D), F32),
            pltpu.VMEM((8, D), F32),
            pltpu.VMEM(small, F32),
            pltpu.SemaphoreType.DMA((2,)),
            *(
                reduce_buffers(grad_conv.shape[2], CONV_COLS, CONV_CHUNKS)
                + reduce_buffers(grad_conv.shape[2], CONV_LEFT, 1)
                + small_buffers(16, SMALL_COLS)
                + reduce_sems(CONV_CHUNKS + 1)
                + [pltpu.SemaphoreType.DMA((5,)), pltpu.SemaphoreType.DMA((5,))]
                if remote
                else []
            ),
        ],
        compiler_params=pltpu.CompilerParams(
            vmem_limit_bytes=VMEM_LIMIT, **(dict(collective_id=2, has_side_effects=True) if remote else {})
        ),
        cost_estimate=pl.CostEstimate(flops=2 * length * D * 4480, bytes_accessed=22 << 20, transcendentals=0),
    )(gg, gc, wg, wc, tok, cot, vec, taps_sum, vec_sum, *((grad_conv,) if remote else ()))


def adam_step(master, first, second, grad, rate):
    first_new = BETA_FIRST * first + (1.0 - BETA_FIRST) * grad
    second_new = BETA_SECOND * second + (1.0 - BETA_SECOND) * grad * grad
    first_fix = 1.0 - BETA_FIRST**STEP
    second_fix = 1.0 - BETA_SECOND**STEP
    master_new = master - rate * (
        first_new / first_fix / (jnp.sqrt(second_new / second_fix) + ADAM_EPSILON) + WEIGHT_DECAY * master
    )
    return (master_new, first_new, second_new)


def adam_rows(rate, grad, refs, rows):
    ins, outs = refs
    for ref, value in zip(outs, adam_step(*(r[rows] for r in ins), grad, rate)):
        ref[rows] = value


def adam_turned_kernel(rate, tiles, first_ref, second_ref, *refs):
    j = pl.program_id(0)
    for which, grad_ref in enumerate((first_ref, second_ref)):

        @pl.when((j >= tiles) == bool(which))
        def _():
            for r in range(0, 2 * W, LANES):
                rows = slice(r, r + LANES)
                adam_rows(rate, grad_ref[:, rows].astype(F32).T, (refs[:3], refs[3:]), rows)


def adam_kernel(rate, grad_ref, *refs):
    for r in range(0, refs[0].shape[0], 32):
        rows = slice(r, r + 32)
        adam_rows(rate, grad_ref[rows].astype(F32), (refs[:3], refs[3:]), rows)


def adam_call(grads, master, first, second, rate):
    rows, cols = master.shape
    if len(grads) == 2:
        tile = 2 * W
        tiles = grads[0].shape[1] // tile
        kernel = functools.partial(adam_turned_kernel, rate, tiles)
        grad_specs = [
            pl.BlockSpec((cols, tile), lambda j: (0, jnp.minimum(j, tiles - 1))),
            pl.BlockSpec((cols, tile), lambda j: (0, jnp.maximum(j - tiles, 0))),
        ]
    else:
        tile = rows // 4
        kernel = functools.partial(adam_kernel, rate)
        grad_specs = [pl.BlockSpec((tile, cols), lambda j: (j, 0))]
    down = pl.BlockSpec((tile, cols), lambda j: (j, 0))
    return pl.pallas_call(
        kernel,
        grid=(-(-rows // tile),),
        in_specs=[*grad_specs, down, down, down],
        out_specs=[down] * 3,
        out_shape=[jax.ShapeDtypeStruct((rows, cols), F32)] * 3,
        compiler_params=pltpu.CompilerParams(vmem_limit_bytes=VMEM_LIMIT),
        cost_estimate=pl.CostEstimate(flops=0, bytes_accessed=26 * rows * cols, transcendentals=0),
    )(*grads, master, first, second)


def owners(grad, parts, remote):
    return grad.reshape(*((2, 2) if remote else (parts,)), -1, grad.shape[1])


def row_pass(projected, tok, cot, seg, wg, wc, wo, parts, remote):
    act, dsilu, cin, y, states, sraw, nrm, segb, taps, vec, hv, skip = projected
    block_out, mixed, gy, gg, rsum, dgain, dskip = fwd_call(act, y, nrm, tok, cot, wg, wo, vec, skip)
    grad_out = owners(dot_tn(mixed, cot).astype(BF16), parts, remote)
    grad_gate = owners(dot_tn(nrm, gg).astype(BF16), parts, remote)
    gc, dtaps, dhv, *totals = bwd_call(
        act, sraw, segb, seg, gy, states, rsum, dsilu, cin, hv, skip, taps, *((grad_out, grad_gate) if remote else ())
    )
    grad_conv = owners(dot_tn(nrm, gc).astype(BF16), parts, remote)
    dtaps = dtaps.reshape(KERNEL + 1, 8, CONV_CH).sum(1)
    dhv = dhv.reshape(2, 8, LANES).sum(1)
    vec_sum = jnp.concatenate(
        [
            jnp.zeros((D,), F32),
            dgain.sum(0),
            dtaps[KERNEL],
            dhv[0, :H],
            dhv[1, :H],
            dskip.sum(0).reshape(H, P_SIZE).sum(1),
            jnp.zeros((VEC_PAD - VEC,), F32),
        ]
    )[None]
    token_grad, small, *conv_total = token_call(
        gg, gc, wg, wc, tok, cot, vec, dtaps, vec_sum, parts, *((grad_conv,) if remote else ())
    )
    if remote:
        out_total, gate_total = totals
        return block_out, token_grad, gate_total, conv_total[0], out_total, small
    return block_out, token_grad, grad_gate, grad_conv, grad_out, small


def local(
    tokens, cotangent, segment_ids, in_weight, out_weight, filter_weight, vectors,
    in_first, out_first, filter_first, vector_first, in_second, out_second, filter_second, vector_second,
):
    remote = lax.axis_size("grp") == 4 and lax.axis_size("dp") == 8
    parts = D // in_weight.shape[0]
    vec_size = vectors.size
    in_turned = in_weight.T
    small = jnp.pad(filter_weight, ((0, 12), (0, SMALL_COLS - filter_weight.shape[1])))
    small = small.at[8, :vec_size].set(vectors)
    tok, cot = tokens[0], cotangent[0]
    if remote:
        *projected, wg, wc, wo = project_call(tok, segment_ids, in_turned, out_weight, small)
    else:
        in_full = lax.all_gather(in_weight.astype(BF16), "grp", axis=0, tiled=True)
        wo = lax.all_gather(out_weight.astype(BF16), "grp", axis=0, tiled=True)
        slots = lax.all_gather(small, "grp")
        wg = in_full[:, :D_INNER]
        wc = jnp.pad(in_full[:, D_INNER:], ((0, 0), (0, LANES - H)))
        projected = plain_project_call(tok, segment_ids, wc, slots)
    block_out, token_grad, *grads = row_pass(projected, tok, cot, segment_ids, wg, wc, wo, parts, remote)
    if not remote:
        grads = [lax.psum(lax.psum_scatter(g, "grp", scatter_dimension=0, tiled=False), "dp") for g in grads]
    gate_total, conv_total, out_total, small_total = grads
    in_new = [a.T for a in adam_call((gate_total, conv_total), in_turned, in_first.T, in_second.T, 0.03)]
    out_new = adam_call((out_total,), out_weight, out_first, out_second, 0.02)
    filter_new = adam_step(
        filter_weight, filter_first, filter_second, small_total[:KERNEL, : filter_weight.shape[1]], 0.3
    )
    vector_new = adam_step(vectors, vector_first, vector_second, small_total[8, :vec_size], 0.3)
    results = (in_new, out_new, filter_new, vector_new)
    return (block_out[None], token_grad[None], *(r[n] for n in range(3) for r in results))


def solution(mesh):
    rows = P(("grp", "dp"), None, None)
    shards = (P("grp", None), P("grp", None), P(None, "grp"), P("grp"))
    in_specs = (rows, rows, P(("grp", "dp"), None)) + shards * 3
    out_specs = (rows, rows) + shards * 3
    return jax.shard_map(local, mesh=mesh, in_specs=in_specs, out_specs=out_specs, check_vma=False)
```

```python
import functools
import itertools
import math

import jax
import jax.numpy as jnp
from jax import lax
from jax.experimental import pallas as pl
from jax.experimental.pallas import tpu as pltpu
from jax.sharding import PartitionSpec as P

D = 1024
H = 32
P_SIZE = 64
NSTATE = 128
KERNEL = 4
STEP = 7
D_INNER = 2048
CONV_CH = 2304
XBC = D_INNER + CONV_CH
LANES = 128
T = 256
W = 256
HPT = W // P_SIZE
NT = D_INNER // W
CT = CONV_CH // W
SMALL_COLS = 1408
CHUNK = 32
HEADS_AT = D + D_INNER + CONV_CH
VEC = HEADS_AT + 3 * H
VEC_PAD = 5504
STEP_AT = D_INNER + CONV_CH
ALL = STEP_AT + LANES
LOG2E = math.log2(math.e)

EPSILON = 1e-05
ADAM_EPSILON = 1e-08
BETA_FIRST = 0.5
BETA_SECOND = 0.5
WEIGHT_DECAY = 0.1

F32 = jnp.float32
BF16 = jnp.bfloat16
HIGHEST = lax.Precision.HIGHEST
VMEM_LIMIT = 58 * 1024 * 1024


def dot_nn(a, b):
    return lax.dot_general(a, b, (((1,), (0,)), ((), ())), preferred_element_type=F32)


def dot_nt(a, b):
    return lax.dot_general(a, b, (((1,), (1,)), ((), ())), preferred_element_type=F32)


def dot_tn(a, b):
    return lax.dot_general(a, b, (((0,), (0,)), ((), ())), preferred_element_type=F32)


def sigmoid(v):
    return 0.5 * jnp.tanh(0.5 * v) + 0.5


def rows8(v):
    return jnp.sum(v.reshape(v.shape[0] // 8, 8, v.shape[1]), axis=0)


def tile_of(i):
    return slice(i * W, (i + 1) * W)


def tile_at(i, width=W):
    return pl.ds(pl.multiple_of(i * width, width), width)


def whole(shape):
    zeros = (0,) * len(shape)
    return pl.BlockSpec(shape, lambda *_: zeros, pipeline_mode=pl.Buffered(1))


MESH = pl.DeviceIdType.MESH
HOPS = (("dp", 1), ("grp", 1), ("grp", 2), ("dp", 2), ("dp", 4))
CORE, ALONG_X, ALONG_Y, Z_NEAR, Z_FAR = range(5)


def bit(hop):
    name, size = HOPS[hop]
    return lax.rem(lax.div(lax.axis_index(name), size), 2)


def across(hop):
    name, size = HOPS[hop]
    return {name: lax.axis_index(name) + size * (1 - 2 * bit(hop))}


def greet(hops):
    barrier = pltpu.get_barrier_semaphore()
    for hop in hops:
        pl.semaphore_signal(barrier, inc=1, device_id=across(hop), device_id_type=MESH)
    pl.semaphore_wait(barrier, len(hops))


class Transfer:
    def __init__(self, hop, src, dst, send, recv, ways):
        rows = src.shape[-2]
        lead = (slice(None),) * (len(src.shape) - 2)
        parts = [(*lead, pl.ds(i * rows // ways, rows // ways)) for i in range(ways)]

        def copy(a, b):
            return pltpu.make_async_remote_copy(
                src_ref=a, dst_ref=b, send_sem=send, recv_sem=recv, device_id=across(hop), device_id_type=MESH
            )

        self.parts = [copy(src.at[at], dst.at[at]) for at in parts] if ways > 1 else [copy(src, dst)]
        self.whole = copy(src, dst)

    def start(self):
        for part in self.parts:
            part.start()

    def wait_recv(self):
        self.whole.wait_recv()

    def wait_send(self):
        self.whole.wait_send()


def rows_at(start, size):
    return pl.ds(pl.multiple_of(start, size), size)


def add_rows(out, a, b):
    *lead, rows, cols = out.shape
    size = min(rows, max(16, 8192 // cols))
    for at in itertools.product(*(range(n) for n in lead)):
        for r in range(0, rows, size):
            here = (*at, slice(r, r + size))
            out[here] = a[here] + b[here]


def reduce_chunk(src, cols, first_x, bufs, total, sends, recvs, index, local_sem):
    own, r1, r2, r3, r4, r0 = bufs
    rows = src.shape[2]
    half, quarter, eighth = rows // 2, rows // 4, rows // 8
    c, x, y, z1, z2 = (bit(hop) for hop in range(5))
    first, second = (ALONG_X, ALONG_Y) if first_x else (ALONG_Y, ALONG_X)
    base = c * half
    base1 = base + z1 * quarter
    base2 = base1 + z2 * eighth

    def copy(n, hop, a, b, ways=1):
        return Transfer(hop, a, b, sends.at[index, n], recvs.at[index, n], ways)

    def pair(u):
        return own.at[:, u] if first_x else own.at[u]

    kept = bit(first)
    load = pltpu.make_async_copy(src.at[:, :, rows_at(base, half), cols], own, local_sem)
    here = [total.at[rows_at(base2, eighth)], total.at[rows_at(base1, quarter)], total.at[rows_at(base, half)]]
    copies = [
        copy(0, CORE, src.at[:, :, rows_at((1 - c) * half, half), cols], r0),
        copy(1, first, pair(1 - kept), r1),
        copy(2, second, r1.at[1 - bit(second)], r2),
        copy(3, Z_NEAR, r2.at[rows_at((1 - z1) * quarter, quarter)], r3),
        copy(4, Z_FAR, r3.at[rows_at((1 - z2) * eighth, eighth)], r4),
        copy(5, Z_FAR, here[0], here[0]),
        copy(6, Z_NEAR, here[1], here[1]),
        copy(7, CORE, here[2], here[2]),
    ]

    def begin():
        load.start()
        copies[0].start()

    def after_core():
        load.wait()
        copies[0].wait_recv()
        add_rows(own, own, r0)
        copies[1].start()

    def after_first():
        copies[1].wait_recv()
        add_rows(r1, r1, pair(kept))
        copies[2].start()

    def after_second():
        copies[2].wait_recv()
        add_rows(r2, r2, r1.at[bit(second)])
        copies[3].start()

    def after_near():
        copies[3].wait_recv()
        add_rows(r3, r3, r2.at[rows_at(z1 * quarter, quarter)])
        copies[4].start()

    def after_far():
        copies[4].wait_recv()
        add_rows(here[0], r4, r3.at[rows_at(z2 * eighth, eighth)])
        copies[5].start()

    def gather_far():
        copies[5].wait_recv()
        copies[6].start()

    def gather_near():
        copies[6].wait_recv()
        copies[7].start()

    def arrive():
        copies[7].wait_recv()

    def finish():
        for one in copies:
            one.wait_send()

    return (begin, after_core, after_first, after_second, after_near, after_far, gather_far, gather_near, arrive), finish


def reduce_buffers(rows, cols, count, dtype=BF16):
    half = rows // 2
    shapes = [
        (2, 2, half, cols), (2, 2, half, cols), (2, half, cols), (half, cols), (half // 2, cols), (half // 4, cols), (rows, cols),
    ]
    return [pltpu.VMEM((count, *shape), dtype) for shape in shapes]


BUFFERS = 7
STAGES = 9


def reduce_plan(src, starts, size, slots, pace, bufs, result, sems, base, x_first):
    local_sems, out_sems, sends, recvs = sems
    ticks, ends = [], []
    for n, (start, slot) in enumerate(zip(starts, slots)):
        index = base + n
        own, r0, r1, r2, r3, r4, total = (ref.at[n] for ref in bufs)
        cols = pl.ds(start, size)
        stages, finish = reduce_chunk(
            src, cols, x_first[n], (own, r1, r2, r3, r4, r0), total, sends, recvs, index, local_sems.at[index]
        )
        write = pltpu.make_async_copy(total, result.at[:, cols], out_sems.at[index])
        for later, stage in zip(pace, stages):
            ticks.append((slot + later, stage))
        ticks.append((slot + pace[-1], write.start))
        ends += [finish, write.wait]
    return ticks, ends


def small_plan(src, bufs, total, sems, slot, spacing):
    sends, recvs = sems
    r0, a1, r1, a2, r2, a3, r3, a4, r4 = bufs
    x, y = bit(ALONG_X), bit(ALONG_Y)

    def copy(n, hop, a, b):
        return pltpu.make_async_remote_copy(
            src_ref=a, dst_ref=b, send_sem=sends.at[n], recv_sem=recvs.at[n], device_id=across(hop), device_id_type=MESH
        )

    copies = [
        copy(0, CORE, src, r0),
        copy(1, ALONG_X, a1.at[:, 1 - x], r1),
        copy(2, ALONG_Y, a2.at[1 - y], r2),
        copy(3, Z_NEAR, a3, r3),
        copy(4, Z_FAR, a4, r4),
    ]

    def after(n, out, one, other):
        def stage():
            copies[n].wait_recv()
            out[...] = one[...] + other[...]
            if n < 4:
                copies[n + 1].start()

        return stage

    stages = [
        copies[0].start,
        after(0, a1, src, r0),
        after(1, a2, a1.at[:, x], r1),
        after(2, a3, a2.at[y], r2),
        after(3, a4, a3, r3),
        after(4, total, a4, r4),
    ]
    return [(slot + k * spacing, stage) for k, stage in enumerate(stages)], [one.wait_send for one in copies]


def small_buffers(rows, cols):
    shapes = [(2, 2, rows, cols), (2, 2, rows, cols), (2, rows, cols), (2, rows, cols)] + [(rows, cols)] * 5
    return [pltpu.VMEM(shape, F32) for shape in shapes]


def by_slot(ticks):
    slots = {}
    for slot, action in ticks:
        slots.setdefault(slot, []).append(action)
    return slots


def head_terms(sraw_ref, hv_ref):
    v = sraw_ref[...] + hv_ref[0:1, :]
    step = jnp.maximum(v, 0.0) + jnp.log1p(jnp.exp(-jnp.abs(v)))
    rate = -jnp.exp(hv_ref[1:2, :])
    return v, step, rate


def before(rows, cols):
    return lax.broadcasted_iota(jnp.int32, (rows, cols), 0), lax.broadcasted_iota(jnp.int32, (rows, cols), 1)


def cumulate(logdecay):
    t, s = before(T, T)
    lower = jnp.where(s <= t, 1.0, 0.0)
    return jnp.dot(lower, logdecay * LOG2E, precision=HIGHEST, preferred_element_type=F32)


def spread(cum, cum_b):
    for h in range(H):
        cum_b[h] = jnp.broadcast_to(cum[:, h : h + 1], (T, LANES))


def expand(values, fan, out):
    high = values.astype(BF16)
    low = (values - high.astype(F32)).astype(BF16)
    both = jnp.concatenate([high, low], axis=1)
    for c in range(0, D_INNER, 2 * W):
        out[:, c : c + 2 * W] = dot_nn(both, fan[:, c : c + 2 * W])


def set_fan(fan):
    for c in range(0, D_INNER, W):
        row, lane = before(2 * LANES, W)
        fan[:, c : c + W] = jnp.where(lax.shift_right_logical(lane + c, 6) == (row & (LANES - 1)), 1.0, 0.0).astype(BF16)


def put_diagonal(diag, r, tile):
    lane = lax.broadcasted_iota(jnp.int32, (tile.shape[0], LANES), 1)
    first = jnp.where(lane < P_SIZE, 1.0, 0.0).astype(BF16)
    second = jnp.where(lane < P_SIZE, 0.0, 1.0).astype(BF16)
    for k in range(HPT):
        at = LANES * (k // 2)
        part = tile[:, at : at + LANES]
        diag[k * T + r : k * T + r + tile.shape[0], at : at + LANES] = part * (first if k % 2 == 0 else second)


def from_start_last(cum_b, i):
    lane = lax.broadcasted_iota(jnp.int32, (1, LANES), 1)
    last = slice(T - 1, T)
    halves = [jnp.where(lane < P_SIZE, cum_b[HPT * i + 2 * k, last], cum_b[HPT * i + 2 * k + 1, last]) for k in range(2)]
    return jnp.exp2(jnp.concatenate(halves, axis=1))


def wide(m):
    return jnp.concatenate([m, m], axis=1)


def split_halves(values, high_ref, low_ref, rows):
    high = values.astype(BF16)
    high_ref[rows] = high
    low_ref[rows] = (values - high.astype(F32)).astype(BF16)


def head_sums(high_ref, low_ref, pick):
    return dot_nn(high_ref[...], pick) + dot_nn(low_ref[...], pick)


def set_pick(pick):
    for r in range(0, D_INNER, T):
        row, lane = before(T, LANES)
        pick[r : r + T] = jnp.where(lax.shift_right_logical(row + r, 6) == lane, 1.0, 0.0).astype(BF16)


def chunks(start=0, stop=T):
    return [slice(r, r + CHUNK) for r in range(start, stop, CHUNK)]


def scan_forward(block, act, sraw_ref, segb_ref, seg_ref, hv_ref, skip_ref, y_ref, st_ref, scratch):
    (
        state, cum_b, fan, wcat, cum_rows, xw_scr, carr_scr, diag, scores, prev_seg, step_f, from_start, to_end,
    ) = scratch
    tokens = rows_at(block * T, T)

    @pl.when(block == 0)
    def _():
        state[...] = jnp.zeros_like(state)
        wcat[...] = jnp.zeros_like(wcat)
        diag[...] = jnp.zeros_like(diag)
        prev_seg[...] = jnp.full(prev_seg.shape, -1.0, F32)
        set_fan(fan)

    _, step, rate = head_terms(sraw_ref.at[tokens], hv_ref)
    cum = cumulate(step * rate)
    cum_rows[...] = cum.T
    spread(cum, cum_b)
    bmat = act[tokens, D_INNER : D_INNER + NSTATE]
    cmat = act[tokens, D_INNER + NSTATE : CONV_CH]
    segb = segb_ref[tokens]
    t_at, s_at = before(T, T)
    valid = (wide(segb) == seg_ref[0:1, tokens].astype(F32)) & (s_at <= t_at)
    scores[...] = jnp.where(valid, dot_nt(cmat, bmat), 0.0).astype(BF16)
    prev = prev_seg[0:1]
    last_seg = segb[T - 1 : T]
    last = cum[T - 1 : T]
    expand(step, fan, step_f)
    expand(jnp.exp2(cum) * jnp.where(segb == prev, 1.0, 0.0), fan, from_start)
    expand(jnp.exp2(last - cum) * jnp.where(segb == last_seg, 1.0, 0.0), fan, to_end)
    keep = wide(jnp.where(last_seg == prev, 1.0, 0.0))
    prev_seg[0:1] = last_seg
    b_t = bmat.astype(F32).T.astype(BF16)
    st_ref[0] = state[...].astype(BF16)
    carr_scr[...] = dot_nn(cmat, st_ref[0])

    def here(rows):
        return pl.ds(pl.multiple_of(block * T + rows.start, CHUNK), CHUNK)

    def prepare(i, p):
        cols = tile_of(i)
        for rows in chunks():
            x1 = (act[here(rows), cols].astype(F32) * step_f[rows, cols]).astype(BF16)
            put_diagonal(diag.at[p], rows.start, x1)
            xw_scr[rows, cols] = (x1.astype(F32) * to_end[rows, cols]).astype(BF16)
        for k in range(HPT):
            row = cum_rows[HPT * i + k : HPT * i + k + 1, :]
            for rows in chunks():
                n = LANES if rows.start < LANES else T
                colb = cum_b[HPT * i + k, rows]
                colb = colb if n == LANES else wide(colb)
                decay = jnp.exp2(jnp.minimum(colb - row[:, :n], 0.0)).astype(BF16)
                wcat[p, rows, k * T : k * T + n] = scores[rows, :n] * decay

    prepare(0, 0)
    for i in range(NT):
        cols = tile_of(i)
        y_ref[:, cols] = dot_nn(wcat[i % 2], diag[i % 2])
        if i + 1 < NT:
            prepare(i + 1, (i + 1) % 2)
        skip = skip_ref[0:1, cols]
        for rows in chunks():
            y = y_ref[rows, cols] + carr_scr[rows, cols] * from_start[rows, cols]
            y_ref[rows, cols] = y + act[here(rows), cols].astype(F32) * skip
        fade = from_start_last(cum_b, i) * keep
        for rows in chunks(0, NSTATE):
            state[rows, cols] = state[rows, cols] * fade
    state[...] += dot_nn(b_t, xw_scr[...])


def scan_scratch():
    return [
        pltpu.VMEM((NSTATE, D_INNER), F32),
        pltpu.VMEM((H, T, LANES), F32),
        pltpu.VMEM((2 * LANES, D_INNER), BF16),
        pltpu.VMEM((2, T, HPT * T), BF16),
        pltpu.VMEM((LANES, T), F32),
        pltpu.VMEM((T, D_INNER), BF16),
        pltpu.VMEM((T, D_INNER), F32),
        pltpu.VMEM((2, HPT * T, W), BF16),
        pltpu.VMEM((T, T), BF16),
        pltpu.VMEM((8, LANES), F32),
        pltpu.VMEM((T, D_INNER), F32),
        pltpu.VMEM((T, D_INNER), F32),
        pltpu.VMEM((T, D_INNER), F32),
    ]


def norm_rows(tok_ref, gain, nrm_ref):
    def body(i, _):
        rows = pl.ds(pl.multiple_of(i * CHUNK, CHUNK), CHUNK)
        tok = tok_ref[rows].astype(F32)
        rho = lax.rsqrt(jnp.sum(tok * tok, axis=1, keepdims=True) * (1.0 / D) + EPSILON)
        nrm_ref[rows] = (tok * rho * gain).astype(BF16)
        return 0

    lax.fori_loop(0, tok_ref.shape[0] // CHUNK, body, 0)


def segment_masks(seg_ref, segb_ref, pad, mask):
    length = segb_ref.shape[0]
    column = jnp.broadcast_to(seg_ref[...].astype(F32), (8, length)).T
    pad[0:8] = jnp.full((8, LANES), -1.0, F32)
    for r in range(0, length, T):
        rows = jnp.broadcast_to(column[r : r + T, 0:1], (T, LANES))
        segb_ref[r : r + T] = rows
        pad[8 + r : 8 + r + T] = rows
    for k in range(1, KERNEL):
        for r in range(0, length, T):
            mask[k - 1, r : r + T] = jnp.where(pad[8 + r - k : 8 + r - k + T] == segb_ref[r : r + T], 1.0, 0.0)


def unpack_small(slots, taps_ref, vec_ref, hv_ref, skip_ref):
    parts = slots.shape[0]
    taps_ref[...] = jnp.zeros_like(taps_ref)
    vec_ref[...] = jnp.zeros_like(vec_ref)
    hv_ref[...] = jnp.zeros_like(hv_ref)
    skip_ref[...] = jnp.zeros_like(skip_ref)
    n, m = CONV_CH // parts, VEC // parts
    for p in range(parts):
        taps_ref[0:KERNEL, n * p : n * (p + 1)] = slots[p, 0:KERNEL, 0:n].astype(BF16).astype(F32)
        vec_ref[0:1, m * p : m * (p + 1)] = slots[p, 8:9, 0:m].astype(BF16).astype(F32)
    for k in range(2):
        hv_ref[k : k + 1, 0:H] = vec_ref[0:1, HEADS_AT + k * H : HEADS_AT + (k + 1) * H]
    for h in range(H):
        at = HEADS_AT + 2 * H + h
        skip_ref[0:1, P_SIZE * h : P_SIZE * (h + 1)] = jnp.broadcast_to(vec_ref[0:1, at : at + 1], (1, P_SIZE))


def conv_tile(j, nrm_ref, w, taps_ref, vec_ref, mask, act_ref, dsilu_ref, cin_ref, pad):
    length = nrm_ref.shape[0]
    pad[0:8] = jnp.zeros((8, W), F32)
    cols = tile_at(j)
    taps = [taps_ref[k : k + 1, cols] for k in range(KERNEL)]
    bias = vec_ref[0:1, pl.ds(pl.multiple_of(D + D_INNER + j * W, W), W)]
    def product(top):
        pad[8 + top : 8 + top + T] = dot_nn(nrm_ref[top : top + T], w[:, cols])

    product(0)
    for top in range(0, length, T):
        if top + T < length:
            product(top + T)
        for r in range(top, top + T, CHUNK):
            here = pad[8 + r : 8 + r + CHUNK]
            cin_ref[r : r + CHUNK] = here.astype(BF16)
            total = bias + here * taps[0]
            for k in range(1, KERNEL):
                m = wide(mask[k - 1, r : r + CHUNK])
                total = total + pad[8 + r - k : 8 + r - k + CHUNK] * m * taps[k]
            sig = sigmoid(total)
            act = total * sig
            act_ref[r : r + CHUNK] = act.astype(BF16)
            dsilu_ref[r : r + CHUNK] = (sig + act * (1.0 - sig)).astype(BF16)


def weight_piece(src, src_cols, put, hop_sems, index, rows):
    sends, recvs = hop_sems
    half, quarter = rows // 2, rows // 4
    me = lax.axis_index("grp")
    x, y = bit(ALONG_X), bit(ALONG_Y)
    slot_x, slot_y, slot_d = 2 * y + 1 - x, 2 * (1 - y) + x, 2 * (1 - y) + 1 - x
    top = bit(CORE) * half

    def copy(n, a, b, hop):
        return Transfer(hop, a, b, sends.at[index, n], recvs.at[index, n], 2)

    def onward(n, slot, start, size, hop):
        return copy(n, put(slot * rows + start, size), put(slot * rows + start, size), hop)

    mine = src.at[rows_at(top, half), src_cols]
    copies = [
        copy(0, mine, put(me * rows + top, half), ALONG_X),
        copy(1, mine, put(me * rows + top, half), ALONG_Y),
        onward(2, slot_x, top, quarter, ALONG_Y),
        onward(3, slot_y, top + quarter, quarter, ALONG_X),
        onward(4, slot_x, top, half, CORE),
        onward(5, slot_y, top, half, CORE),
        onward(6, slot_d, top, quarter, CORE),
        onward(7, slot_d, top + quarter, quarter, CORE),
    ]

    def own():
        copies[0].start()
        copies[1].start()

    def pass_on():
        copies[0].wait_recv()
        copies[2].start()
        copies[1].wait_recv()
        copies[3].start()
        copies[4].start()
        copies[5].start()

    def corner():
        copies[2].wait_recv()
        copies[6].start()
        copies[3].wait_recv()
        copies[7].start()

    def arrive():
        for n in range(4, 8):
            copies[n].wait_recv()

    def finish():
        for one in copies:
            one.wait_send()

    return own, pass_on, corner, arrive, finish


def project_kernel(
    tok_ref, seg_ref, wt_ref, wo_ref, small_ref,
    act_ref, dsilu_ref, cin_ref, y_ref, st_ref, sraw_ref, nrm_ref, segb_ref, taps_ref, vec_ref, hv_ref, skip_ref,
    wg_full, wc_full, wo_full,
    wt_f32, wo_f32, stage_in, stage_out, conv_full, slots, pad, segpad, mask, act, *rest,
):
    *scan, local_sems, sends, recvs, small_sends, small_recvs = rest
    j = pl.program_id(0)
    me = lax.axis_index("grp")
    rows_in, rows_out = D // 4, D_INNER // 4
    load_conv = pltpu.make_async_copy(wt_ref.at[D_INNER:], wt_f32.at[D_INNER : D_INNER + CONV_CH + H], local_sems.at[0])
    load_gate = pltpu.make_async_copy(wt_ref.at[:D_INNER], wt_f32.at[:D_INNER], local_sems.at[1])
    load_out = pltpu.make_async_copy(wo_ref, wo_f32, local_sems.at[2])
    keep_conv = pltpu.make_async_copy(
        stage_in.at[:, D_INNER:], conv_full.at[rows_at(me * rows_in, rows_in)], local_sems.at[3]
    )
    keep_gate = pltpu.make_async_copy(
        stage_in.at[:, :D_INNER], wg_full.at[rows_at(me * rows_in, rows_in)], local_sems.at[4]
    )
    keep_out = pltpu.make_async_copy(stage_out, wo_full.at[rows_at(me * rows_out, rows_out)], local_sems.at[5])
    write_conv = pltpu.make_async_copy(conv_full, wc_full, local_sems.at[6])

    def small_copy(n, a, b, hop):
        return pltpu.make_async_remote_copy(
            src_ref=a, dst_ref=b, send_sem=small_sends.at[n], recv_sem=small_recvs.at[n],
            device_id=across(hop), device_id_type=MESH,
        )

    x, y = bit(ALONG_X), bit(ALONG_Y)
    slot_x, slot_y = 2 * y + 1 - x, 2 * (1 - y) + x
    smalls = [
        small_copy(0, small_ref, slots.at[me], ALONG_X),
        small_copy(1, small_ref, slots.at[me], ALONG_Y),
        small_copy(2, slots.at[slot_x, 0:8], slots.at[slot_x, 0:8], ALONG_Y),
        small_copy(3, slots.at[slot_y, 8:16], slots.at[slot_y, 8:16], ALONG_X),
    ]

    def conv_put(start, size):
        return lambda at, n: conv_full.at[rows_at(at, n), start : start + size]

    def gate_put(start, size):
        return lambda at, n: wg_full.at[rows_at(at, n), start : start + size]

    def out_put(start, size):
        return lambda at, n: wo_full.at[rows_at(at, n), start : start + size]

    sems = (sends, recvs)
    pieces = []
    for start, size in ((0, 768), (768, 768), (1536, 896)):
        pieces.append(weight_piece(
            stage_in, slice(D_INNER + start, D_INNER + start + size), conv_put(start, size), sems, len(pieces), rows_in))
    for start, size in ((0, 1024), (1024, 1024)):
        pieces.append(weight_piece(stage_in, slice(start, start + size), gate_put(start, size), sems, len(pieces), rows_in))
    for start, size in ((0, 512), (512, 512)):
        pieces.append(weight_piece(stage_out, slice(start, start + size), out_put(start, size), sems, len(pieces), rows_out))
    OWN, PASS, CORNER, ARRIVE, FINISH = range(5)

    def turn(start, count):
        def body(i, _):
            at = pl.ds(pl.multiple_of(start + i * LANES, LANES), LANES)
            stage_in[:, at] = wt_f32[at, :].T.astype(BF16)
            return 0

        lax.fori_loop(0, count, body, 0)

    @pl.when(j == 0)
    def _():
        load_conv.start()
        load_gate.start()
        load_out.start()
        wt_f32[STEP_AT + H : ALL] = jnp.zeros((LANES - H, wt_f32.shape[1]), F32)
        greet((CORE, ALONG_X, ALONG_Y))
        smalls[0].start()
        smalls[1].start()
        load_conv.wait()
        turn(D_INNER, 6)
        pieces[0][OWN]()
        smalls[0].wait_recv()
        smalls[2].start()
        smalls[1].wait_recv()
        smalls[3].start()
        slots[me] = small_ref[...]
        turn(D_INNER + 768, 6)
        pieces[1][OWN]()
        segment_masks(seg_ref, segb_ref, segpad, mask)
        pieces[0][PASS]()
        smalls[2].wait_recv()
        smalls[3].wait_recv()
        unpack_small(slots, taps_ref, vec_ref, hv_ref, skip_ref)
        turn(D_INNER + 1536, 7)
        keep_conv.start()
        pieces[0][CORNER]()
        pieces[2][OWN]()
        pieces[1][PASS]()
        norm_rows(tok_ref, vec_ref[0:1, :D], nrm_ref)
        keep_conv.wait()
        pieces[0][ARRIVE]()

    @pl.when(j == 1)
    def _():
        pieces[1][CORNER]()
        pieces[2][PASS]()
        load_gate.wait()
        turn(0, 16)
        keep_gate.start()
        pieces[3][OWN]()

    @pl.when(j == 3)
    def _():
        pieces[1][ARRIVE]()
        pieces[2][CORNER]()
        load_out.wait()

        def cast(i, _):
            at = pl.ds(pl.multiple_of(i * 32, 32), 32)
            stage_out[at] = wo_f32[at].astype(BF16)
            return 0

        lax.fori_loop(0, rows_out // 32, cast, 0)
        keep_out.start()
        pieces[4][OWN]()

    @pl.when(j == 4)
    def _():
        pieces[3][PASS]()

    @pl.when(j == 6)
    def _():
        pieces[2][ARRIVE]()
        write_conv.start()
        sraw_ref[...] = dot_nn(nrm_ref[...], conv_full[:, CONV_CH:])
        pieces[3][CORNER]()
        pieces[4][PASS]()
        pieces[5][OWN]()

    @pl.when(j == 8)
    def _():
        pieces[4][CORNER]()
        pieces[6][OWN]()

    @pl.when(j < CT)
    def _():
        conv_tile(j, nrm_ref, conv_full, taps_ref, vec_ref, mask, act_ref, dsilu_ref, cin_ref, pad)
        act[:, tile_at(j)] = act_ref[...]

    @pl.when(j == CT)
    def _():
        pieces[5][PASS]()

    @pl.when(j == CT + 1)
    def _():
        pieces[5][CORNER]()
        pieces[6][PASS]()

    @pl.when(j == CT + 2)
    def _():
        pieces[6][CORNER]()

    @pl.when(j >= CT)
    def _():
        scan_forward(j - CT, act, sraw_ref, segb_ref, seg_ref, hv_ref, skip_ref, y_ref, st_ref, scan)

    @pl.when(j == pl.num_programs(0) - 1)
    def _():
        for n in range(3, 7):
            pieces[n][ARRIVE]()
        for piece in pieces:
            piece[FINISH]()
        for one in smalls:
            one.wait_send()
        keep_gate.wait()
        keep_out.wait()
        write_conv.wait()


def plain_project_kernel(
    tok_ref, seg_ref, w_ref, slots,
    act_ref, dsilu_ref, cin_ref, y_ref, st_ref, sraw_ref, nrm_ref, segb_ref, taps_ref, vec_ref, hv_ref, skip_ref,
    pad, segpad, mask, act, *scan,
):
    j = pl.program_id(0)

    @pl.when(j == 0)
    def _():
        segment_masks(seg_ref, segb_ref, segpad, mask)
        unpack_small(slots, taps_ref, vec_ref, hv_ref, skip_ref)
        norm_rows(tok_ref, vec_ref[0:1, :D], nrm_ref)
        sraw_ref[...] = dot_nn(nrm_ref[...], w_ref[:, CONV_CH:])

    @pl.when(j < CT)
    def _():
        conv_tile(j, nrm_ref, w_ref, taps_ref, vec_ref, mask, act_ref, dsilu_ref, cin_ref, pad)
        act[:, tile_at(j)] = act_ref[...]

    @pl.when(j >= CT)
    def _():
        scan_forward(j - CT, act, sraw_ref, segb_ref, seg_ref, hv_ref, skip_ref, y_ref, st_ref, scan)


def project_outputs(length):
    col = lambda j: (0, jnp.minimum(j, CT - 1))
    fixed = lambda j: (0, 0)
    shapes = [((length, CONV_CH), BF16)] * 3 + [((length, D_INNER), F32), ((length // T, NSTATE, D_INNER), BF16)]
    specs = [pl.BlockSpec((length, W), col)] * 3 + [
        pl.BlockSpec((T, D_INNER), lambda j: (jnp.maximum(j - CT, 0), 0)),
        pl.BlockSpec((1, NSTATE, D_INNER), lambda j: (jnp.maximum(j - CT, 0), 0, 0)),
    ]
    for shape, dtype in (
        ((length, LANES), F32), ((length, D), BF16), ((length, LANES), F32), ((8, CONV_CH), F32), ((8, VEC_PAD), F32),
        ((8, LANES), F32), ((8, D_INNER), F32),
    ):
        shapes.append((shape, dtype))
        specs.append(pl.BlockSpec(shape, fixed))
    scratch = [
        pltpu.VMEM((8 + length, W), F32),
        pltpu.VMEM((8 + length, LANES), F32),
        pltpu.VMEM((KERNEL - 1, length, LANES), F32),
        pltpu.VMEM((length, CONV_CH), BF16),
        *scan_scratch(),
    ]
    return [jax.ShapeDtypeStruct(*one) for one in shapes], specs, scratch


def project_call(tok, seg, wt, wo, small):
    length = tok.shape[0]
    shapes, specs, scratch = project_outputs(length)
    hbm = pl.BlockSpec(memory_space=pl.ANY)
    shapes += [jax.ShapeDtypeStruct(shape, BF16) for shape in ((D, D_INNER), (D, CONV_CH + LANES), (D_INNER, D))]
    return pl.pallas_call(
        project_kernel,
        grid=(CT + length // T,),
        in_specs=[whole(tok.shape), whole(seg.shape), hbm, hbm, whole(small.shape)],
        out_specs=specs + [hbm] * 3,
        out_shape=shapes,
        scratch_shapes=[
            pltpu.VMEM((ALL, D // 4), F32),
            pltpu.VMEM((D_INNER // 4, D), F32),
            pltpu.VMEM((D // 4, ALL), BF16),
            pltpu.VMEM((D_INNER // 4, D), BF16),
            pltpu.VMEM((D, CONV_CH + LANES), BF16),
            pltpu.VMEM((4, *small.shape), F32),
            *scratch,
            pltpu.SemaphoreType.DMA((7,)),
            pltpu.SemaphoreType.DMA((7, 8)),
            pltpu.SemaphoreType.DMA((7, 8)),
            pltpu.SemaphoreType.DMA((4,)),
            pltpu.SemaphoreType.DMA((4,)),
        ],
        compiler_params=pltpu.CompilerParams(collective_id=0, has_side_effects=True, vmem_limit_bytes=VMEM_LIMIT),
        cost_estimate=pl.CostEstimate(flops=2 * length * D * CONV_CH, bytes_accessed=40 << 20, transcendentals=0),
    )(tok, seg, wt, wo, small)


def plain_project_call(tok, seg, w_conv, slots):
    length = tok.shape[0]
    shapes, specs, scratch = project_outputs(length)
    return pl.pallas_call(
        plain_project_kernel,
        grid=(CT + length // T,),
        in_specs=[whole(tok.shape), whole(seg.shape), whole(w_conv.shape), whole(slots.shape)],
        out_specs=specs,
        out_shape=shapes,
        scratch_shapes=scratch,
        compiler_params=pltpu.CompilerParams(vmem_limit_bytes=VMEM_LIMIT),
        cost_estimate=pl.CostEstimate(flops=2 * length * D * CONV_CH, bytes_accessed=20 << 20, transcendentals=0),
    )(tok, seg, w_conv, slots)


def fwd_kernel(
    xs_ref, y_ref, nrm_ref, tok_ref, cot_ref, wg_ref, wo_ref, vec_ref, skip_ref,
    out_ref, mixed_ref, gy_ref, gg_ref, rsum_ref, dgain_ref, dskip_ref,
    silu_scr, sig_scr, gated_scr, gm_scr, sums, rho_b, high, low, pick,
):
    block = pl.program_id(0)

    @pl.when(block == 0)
    def _():
        dgain_ref[...] = jnp.zeros_like(dgain_ref)
        dskip_ref[...] = jnp.zeros_like(dskip_ref)
        set_pick(pick)

    sums[...] = jnp.zeros_like(sums)

    def gate_product(i):
        cols = tile_of(i)
        silu_scr[:, cols] = dot_nn(nrm_ref[...], wg_ref[:, cols])

    gate_product(0)
    for i in range(NT):
        if i + 1 < NT:
            gate_product(i + 1)
        cols = tile_of(i)
        for rows in chunks():
            gate = silu_scr[rows, cols]
            sig = sigmoid(gate)
            silu = gate * sig
            sig_scr[rows, cols] = sig
            silu_scr[rows, cols] = silu
            gated = y_ref[rows, cols] * silu
            gated_scr[rows, cols] = gated
            g2 = gated * gated
            sums[rows] += g2[:, :LANES] + g2[:, LANES:]

    def mixed_product(i):
        cols = tile_of(i)
        gm_scr[:, cols] = dot_nt(cot_ref[...], wo_ref[cols, :])

    mixed_product(0)
    mean2 = jnp.sum(sums[...], axis=1, keepdims=True) * (1.0 / D_INNER)
    rho_b[...] = jnp.broadcast_to(lax.rsqrt(mean2 + EPSILON), (T, LANES))
    sums[...] = jnp.zeros_like(sums)

    for i in range(NT):
        if i + 1 < NT:
            mixed_product(i + 1)
        cols = tile_of(i)
        gain = vec_ref[0:1, D + i * W : D + (i + 1) * W]
        total = jnp.zeros((8, W), F32)
        for rows in chunks():
            gated = gated_scr[rows, cols]
            unit = gated * wide(rho_b[rows])
            mixed_ref[rows, cols] = (unit * gain).astype(BF16)
            gm = gm_scr[rows, cols]
            total = total + rows8(gm * unit)
            e = gm * gain
            gm_scr[rows, cols] = e
            eg = e * gated
            sums[rows] += eg[:, :LANES] + eg[:, LANES:]
        dgain_ref[:, cols] += total

    rho = rho_b[...]
    inner = jnp.sum(sums[...], axis=1, keepdims=True) * (1.0 / D_INNER)
    sums[...] = inner * rho * rho * rho
    rsum_ref[...] = jnp.zeros_like(rsum_ref)

    def out_product(j):
        cols = tile_of(j)
        branch = dot_nn(mixed_ref[...], wo_ref[:, cols])
        out_ref[:, cols] = (tok_ref[:, cols].astype(F32) + branch).astype(BF16)

    for i in range(NT):
        if i % 2 == 0:
            out_product(i // 2)
        cols = tile_of(i)
        skip = skip_ref[0:1, cols]
        total = jnp.zeros((8, W), F32)
        p = i % 2
        for rows in chunks():
            sig = sig_scr[rows, cols]
            silu = silu_scr[rows, cols]
            y = y_ref[rows, cols]
            grad_gated = wide(rho_b[rows]) * gm_scr[rows, cols] - gated_scr[rows, cols] * wide(sums[rows])
            gg_ref[rows, cols] = (grad_gated * y * (sig + silu * (1.0 - sig))).astype(BF16)
            gy = (grad_gated * silu).astype(BF16)
            gy_ref[rows, cols] = gy
            gy = gy.astype(F32)
            xs = xs_ref[rows, cols].astype(F32)
            total = total + rows8(gy * xs)
            split_halves(gy * (y - xs * skip), high.at[p], low.at[p], rows)
        dskip_ref[:, cols] += total
        rsum_ref[...] += head_sums(high.at[p], low.at[p], pick[cols, :])


def fwd_call(xs_bc, y, nrm, tok, cot, wg, wo, vec, skip):
    length = nrm.shape[0]
    blocks = length // T
    tokens = lambda b: (b, 0)
    fixed = lambda b: (0, 0)
    wide_block = pl.BlockSpec((T, D_INNER), tokens)
    return pl.pallas_call(
        fwd_kernel,
        grid=(blocks,),
        in_specs=[
            wide_block,
            wide_block,
            pl.BlockSpec((T, D), tokens),
            pl.BlockSpec((T, D), tokens),
            pl.BlockSpec((T, D), tokens),
            whole(wg.shape),
            whole(wo.shape),
            whole(vec.shape),
            whole(skip.shape),
        ],
        out_specs=[
            pl.BlockSpec((T, D), tokens),
            wide_block,
            wide_block,
            wide_block,
            pl.BlockSpec((T, LANES), tokens),
            pl.BlockSpec((8, D_INNER), fixed),
            pl.BlockSpec((8, D_INNER), fixed),
        ],
        out_shape=[
            jax.ShapeDtypeStruct((length, D), BF16),
            jax.ShapeDtypeStruct((length, D_INNER), BF16),
            jax.ShapeDtypeStruct((length, D_INNER), BF16),
            jax.ShapeDtypeStruct((length, D_INNER), BF16),
            jax.ShapeDtypeStruct((length, LANES), F32),
            jax.ShapeDtypeStruct((8, D_INNER), F32),
            jax.ShapeDtypeStruct((8, D_INNER), F32),
        ],
        scratch_shapes=[
            pltpu.VMEM((T, D_INNER), F32),
            pltpu.VMEM((T, D_INNER), F32),
            pltpu.VMEM((T, D_INNER), F32),
            pltpu.VMEM((T, D_INNER), F32),
            pltpu.VMEM((T, LANES), F32),
            pltpu.VMEM((T, LANES), F32),
            pltpu.VMEM((2, T, W), BF16),
            pltpu.VMEM((2, T, W), BF16),
            pltpu.VMEM((D_INNER, LANES), BF16),
        ],
        compiler_params=pltpu.CompilerParams(vmem_limit_bytes=VMEM_LIMIT),
        cost_estimate=pl.CostEstimate(flops=2 * length * D * D_INNER * 3, bytes_accessed=40 << 20, transcendentals=0),
    )(xs_bc, y, nrm, tok, cot, wg, wo, vec, skip)


def bwd_kernel(remote, *refs):
    if remote:
        ticks, ends, refs = gate_out_plan(refs)
        slots = by_slot(ticks)
    (
        xs_ref, bc_ref, sraw_ref, segb_ref, seg_ref, prev_ref, gy_ref, st_ref, rsum_ref, dsilu_ref, cin_ref,
        hv_ref, skip_ref, taps_ref,
        gc_ref, dtaps_ref, dhv_ref,
        gstate, cum_b, fan, wcat, cum_rows, gf, gscore, gyw_scr, xw_scr, back_scr, through, diag_x, diag_y, gw_scr, gx_scr,
        scores, x1_scr, high, low, high_s, pick, segpad, mask, inner_ref, outer_ref, step_f, from_start, to_end,
    ) = refs
    turn = pl.program_id(0)
    last_turn = pl.num_programs(0) - 1

    @pl.when(turn == 0)
    def _():
        gstate[...] = jnp.zeros_like(gstate)
        wcat[...] = jnp.zeros_like(wcat)
        diag_x[...] = jnp.zeros_like(diag_x)
        diag_y[...] = jnp.zeros_like(diag_y)
        dtaps_ref[...] = jnp.zeros_like(dtaps_ref)
        dhv_ref[...] = jnp.zeros_like(dhv_ref)
        gf[T : T + 8] = jnp.zeros((8, CONV_CH), F32)
        segpad[T : T + 8] = jnp.full((8, LANES), -1.0, F32)
        set_pick(pick)
        set_fan(fan)
        if remote:
            greet(range(5))

    @pl.when(turn > 0)
    def _():
        gf[T : T + 8] = gf[0:8]
        segpad[T : T + 8] = segpad[0:8]

    segb = segb_ref[...]
    segpad[0:T] = segb
    for k in range(1, KERNEL):
        mask[k - 1] = jnp.where(segpad[k : k + T] == segb, 1.0, 0.0)
    v, step, rate = head_terms(sraw_ref, hv_ref)
    logdecay = step * rate
    cum = cumulate(logdecay)
    cum_rows[...] = cum.T
    spread(cum, cum_b)
    bmat = bc_ref[:, :NSTATE]
    cmat = bc_ref[:, NSTATE:]
    s_at, t_at = before(T, T)
    same = wide(segb) == seg_ref[...].astype(F32)
    valid = same & (s_at <= t_at)
    scores[...] = jnp.where(valid, dot_nt(bmat, cmat), 0.0).astype(BF16)
    prev = jnp.where(turn == last_turn, -1.0, prev_ref[7:8])
    last_seg = segb[T - 1 : T]
    last = cum[T - 1 : T]
    expand(step, fan, step_f)
    expand(jnp.exp2(cum) * jnp.where(segb == prev, 1.0, 0.0), fan, from_start)
    expand(jnp.exp2(last - cum) * jnp.where(segb == last_seg, 1.0, 0.0), fan, to_end)
    keep = wide(jnp.where(last_seg == prev, 1.0, 0.0))
    c_t = cmat.astype(F32).T.astype(BF16)
    gst_b = gstate[...].astype(BF16)
    back_scr[...] = dot_nn(bmat, gst_b)
    gscore[...] = jnp.zeros_like(gscore)
    inner_ref[...] = jnp.zeros_like(inner_ref)
    outer_ref[...] = jnp.zeros_like(outer_ref)

    def spread_out(i, p):
        cols = tile_at(i)
        for rows in chunks():
            x1 = (xs_ref[rows, cols].astype(F32) * step_f[rows, cols]).astype(BF16)
            x1_scr[p, rows] = x1
            put_diagonal(diag_x.at[p], rows.start, x1)
            gy = gy_ref[rows, cols]
            put_diagonal(diag_y.at[p], rows.start, gy)
            xw_scr[rows, cols] = (x1.astype(F32) * to_end[rows, cols]).astype(BF16)
            gyw_scr[rows, cols] = (gy.astype(F32) * from_start[rows, cols]).astype(BF16)

    def pair_product(i, p):
        gw_scr[p] = dot_nt(diag_x[p], gy_ref[:, tile_at(i)])

    def decays(i, p):
        for rows in chunks():
            start = 0 if rows.start < LANES else LANES
            total = gscore[rows, start:]
            score = scores[rows, start:]
            for k in range(HPT):
                row = cum_rows[pl.ds(HPT * i + k, 1), :]
                colb = cum_b[HPT * i + k, rows]
                colb = colb if start else wide(colb)
                decay = jnp.exp2(jnp.minimum(row[:, start:] - colb, 0.0))
                wcat[p, rows, k * T + start : (k + 1) * T] = score * decay.astype(BF16)
                total = total + gw_scr[p, k * T + rows.start : k * T + rows.stop, start:] * decay
            gscore[rows, start:] = total

    def grad_product(p):
        gx_scr[p] = dot_nn(wcat[p], diag_y[p])

    def collect(i, p):
        cols = tile_at(i)
        skip = skip_ref[0:1, cols]
        for rows in chunks():
            gx1 = gx_scr[p, rows]
            x1 = x1_scr[p, rows].astype(F32)
            from_state = back_scr[rows, cols] * to_end[rows, cols]
            split_halves(x1 * gx1, high.at[p], low.at[p], rows)
            high_s[p, rows] = (x1 * from_state).astype(BF16)
            gx = (gx1 + from_state) * step_f[rows, cols] + gy_ref[rows, cols].astype(F32) * skip
            gf[rows, cols] = gx * dsilu_ref[rows, cols].astype(F32)
        fade = from_start_last(cum_b, i) * keep
        total = jnp.zeros((8, W), F32)
        for rows in chunks(0, NSTATE):
            gst = gstate[rows, cols] * fade
            gstate[rows, cols] = gst
            total = total + rows8(gst * st_ref[0, rows, cols].astype(F32))
        through[:, cols] = total

    def head_product(i, p):
        pick_i = pick[tile_at(i), :]
        inner_ref[...] += head_sums(high.at[p], low.at[p], pick_i)
        outer_ref[...] += dot_nn(high_s[p], pick_i)

    def two_groups(n, _):
        a, b = 2 * n, 2 * n + 1
        spread_out(a, 0)
        pair_product(a, 0)
        spread_out(b, 1)
        pair_product(b, 1)
        decays(a, 0)
        grad_product(0)
        decays(b, 1)
        grad_product(1)
        collect(a, 0)
        head_product(a, 0)
        collect(b, 1)
        head_product(b, 1)
        if remote:
            for slot, actions in slots.items():

                @pl.when(turn * NT + a == slot - slot % 2)
                def _():
                    for action in actions:
                        action()

        return 0

    lax.fori_loop(0, NT // 2, two_groups, 0)
    gyw = gyw_scr[...]
    gstate[...] += dot_nn(c_t, gyw)
    gsc = jnp.where(valid, gscore[...], 0.0)
    g_b = dot_nn(gsc.astype(BF16), cmat) + dot_nt(xw_scr[...], gst_b)
    g_c = dot_nn(gsc.T.astype(BF16), bmat) + dot_nt(gyw, st_ref[0])
    tail_cols = slice(D_INNER, CONV_CH)
    gf[0:T, tail_cols] = jnp.concatenate([g_b, g_c], axis=1) * dsilu_ref[:, tail_cols].astype(F32)

    inner_sum, outer_sum = inner_ref[...], outer_ref[...]
    after = jnp.where(valid, 1.0, 0.0)
    ahead = jnp.where(same & (s_at > t_at), 1.0, 0.0)
    flow = through[...]
    flow_high = flow.astype(BF16)
    flow_low = (flow - flow_high.astype(F32)).astype(BF16)
    over = jnp.sum(dot_nn(flow_high, pick[...]) + dot_nn(flow_low, pick[...]), axis=0, keepdims=True)
    gl = jnp.dot(after, rsum_ref[...] - inner_sum, precision=HIGHEST, preferred_element_type=F32)
    gl = gl + jnp.dot(ahead, outer_sum, precision=HIGHEST, preferred_element_type=F32) + over
    grad_step = (inner_sum + outer_sum) / jnp.maximum(step, 1e-37) + gl * rate
    lane = lax.broadcasted_iota(jnp.int32, (T, LANES), 1)
    g_sraw = jnp.where(lane < H, grad_step * sigmoid(v), 0.0)
    gc_ref[:, CONV_CH:] = g_sraw.astype(BF16)
    dhv_ref[0:8] += rows8(g_sraw)
    dhv_ref[8:16] += rows8(gl * logdecay)

    def conv_group(j, _):
        cols = tile_at(j)
        taps = [taps_ref[k : k + 1, cols] for k in range(KERNEL)]
        totals = [jnp.zeros((8, W), F32) for _ in range(KERNEL + 1)]
        for rows in chunks():
            here = gf[rows, cols]
            cin = cin_ref[rows, cols].astype(F32)
            totals[KERNEL] = totals[KERNEL] + rows8(here)
            totals[0] = totals[0] + rows8(cin * here)
            total = here * taps[0]
            for k in range(1, KERNEL):
                u = gf[rows.start + k : rows.stop + k, cols] * wide(mask[k - 1, rows])
                total = total + u * taps[k]
                totals[k] = totals[k] + rows8(cin * u)
            gc_ref[rows, cols] = total.astype(BF16)
        for k in range(KERNEL + 1):
            dtaps_ref[8 * k : 8 * k + 8, cols] += totals[k]
        return 0

    lax.fori_loop(0, CT, conv_group, 0)

    if remote:

        @pl.when(turn == last_turn)
        def _():
            for end in ends:
                end()


OUT_CHUNKS, GATE_CHUNKS = 4, 4
OUT_COLS, GATE_COLS = D // OUT_CHUNKS, D_INNER // GATE_CHUNKS
BWD_PACE = (0, 4, 8, 10, 12, 14, 16, 18, 20)
BWD_SLOTS = (0, 1, 3, 4, 6, 7, 9, 11)
TOKEN_PACE = (0, 2, 4, 6, 7, 8, 9, 10, 11)


def gate_out_plan(refs):
    ins, outs, scratch = 14, 3, 28
    head, rest = refs[:ins], refs[ins:]
    (grad_out, grad_gate), rest = rest[:2], rest[2:]
    mid, rest = rest[:outs], rest[outs:]
    (out_total, gate_total), rest = rest[:2], rest[2:]
    tail, rest = rest[:scratch], rest[scratch:]
    out_bufs, gate_bufs, sems = rest[:BUFFERS], rest[BUFFERS : 2 * BUFFERS], rest[2 * BUFFERS :]
    out_starts = [OUT_COLS * n for n in range(OUT_CHUNKS)]
    gate_starts = [GATE_COLS * n for n in range(GATE_CHUNKS)]
    ticks, ends = reduce_plan(
        grad_out, out_starts, OUT_COLS, BWD_SLOTS[0::2], BWD_PACE, out_bufs, out_total, sems, 0, [True] * OUT_CHUNKS
    )
    more, more_ends = reduce_plan(
        grad_gate, gate_starts, GATE_COLS, BWD_SLOTS[1::2], BWD_PACE, gate_bufs, gate_total, sems, OUT_CHUNKS,
        [False] * GATE_CHUNKS,
    )
    return ticks + more, ends + more_ends, (*head, *mid, *tail)


def reduce_sems(count):
    return [
        pltpu.SemaphoreType.DMA((count,)),
        pltpu.SemaphoreType.DMA((count,)),
        pltpu.SemaphoreType.DMA((count, 8)),
        pltpu.SemaphoreType.DMA((count, 8)),
    ]


def bwd_call(xs_bc, sraw, segb, seg, gy, states, rsum, dsilu, cin, hv, skip, taps, grad_out=None, grad_gate=None):
    remote = grad_out is not None
    hbm = pl.BlockSpec(memory_space=pl.ANY)
    length = gy.shape[0]
    blocks = length // T
    tokens = lambda b: (blocks - 1 - b, 0)
    third = lambda b: (blocks - 1 - b, 0, 0)
    fixed = lambda b: (0, 0)
    return pl.pallas_call(
        functools.partial(bwd_kernel, remote),
        grid=(blocks,),
        in_specs=[
            pl.BlockSpec((T, D_INNER), tokens),
            pl.BlockSpec((T, 2 * NSTATE), lambda b: (blocks - 1 - b, D_INNER // (2 * NSTATE))),
            pl.BlockSpec((T, LANES), tokens),
            pl.BlockSpec((T, LANES), tokens),
            pl.BlockSpec((1, T), lambda b: (0, blocks - 1 - b)),
            pl.BlockSpec((8, LANES), lambda b: (jnp.maximum((blocks - 1 - b) * (T // 8) - 1, 0), 0)),
            pl.BlockSpec((T, D_INNER), tokens),
            pl.BlockSpec((1, NSTATE, D_INNER), third),
            pl.BlockSpec((T, LANES), tokens),
            pl.BlockSpec((T, CONV_CH), tokens),
            pl.BlockSpec((T, CONV_CH), tokens),
            whole(hv.shape),
            whole(skip.shape),
            whole(taps.shape),
            *([hbm] * 2 if remote else []),
        ],
        out_specs=[
            pl.BlockSpec((T, CONV_CH + LANES), tokens),
            pl.BlockSpec((8 * (KERNEL + 1), CONV_CH), fixed),
            pl.BlockSpec((16, LANES), fixed),
            *([hbm] * 2 if remote else []),
        ],
        out_shape=[
            jax.ShapeDtypeStruct((length, CONV_CH + LANES), BF16),
            jax.ShapeDtypeStruct((8 * (KERNEL + 1), CONV_CH), F32),
            jax.ShapeDtypeStruct((16, LANES), F32),
            *([jax.ShapeDtypeStruct(g.shape[2:], BF16) for g in (grad_out, grad_gate)] if remote else []),
        ],
        scratch_shapes=[
            pltpu.VMEM((NSTATE, D_INNER), F32),
            pltpu.VMEM((H, T, LANES), F32),
            pltpu.VMEM((2 * LANES, D_INNER), BF16),
            pltpu.VMEM((2, T, HPT * T), BF16),
            pltpu.VMEM((LANES, T), F32),
            pltpu.VMEM((T + 8, CONV_CH), F32),
            pltpu.VMEM((T, T), F32),
            pltpu.VMEM((T, D_INNER), BF16),
            pltpu.VMEM((T, D_INNER), BF16),
            pltpu.VMEM((T, D_INNER), F32),
            pltpu.VMEM((8, D_INNER), F32),
            pltpu.VMEM((2, HPT * T, W), BF16),
            pltpu.VMEM((2, HPT * T, W), BF16),
            pltpu.VMEM((2, HPT * T, T), F32),
            pltpu.VMEM((2, T, W), F32),
            pltpu.VMEM((T, T), BF16),
            pltpu.VMEM((2, T, W), BF16),
            pltpu.VMEM((2, T, W), BF16),
            pltpu.VMEM((2, T, W), BF16),
            pltpu.VMEM((2, T, W), BF16),
            pltpu.VMEM((D_INNER, LANES), BF16),
            pltpu.VMEM((T + 8, LANES), F32),
            pltpu.VMEM((KERNEL - 1, T, LANES), F32),
            pltpu.VMEM((T, LANES), F32),
            pltpu.VMEM((T, LANES), F32),
            pltpu.VMEM((T, D_INNER), F32),
            pltpu.VMEM((T, D_INNER), F32),
            pltpu.VMEM((T, D_INNER), F32),
            *(
                reduce_buffers(grad_out.shape[2], OUT_COLS, OUT_CHUNKS)
                + reduce_buffers(grad_gate.shape[2], GATE_COLS, GATE_CHUNKS)
                + reduce_sems(OUT_CHUNKS + GATE_CHUNKS)
                if remote
                else []
            ),
        ],
        compiler_params=pltpu.CompilerParams(
            vmem_limit_bytes=VMEM_LIMIT, **(dict(collective_id=1, has_side_effects=True) if remote else {})
        ),
        cost_estimate=pl.CostEstimate(flops=2 * length * D * D_INNER * 4, bytes_accessed=30 << 20, transcendentals=0),
    )(xs_bc, xs_bc, sraw, segb, seg, segb, gy, states, rsum, dsilu, cin, hv, skip, taps, *((grad_out, grad_gate) if remote else ()))


CONV_COLS = 2 * W
CONV_CHUNKS = (CONV_CH + LANES) // CONV_COLS
CONV_DONE = CONV_CHUNKS * CONV_COLS
CONV_LEFT = CONV_CH + LANES - CONV_DONE


def token_kernel(remote, *refs):
    (gg_ref, gc_ref, wg_hbm, wc_hbm, tok_ref, cot_ref, vec_ref, taps_sum, vec_sum), refs = refs[:9], refs[9:]
    if remote:
        grad_conv, refs = refs[0], refs[1:]
        (tg_ref, small_total, conv_total), refs = refs[:3], refs[3:]
    else:
        (tg_ref, small_total), refs = refs[:2], refs[2:]
    (wg, wc, grad, dpre, small, load_sems), refs = refs[:6], refs[6:]
    turn = pl.program_id(0)
    last_turn = pl.num_programs(0) - 1
    loads = [
        pltpu.make_async_copy(wg_hbm, wg, load_sems.at[0]),
        pltpu.make_async_copy(wc_hbm, wc, load_sems.at[1]),
    ]
    pieces = D // CONV_COLS
    slots = {}
    if remote:
        conv_bufs, step_bufs, refs = refs[:BUFFERS], refs[BUFFERS : 2 * BUFFERS], refs[2 * BUFFERS :]
        small_bufs, refs = refs[:9], refs[9:]
        sems, small_sems = refs[:4], refs[4:]
        starts = [CONV_COLS * n for n in range(CONV_CHUNKS)]
        ticks, ends = reduce_plan(
            grad_conv, starts, CONV_COLS, range(CONV_CHUNKS), TOKEN_PACE, conv_bufs, conv_total, sems, 0,
            [n % 2 == 0 for n in range(CONV_CHUNKS)],
        )
        more, more_ends = reduce_plan(
            grad_conv, [CONV_DONE], CONV_LEFT, [CONV_CHUNKS], TOKEN_PACE, step_bufs, conv_total, sems, CONV_CHUNKS,
            [True],
        )
        done = 4 * pieces
        last, last_ends = small_plan(small, small_bufs, small_total, small_sems, done, 1)
        slots = by_slot(ticks + more + last)
        ends = ends + more_ends + last_ends

    @pl.when(turn == 0)
    def _():
        for load in loads:
            load.start()
        dpre[...] = jnp.zeros_like(dpre)
        if remote:
            greet(range(5))
            for action in slots.pop(0):
                action()
        for load in loads:
            load.wait()

    def piece(q, _):
        rows = tile_at(q, CONV_COLS)
        grad[:, rows] = dot_nt(gg_ref[...], wg[rows, :]) + dot_nt(gc_ref[...], wc[rows, :])
        for slot, actions in slots.items():
            if slot < 4 * pieces:

                @pl.when(turn * pieces + q == slot)
                def _():
                    for action in actions:
                        action()

        return 0

    lax.fori_loop(0, pieces, piece, 0)
    gain = vec_ref[0:1, :D]
    total = jnp.zeros((8, D), F32)
    step = 16
    for r in range(0, T, step):
        rows = slice(r, r + step)
        tok = tok_ref[rows].astype(F32)
        rho = lax.rsqrt(jnp.sum(tok * tok, axis=1, keepdims=True) * (1.0 / D) + EPSILON)
        unit = tok * rho
        g = grad[rows]
        total = total + rows8(g * unit)
        e = g * gain
        mean = jnp.sum(e * unit, axis=1, keepdims=True) * (1.0 / D)
        tg_ref[rows] = cot_ref[rows].astype(F32) + rho * (e - unit * mean)
    dpre[...] += total

    @pl.when(turn == last_turn)
    def _():
        vec_sum_all = vec_sum[0:1, :]
        pre = jnp.sum(dpre[...], axis=0, keepdims=True)
        vec_all = jnp.concatenate([pre, vec_sum_all[:, D:]], axis=1)
        parts = small.shape[0] * small.shape[1] if remote else small.shape[0]
        n, m = CONV_CH // parts, VEC // parts
        small[...] = jnp.zeros_like(small)
        for p in range(parts):
            at = (p // 2, p % 2) if remote else (p,)
            small[(*at, slice(0, KERNEL), slice(0, n))] = taps_sum[0:KERNEL, n * p : n * (p + 1)]
            small[(*at, slice(8, 9), slice(0, m))] = vec_all[:, m * p : m * (p + 1)]
        if remote:
            for slot in sorted(slots):
                if slot >= 4 * pieces:
                    for action in slots[slot]:
                        action()
            for end in ends:
                end()
        else:
            small_total[...] = small[...]


def token_call(gg, gc, wg, wc, tok, cot, vec, taps_sum, vec_sum, parts, grad_conv=None):
    remote = grad_conv is not None
    length = tok.shape[0]
    tokens = lambda b: (b, 0)
    hbm = pl.BlockSpec(memory_space=pl.ANY)
    small = (2, 2, 16, SMALL_COLS) if remote else (parts, 16, SMALL_COLS)
    small_out = small[2:] if remote else small
    zeros = (0,) * len(small_out)
    return pl.pallas_call(
        functools.partial(token_kernel, remote),
        grid=(length // T,),
        in_specs=[
            pl.BlockSpec((T, D_INNER), tokens),
            pl.BlockSpec((T, CONV_CH + LANES), tokens),
            hbm,
            hbm,
            pl.BlockSpec((T, D), tokens),
            pl.BlockSpec((T, D), tokens),
            whole(vec.shape),
            whole(taps_sum.shape),
            whole(vec_sum.shape),
            *([hbm] if remote else []),
        ],
        out_specs=[
            pl.BlockSpec((T, D), tokens),
            pl.BlockSpec(small_out, lambda b: zeros),
            *([hbm] if remote else []),
        ],
        out_shape=[
            jax.ShapeDtypeStruct((length, D), F32),
            jax.ShapeDtypeStruct(small_out, F32),
            *([jax.ShapeDtypeStruct(grad_conv.shape[2:], BF16)] if remote else []),
        ],
        scratch_shapes=[
            pltpu.VMEM(wg.shape, BF16),
            pltpu.VMEM(wc.shape, BF16),
            pltpu.VMEM((T, D), F32),
            pltpu.VMEM((8, D), F32),
            pltpu.VMEM(small, F32),
            pltpu.SemaphoreType.DMA((2,)),
            *(
                reduce_buffers(grad_conv.shape[2], CONV_COLS, CONV_CHUNKS)
                + reduce_buffers(grad_conv.shape[2], CONV_LEFT, 1)
                + small_buffers(16, SMALL_COLS)
                + reduce_sems(CONV_CHUNKS + 1)
                + [pltpu.SemaphoreType.DMA((5,)), pltpu.SemaphoreType.DMA((5,))]
                if remote
                else []
            ),
        ],
        compiler_params=pltpu.CompilerParams(
            vmem_limit_bytes=VMEM_LIMIT, **(dict(collective_id=2, has_side_effects=True) if remote else {})
        ),
        cost_estimate=pl.CostEstimate(flops=2 * length * D * 4480, bytes_accessed=22 << 20, transcendentals=0),
    )(gg, gc, wg, wc, tok, cot, vec, taps_sum, vec_sum, *((grad_conv,) if remote else ()))


FIRST_FIX = 1.0 / (1.0 - BETA_FIRST**STEP)
SECOND_FIX = 1.0 / (1.0 - BETA_SECOND**STEP)


def adam_step(master, first, second, grad, rate):
    first_new = BETA_FIRST * first + (1.0 - BETA_FIRST) * grad
    second_new = BETA_SECOND * second + (1.0 - BETA_SECOND) * grad * grad
    step = (rate * FIRST_FIX) * first_new / (jnp.sqrt(second_new * SECOND_FIX) + ADAM_EPSILON)
    return ((1.0 - rate * WEIGHT_DECAY) * master - step, first_new, second_new)


def adam_rows(rate, grad, refs, at):
    ins, outs = refs
    for ref, value in zip(outs, adam_step(*(r[at] for r in ins), grad, rate)):
        ref[at] = value


def adam_turned_kernel(rate, tiles, first_ref, second_ref, *refs):
    *refs, turned = refs
    j = pl.program_id(0)
    for which, grad_ref in enumerate((first_ref, second_ref)):

        @pl.when((j >= tiles) == bool(which))
        def _():
            for r in range(0, 2 * W, LANES):
                turned[r : r + LANES] = grad_ref[:, r : r + LANES].astype(F32).T

    for r in range(0, 2 * W, CHUNK):
        at = slice(r, r + CHUNK)
        adam_rows(rate, turned[at], (refs[:3], refs[3:]), at)


def adam_kernel(rate, grad_ref, *refs):
    rows, cols = refs[0].shape
    for r in range(0, rows, CHUNK):
        for c in range(0, cols, W):
            at = (slice(r, r + CHUNK), slice(c, c + W))
            adam_rows(rate, grad_ref[at].astype(F32), (refs[:3], refs[3:]), at)


def adam_call(grads, master, first, second, rate):
    rows, cols = master.shape
    if len(grads) == 2:
        tile = 2 * W
        tiles = grads[0].shape[1] // tile
        kernel = functools.partial(adam_turned_kernel, rate, tiles)
        grad_specs = [
            pl.BlockSpec((cols, tile), lambda j: (0, jnp.minimum(j, tiles - 1))),
            pl.BlockSpec((cols, tile), lambda j: (0, jnp.maximum(j - tiles, 0))),
        ]
    else:
        tile = rows // 4
        kernel = functools.partial(adam_kernel, rate)
        grad_specs = [pl.BlockSpec((tile, cols), lambda j: (j, 0))]
    down = pl.BlockSpec((tile, cols), lambda j: (j, 0))
    scratch = [pltpu.VMEM((tile, cols), F32)] if len(grads) == 2 else []
    return pl.pallas_call(
        kernel,
        grid=(-(-rows // tile),),
        in_specs=[*grad_specs, down, down, down],
        out_specs=[down] * 3,
        out_shape=[jax.ShapeDtypeStruct((rows, cols), F32)] * 3,
        scratch_shapes=scratch,
        compiler_params=pltpu.CompilerParams(vmem_limit_bytes=VMEM_LIMIT),
        cost_estimate=pl.CostEstimate(flops=0, bytes_accessed=26 * rows * cols, transcendentals=0),
    )(*grads, master, first, second)


def owners(grad, parts, remote):
    return grad.reshape(*((2, 2) if remote else (parts,)), -1, grad.shape[1])


def row_pass(projected, tok, cot, seg, wg, wc, wo, parts, remote):
    act, dsilu, cin, y, states, sraw, nrm, segb, taps, vec, hv, skip = projected
    block_out, mixed, gy, gg, rsum, dgain, dskip = fwd_call(act, y, nrm, tok, cot, wg, wo, vec, skip)
    grad_out = owners(dot_tn(mixed, cot).astype(BF16), parts, remote)
    grad_gate = owners(dot_tn(nrm, gg).astype(BF16), parts, remote)
    gc, dtaps, dhv, *totals = bwd_call(
        act, sraw, segb, seg, gy, states, rsum, dsilu, cin, hv, skip, taps, *((grad_out, grad_gate) if remote else ())
    )
    grad_conv = owners(dot_tn(nrm, gc).astype(BF16), parts, remote)
    dtaps = dtaps.reshape(KERNEL + 1, 8, CONV_CH).sum(1)
    dhv = dhv.reshape(2, 8, LANES).sum(1)
    vec_sum = jnp.concatenate(
        [
            jnp.zeros((D,), F32),
            dgain.sum(0),
            dtaps[KERNEL],
            dhv[0, :H],
            dhv[1, :H],
            dskip.sum(0).reshape(H, P_SIZE).sum(1),
            jnp.zeros((VEC_PAD - VEC,), F32),
        ]
    )[None]
    token_grad, small, *conv_total = token_call(
        gg, gc, wg, wc, tok, cot, vec, dtaps, vec_sum, parts, *((grad_conv,) if remote else ())
    )
    if remote:
        out_total, gate_total = totals
        return block_out, token_grad, gate_total, conv_total[0], out_total, small
    return block_out, token_grad, grad_gate, grad_conv, grad_out, small


def local(
    tokens, cotangent, segment_ids, in_weight, out_weight, filter_weight, vectors,
    in_first, out_first, filter_first, vector_first, in_second, out_second, filter_second, vector_second,
):
    remote = lax.axis_size("grp") == 4 and lax.axis_size("dp") == 8
    parts = D // in_weight.shape[0]
    vec_size = vectors.size
    in_turned = in_weight.T
    small = jnp.pad(filter_weight, ((0, 12), (0, SMALL_COLS - filter_weight.shape[1])))
    small = small.at[8, :vec_size].set(vectors)
    tok, cot = tokens[0], cotangent[0]
    if remote:
        *projected, wg, wc, wo = project_call(tok, segment_ids, in_turned, out_weight, small)
    else:
        in_full = lax.all_gather(in_weight.astype(BF16), "grp", axis=0, tiled=True)
        wo = lax.all_gather(out_weight.astype(BF16), "grp", axis=0, tiled=True)
        slots = lax.all_gather(small, "grp")
        wg = in_full[:, :D_INNER]
        wc = jnp.pad(in_full[:, D_INNER:], ((0, 0), (0, LANES - H)))
        projected = plain_project_call(tok, segment_ids, wc, slots)
    block_out, token_grad, *grads = row_pass(projected, tok, cot, segment_ids, wg, wc, wo, parts, remote)
    if not remote:
        grads = [lax.psum(lax.psum_scatter(g, "grp", scatter_dimension=0, tiled=False), "dp") for g in grads]
    gate_total, conv_total, out_total, small_total = grads
    in_new = [a.T for a in adam_call((gate_total, conv_total), in_turned, in_first.T, in_second.T, 0.03)]
    out_new = adam_call((out_total,), out_weight, out_first, out_second, 0.02)
    filter_new = adam_step(
        filter_weight, filter_first, filter_second, small_total[:KERNEL, : filter_weight.shape[1]], 0.3
    )
    vector_new = adam_step(vectors, vector_first, vector_second, small_total[8, :vec_size], 0.3)
    results = (in_new, out_new, filter_new, vector_new)
    return (block_out[None], token_grad[None], *(r[n] for n in range(3) for r in results))


def solution(mesh):
    rows = P(("grp", "dp"), None, None)
    shards = (P("grp", None), P("grp", None), P(None, "grp"), P("grp"))
    in_specs = (rows, rows, P(("grp", "dp"), None)) + shards * 3
    out_specs = (rows, rows) + shards * 3
    return jax.shard_map(local, mesh=mesh, in_specs=in_specs, out_specs=out_specs, check_vma=False)
```

```python
import functools
import itertools
import math

import jax
import jax.numpy as jnp
from jax import lax
from jax.experimental import pallas as pl
from jax.experimental.pallas import tpu as pltpu
from jax.sharding import PartitionSpec as P

D = 1024
H = 32
P_SIZE = 64
NSTATE = 128
KERNEL = 4
STEP = 7
D_INNER = 2048
CONV_CH = 2304
XBC = D_INNER + CONV_CH
LANES = 128
T = 256
W = 256
HPT = W // P_SIZE
NT = D_INNER // W
CT = CONV_CH // W
SMALL_COLS = 1408
SMALL_ROWS = 8
CHUNK = 32
HEADS_AT = D + D_INNER + CONV_CH
VEC = HEADS_AT + 3 * H
VEC_PAD = 5504
STEP_AT = D_INNER + CONV_CH
ALL = STEP_AT + LANES
LOG2E = math.log2(math.e)

EPSILON = 1e-05
ADAM_EPSILON = 1e-08
BETA_FIRST = 0.5
BETA_SECOND = 0.5
WEIGHT_DECAY = 0.1

F32 = jnp.float32
BF16 = jnp.bfloat16
HIGHEST = lax.Precision.HIGHEST
VMEM_LIMIT = 61 * 1024 * 1024


def dot_nn(a, b):
    return lax.dot_general(a, b, (((1,), (0,)), ((), ())), preferred_element_type=F32)


def dot_nt(a, b):
    return lax.dot_general(a, b, (((1,), (1,)), ((), ())), preferred_element_type=F32)


def dot_tn(a, b):
    return lax.dot_general(a, b, (((0,), (0,)), ((), ())), preferred_element_type=F32)


def sigmoid(v):
    return 0.5 * jnp.tanh(0.5 * v) + 0.5


def rows8(v):
    return jnp.sum(v.reshape(v.shape[0] // 8, 8, v.shape[1]), axis=0)


def tile_of(i):
    return slice(i * W, (i + 1) * W)


def tile_at(i, width=W):
    return pl.ds(pl.multiple_of(i * width, width), width)


def whole(shape):
    zeros = (0,) * len(shape)
    return pl.BlockSpec(shape, lambda *_: zeros, pipeline_mode=pl.Buffered(1))


MESH = pl.DeviceIdType.MESH
HOPS = (("dp", 1), ("grp", 1), ("grp", 2), ("dp", 2), ("dp", 4))
CORE, ALONG_X, ALONG_Y, Z_NEAR, Z_FAR = range(5)


def bit(hop):
    name, size = HOPS[hop]
    return lax.rem(lax.div(lax.axis_index(name), size), 2)


def across(hop):
    name, size = HOPS[hop]
    return {name: lax.axis_index(name) + size * (1 - 2 * bit(hop))}


def greet(hops):
    barrier = pltpu.get_barrier_semaphore()
    for hop in hops:
        pl.semaphore_signal(barrier, inc=1, device_id=across(hop), device_id_type=MESH)
    pl.semaphore_wait(barrier, len(hops))


class Transfer:
    def __init__(self, hop, src, dst, send, recv, ways):
        rows = src.shape[-2]
        lead = (slice(None),) * (len(src.shape) - 2)
        parts = [(*lead, pl.ds(i * rows // ways, rows // ways)) for i in range(ways)]

        def copy(a, b):
            return pltpu.make_async_remote_copy(
                src_ref=a, dst_ref=b, send_sem=send, recv_sem=recv, device_id=across(hop), device_id_type=MESH
            )

        self.parts = [copy(src.at[at], dst.at[at]) for at in parts] if ways > 1 else [copy(src, dst)]
        self.whole = copy(src, dst)

    def start(self):
        for part in self.parts:
            part.start()

    def wait_recv(self):
        self.whole.wait_recv()

    def wait_send(self):
        self.whole.wait_send()


def rows_at(start, size):
    return pl.ds(pl.multiple_of(start, size), size)


def add_rows(out, a, b):
    *lead, rows, cols = out.shape
    size = min(rows, max(16, 8192 // cols))
    for at in itertools.product(*(range(n) for n in lead)):
        for r in range(0, rows, size):
            here = (*at, slice(r, r + size))
            out[here] = a[here] + b[here]


def reduce_chunk(src, first_x, bufs, total, sends, recvs, index, local_sem):
    own, r1, r2, r3, r4, r0 = bufs
    rows = src.shape[2]
    half, quarter, eighth = rows // 2, rows // 4, rows // 8
    c, x, y, z1, z2 = (bit(hop) for hop in range(5))
    first, second = (ALONG_X, ALONG_Y) if first_x else (ALONG_Y, ALONG_X)
    base = c * half
    base1 = base + z1 * quarter
    base2 = base1 + z2 * eighth

    def copy(n, hop, a, b, ways=1):
        return Transfer(hop, a, b, sends.at[index, n], recvs.at[index, n], ways)

    def pair(u):
        return own.at[:, u] if first_x else own.at[u]

    kept = bit(first)
    load = pltpu.make_async_copy(src.at[:, :, rows_at(base, half)], own, local_sem)
    here = [total.at[rows_at(base2, eighth)], total.at[rows_at(base1, quarter)], total.at[rows_at(base, half)]]
    copies = [
        copy(0, CORE, src.at[:, :, rows_at((1 - c) * half, half)], r0),
        copy(1, first, pair(1 - kept), r1),
        copy(2, second, r1.at[1 - bit(second)], r2),
        copy(3, Z_NEAR, r2.at[rows_at((1 - z1) * quarter, quarter)], r3),
        copy(4, Z_FAR, r3.at[rows_at((1 - z2) * eighth, eighth)], r4),
        copy(5, Z_FAR, here[0], here[0]),
        copy(6, Z_NEAR, here[1], here[1]),
        copy(7, CORE, here[2], here[2]),
    ]

    def begin():
        load.start()
        copies[0].start()

    def after_core():
        load.wait()
        copies[0].wait_recv()
        add_rows(own, own, r0)
        copies[1].start()

    def after_first():
        copies[1].wait_recv()
        add_rows(r1, r1, pair(kept))
        copies[2].start()

    def after_second():
        copies[2].wait_recv()
        add_rows(r2, r2, r1.at[bit(second)])
        copies[3].start()

    def after_near():
        copies[3].wait_recv()
        add_rows(r3, r3, r2.at[rows_at(z1 * quarter, quarter)])
        copies[4].start()

    def after_far():
        copies[4].wait_recv()
        add_rows(here[0], r4, r3.at[rows_at(z2 * eighth, eighth)])
        copies[5].start()

    def gather_far():
        copies[5].wait_recv()
        copies[6].start()

    def gather_near():
        copies[6].wait_recv()
        copies[7].start()

    def arrive():
        copies[7].wait_recv()

    def finish():
        for one in copies:
            one.wait_send()

    return (begin, after_core, after_first, after_second, after_near, after_far, gather_far, gather_near, arrive), finish


def reduce_buffers(rows, cols, count, dtype=BF16):
    half = rows // 2
    shapes = [
        (2, 2, half, cols), (2, 2, half, cols), (2, half, cols), (half, cols), (half // 2, cols), (half // 4, cols), (rows, cols),
    ]
    return [pltpu.VMEM((count, *shape), dtype) for shape in shapes]


BUFFERS = 7
STAGES = 9


def reduce_plan(sources, starts, slots, pace, bufs, result, sems, base, x_first):
    local_sems, out_sems, sends, recvs = sems
    ticks, ends = [], []
    for n, (src, start, slot) in enumerate(zip(sources, starts, slots)):
        index = base + n
        own, r0, r1, r2, r3, r4, total = (ref.at[n] for ref in bufs)
        stages, finish = reduce_chunk(
            src, x_first[n], (own, r1, r2, r3, r4, r0), total, sends, recvs, index, local_sems.at[index]
        )
        write = pltpu.make_async_copy(total, result.at[:, pl.ds(start, src.shape[-1])], out_sems.at[index])
        for later, stage in zip(pace, stages):
            ticks.append((slot + later, stage))
        ticks.append((slot + pace[-1], write.start))
        ends += [finish, write.wait]
    return ticks, ends


def small_plan(src, bufs, total, sems, slot, spacing):
    sends, recvs = sems
    r0, a1, r1, a2, r2, a3, r3, a4, r4 = bufs
    x, y = bit(ALONG_X), bit(ALONG_Y)

    def copy(n, hop, a, b):
        return pltpu.make_async_remote_copy(
            src_ref=a, dst_ref=b, send_sem=sends.at[n], recv_sem=recvs.at[n], device_id=across(hop), device_id_type=MESH
        )

    copies = [
        copy(0, CORE, src, r0),
        copy(1, ALONG_X, a1.at[:, 1 - x], r1),
        copy(2, ALONG_Y, a2.at[1 - y], r2),
        copy(3, Z_NEAR, a3, r3),
        copy(4, Z_FAR, a4, r4),
    ]

    def after(n, out, one, other):
        def stage():
            copies[n].wait_recv()
            out[...] = one[...] + other[...]
            if n < 4:
                copies[n + 1].start()

        return stage

    stages = [
        copies[0].start,
        after(0, a1, src, r0),
        after(1, a2, a1.at[:, x], r1),
        after(2, a3, a2.at[y], r2),
        after(3, a4, a3, r3),
        after(4, total, a4, r4),
    ]
    return [(slot + k * spacing, stage) for k, stage in enumerate(stages)], [one.wait_send for one in copies]


def small_buffers(rows, cols):
    shapes = [(2, 2, rows, cols), (2, 2, rows, cols), (2, rows, cols), (2, rows, cols)] + [(rows, cols)] * 5
    return [pltpu.VMEM(shape, F32) for shape in shapes]


def by_slot(ticks):
    slots = {}
    for slot, action in ticks:
        slots.setdefault(slot, []).append(action)
    return slots


def head_terms(sraw_ref, hv_ref):
    v = sraw_ref[...] + hv_ref[0:1, :]
    step = jnp.maximum(v, 0.0) + jnp.log1p(jnp.exp(-jnp.abs(v)))
    rate = -jnp.exp(hv_ref[1:2, :])
    return v, step, rate


def before(rows, cols):
    return lax.broadcasted_iota(jnp.int32, (rows, cols), 0), lax.broadcasted_iota(jnp.int32, (rows, cols), 1)


def cumulate(logdecay):
    t, s = before(T, T)
    lower = jnp.where(s <= t, 1.0, 0.0)
    return jnp.dot(lower, logdecay * LOG2E, precision=HIGHEST, preferred_element_type=F32)


def spread(cum, cum_b):
    for h in range(H):
        cum_b[h] = jnp.broadcast_to(cum[:, h : h + 1], (T, LANES))


def expand(values, fan, out):
    high = values.astype(BF16)
    low = (values - high.astype(F32)).astype(BF16)
    both = jnp.concatenate([high, low], axis=1)
    for c in range(0, D_INNER, 2 * W):
        out[:, c : c + 2 * W] = dot_nn(both, fan[:, c : c + 2 * W])


def set_fan(fan):
    for c in range(0, D_INNER, W):
        row, lane = before(2 * LANES, W)
        fan[:, c : c + W] = jnp.where(lax.shift_right_logical(lane + c, 6) == (row & (LANES - 1)), 1.0, 0.0).astype(BF16)


def put_diagonal(diag, r, tile):
    lane = lax.broadcasted_iota(jnp.int32, (tile.shape[0], LANES), 1)
    first = jnp.where(lane < P_SIZE, 1.0, 0.0).astype(BF16)
    second = jnp.where(lane < P_SIZE, 0.0, 1.0).astype(BF16)
    for k in range(HPT):
        at = LANES * (k // 2)
        part = tile[:, at : at + LANES]
        diag[k * T + r : k * T + r + tile.shape[0], at : at + LANES] = part * (first if k % 2 == 0 else second)


def from_start_last(cum_b, i):
    lane = lax.broadcasted_iota(jnp.int32, (1, LANES), 1)
    last = slice(T - 1, T)
    halves = [jnp.where(lane < P_SIZE, cum_b[HPT * i + 2 * k, last], cum_b[HPT * i + 2 * k + 1, last]) for k in range(2)]
    return jnp.exp2(jnp.concatenate(halves, axis=1))


def wide(m):
    return jnp.concatenate([m, m], axis=1)


def split_halves(values, high_ref, low_ref, rows):
    high = values.astype(BF16)
    high_ref[rows] = high
    low_ref[rows] = (values - high.astype(F32)).astype(BF16)


def head_sums(high_ref, low_ref, pick):
    return dot_nn(high_ref[...], pick) + dot_nn(low_ref[...], pick)


def set_pick(pick):
    for r in range(0, D_INNER, T):
        row, lane = before(T, LANES)
        pick[r : r + T] = jnp.where(lax.shift_right_logical(row + r, 6) == lane, 1.0, 0.0).astype(BF16)


def chunks(start=0, stop=T):
    return [slice(r, r + CHUNK) for r in range(start, stop, CHUNK)]


def scan_forward(block, act, sraw_ref, segb_ref, seg_ref, hv_ref, skip_ref, y_ref, st_ref, scratch):
    (
        state, cum_b, fan, wcat, cum_rows, xw_scr, carr_scr, diag, scores, prev_seg, step_f, from_start, to_end,
    ) = scratch
    tokens = rows_at(block * T, T)

    @pl.when(block == 0)
    def _():
        state[...] = jnp.zeros_like(state)
        wcat[...] = jnp.zeros_like(wcat)
        diag[...] = jnp.zeros_like(diag)
        prev_seg[...] = jnp.full(prev_seg.shape, -1.0, F32)
        set_fan(fan)

    _, step, rate = head_terms(sraw_ref.at[tokens], hv_ref)
    cum = cumulate(step * rate)
    cum_rows[...] = cum.T
    spread(cum, cum_b)
    bmat = act[tokens, D_INNER : D_INNER + NSTATE]
    cmat = act[tokens, D_INNER + NSTATE : CONV_CH]
    segb = segb_ref[tokens]
    t_at, s_at = before(T, T)
    valid = (wide(segb) == seg_ref[0:1, tokens].astype(F32)) & (s_at <= t_at)
    scores[...] = jnp.where(valid, dot_nt(cmat, bmat), 0.0).astype(BF16)
    prev = prev_seg[0:1]
    last_seg = segb[T - 1 : T]
    last = cum[T - 1 : T]
    expand(step, fan, step_f)
    expand(jnp.exp2(cum) * jnp.where(segb == prev, 1.0, 0.0), fan, from_start)
    expand(jnp.exp2(last - cum) * jnp.where(segb == last_seg, 1.0, 0.0), fan, to_end)
    keep = wide(jnp.where(last_seg == prev, 1.0, 0.0))
    prev_seg[0:1] = last_seg
    b_t = bmat.astype(F32).T.astype(BF16)
    st_ref[0] = state[...].astype(BF16)
    carr_scr[...] = dot_nn(cmat, st_ref[0])

    def here(rows):
        return pl.ds(pl.multiple_of(block * T + rows.start, CHUNK), CHUNK)

    def prepare(i, p):
        cols = tile_of(i)
        for rows in chunks():
            x1 = (act[here(rows), cols].astype(F32) * step_f[rows, cols]).astype(BF16)
            put_diagonal(diag.at[p], rows.start, x1)
            xw_scr[rows, cols] = (x1.astype(F32) * to_end[rows, cols]).astype(BF16)
        for k in range(HPT):
            row = cum_rows[HPT * i + k : HPT * i + k + 1, :]
            for rows in chunks():
                n = LANES if rows.start < LANES else T
                colb = cum_b[HPT * i + k, rows]
                colb = colb if n == LANES else wide(colb)
                decay = jnp.exp2(jnp.minimum(colb - row[:, :n], 0.0)).astype(BF16)
                wcat[p, rows, k * T : k * T + n] = scores[rows, :n] * decay

    prepare(0, 0)
    for i in range(NT):
        cols = tile_of(i)
        y_ref[:, cols] = dot_nn(wcat[i % 2], diag[i % 2])
        if i + 1 < NT:
            prepare(i + 1, (i + 1) % 2)
        skip = skip_ref[0:1, cols]
        for rows in chunks():
            y = y_ref[rows, cols] + carr_scr[rows, cols] * from_start[rows, cols]
            y_ref[rows, cols] = y + act[here(rows), cols].astype(F32) * skip
        fade = from_start_last(cum_b, i) * keep
        for rows in chunks(0, NSTATE):
            state[rows, cols] = state[rows, cols] * fade
    state[...] += dot_nn(b_t, xw_scr[...])


def scan_scratch():
    return [
        pltpu.VMEM((NSTATE, D_INNER), F32),
        pltpu.VMEM((H, T, LANES), F32),
        pltpu.VMEM((2 * LANES, D_INNER), BF16),
        pltpu.VMEM((2, T, HPT * T), BF16),
        pltpu.VMEM((LANES, T), F32),
        pltpu.VMEM((T, D_INNER), BF16),
        pltpu.VMEM((T, D_INNER), F32),
        pltpu.VMEM((2, HPT * T, W), BF16),
        pltpu.VMEM((T, T), BF16),
        pltpu.VMEM((8, LANES), F32),
        pltpu.VMEM((T, D_INNER), F32),
        pltpu.VMEM((T, D_INNER), F32),
        pltpu.VMEM((T, D_INNER), F32),
    ]


def norm_rows(tok_ref, gain, nrm_ref):
    def body(i, _):
        rows = pl.ds(pl.multiple_of(i * CHUNK, CHUNK), CHUNK)
        tok = tok_ref[rows].astype(F32)
        rho = lax.rsqrt(jnp.sum(tok * tok, axis=1, keepdims=True) * (1.0 / D) + EPSILON)
        nrm_ref[rows] = (tok * rho * gain).astype(BF16)
        return 0

    lax.fori_loop(0, tok_ref.shape[0] // CHUNK, body, 0)


def segment_masks(seg_ref, segb_ref, pad, mask):
    length = segb_ref.shape[0]
    column = jnp.broadcast_to(seg_ref[...].astype(F32), (8, length)).T
    pad[0:8] = jnp.full((8, LANES), -1.0, F32)
    for r in range(0, length, T):
        rows = jnp.broadcast_to(column[r : r + T, 0:1], (T, LANES))
        segb_ref[r : r + T] = rows
        pad[8 + r : 8 + r + T] = rows
    for k in range(1, KERNEL):
        for r in range(0, length, T):
            mask[k - 1, r : r + T] = jnp.where(pad[8 + r - k : 8 + r - k + T] == segb_ref[r : r + T], 1.0, 0.0)


def unpack_small(slots, taps_ref, vec_ref, hv_ref, skip_ref):
    parts = slots.shape[0]
    taps_ref[...] = jnp.zeros_like(taps_ref)
    vec_ref[...] = jnp.zeros_like(vec_ref)
    hv_ref[...] = jnp.zeros_like(hv_ref)
    skip_ref[...] = jnp.zeros_like(skip_ref)
    n, m = CONV_CH // parts, VEC // parts
    for p in range(parts):
        taps_ref[0:KERNEL, n * p : n * (p + 1)] = slots[p, 0:KERNEL, 0:n].astype(BF16).astype(F32)
        vec_ref[0:1, m * p : m * (p + 1)] = slots[p, 8:9, 0:m].astype(BF16).astype(F32)
    for k in range(2):
        hv_ref[k : k + 1, 0:H] = vec_ref[0:1, HEADS_AT + k * H : HEADS_AT + (k + 1) * H]
    for h in range(H):
        at = HEADS_AT + 2 * H + h
        skip_ref[0:1, P_SIZE * h : P_SIZE * (h + 1)] = jnp.broadcast_to(vec_ref[0:1, at : at + 1], (1, P_SIZE))


def conv_tile(j, nrm_ref, w, taps_ref, vec_ref, mask, act_ref, dsilu_ref, cin_ref, pad):
    length = nrm_ref.shape[0]
    pad[0:8] = jnp.zeros((8, W), F32)
    cols = tile_at(j)
    taps = [taps_ref[k : k + 1, cols] for k in range(KERNEL)]
    bias = vec_ref[0:1, pl.ds(pl.multiple_of(D + D_INNER + j * W, W), W)]
    def product(top):
        pad[8 + top : 8 + top + T] = dot_nn(nrm_ref[top : top + T], w[:, cols])

    product(0)
    for top in range(0, length, T):
        if top + T < length:
            product(top + T)
        for r in range(top, top + T, CHUNK):
            here = pad[8 + r : 8 + r + CHUNK]
            cin_ref[r : r + CHUNK] = here.astype(BF16)
            total = bias + here * taps[0]
            for k in range(1, KERNEL):
                m = wide(mask[k - 1, r : r + CHUNK])
                total = total + pad[8 + r - k : 8 + r - k + CHUNK] * m * taps[k]
            sig = sigmoid(total)
            act = total * sig
            act_ref[r : r + CHUNK] = act.astype(BF16)
            dsilu_ref[r : r + CHUNK] = (sig + act * (1.0 - sig)).astype(BF16)


def weight_piece(src, src_cols, put, hop_sems, index, rows):
    sends, recvs = hop_sems
    half, quarter = rows // 2, rows // 4
    me = lax.axis_index("grp")
    x, y = bit(ALONG_X), bit(ALONG_Y)
    slot_x, slot_y, slot_d = 2 * y + 1 - x, 2 * (1 - y) + x, 2 * (1 - y) + 1 - x
    top = bit(CORE) * half

    def copy(n, a, b, hop):
        return Transfer(hop, a, b, sends.at[index, n], recvs.at[index, n], 2)

    def onward(n, slot, start, size, hop):
        return copy(n, put(slot * rows + start, size), put(slot * rows + start, size), hop)

    mine = src.at[rows_at(top, half), src_cols]
    copies = [
        copy(0, mine, put(me * rows + top, half), ALONG_X),
        copy(1, mine, put(me * rows + top, half), ALONG_Y),
        onward(2, slot_x, top, quarter, ALONG_Y),
        onward(3, slot_y, top + quarter, quarter, ALONG_X),
        onward(4, slot_x, top, half, CORE),
        onward(5, slot_y, top, half, CORE),
        onward(6, slot_d, top, quarter, CORE),
        onward(7, slot_d, top + quarter, quarter, CORE),
    ]

    def own():
        copies[0].start()
        copies[1].start()

    def pass_on():
        copies[0].wait_recv()
        copies[2].start()
        copies[1].wait_recv()
        copies[3].start()
        copies[4].start()
        copies[5].start()

    def corner():
        copies[2].wait_recv()
        copies[6].start()
        copies[3].wait_recv()
        copies[7].start()

    def arrive():
        for n in range(4, 8):
            copies[n].wait_recv()

    def finish():
        for one in copies:
            one.wait_send()

    return own, pass_on, corner, arrive, finish


def project_kernel(
    tok_ref, seg_ref, wt_ref, wo_ref, small_ref,
    act_ref, dsilu_ref, cin_ref, y_ref, st_ref, sraw_ref, nrm_ref, segb_ref, taps_ref, vec_ref, hv_ref, skip_ref,
    wg_full, wc_full, wo_full,
    wt_f32, wo_f32, stage_in, stage_out, conv_full, slots, pad, segpad, mask, act, *rest,
):
    *scan, local_sems, sends, recvs, small_sends, small_recvs = rest
    j = pl.program_id(0)
    me = lax.axis_index("grp")
    rows_in, rows_out = D // 4, D_INNER // 4
    load_conv = pltpu.make_async_copy(wt_ref.at[D_INNER:], wt_f32.at[D_INNER : D_INNER + CONV_CH + H], local_sems.at[0])
    load_gate = pltpu.make_async_copy(wt_ref.at[:D_INNER], wt_f32.at[:D_INNER], local_sems.at[1])
    load_out = pltpu.make_async_copy(wo_ref, wo_f32, local_sems.at[2])
    keep_conv = pltpu.make_async_copy(
        stage_in.at[:, D_INNER:], conv_full.at[rows_at(me * rows_in, rows_in)], local_sems.at[3]
    )
    keep_gate = pltpu.make_async_copy(
        stage_in.at[:, :D_INNER], wg_full.at[rows_at(me * rows_in, rows_in)], local_sems.at[4]
    )
    keep_out = pltpu.make_async_copy(stage_out, wo_full.at[rows_at(me * rows_out, rows_out)], local_sems.at[5])
    write_conv = pltpu.make_async_copy(conv_full, wc_full, local_sems.at[6])

    def small_copy(n, a, b, hop):
        return pltpu.make_async_remote_copy(
            src_ref=a, dst_ref=b, send_sem=small_sends.at[n], recv_sem=small_recvs.at[n],
            device_id=across(hop), device_id_type=MESH,
        )

    x, y = bit(ALONG_X), bit(ALONG_Y)
    slot_x, slot_y = 2 * y + 1 - x, 2 * (1 - y) + x
    smalls = [
        small_copy(0, small_ref, slots.at[me], ALONG_X),
        small_copy(1, small_ref, slots.at[me], ALONG_Y),
        small_copy(2, slots.at[slot_x, 0:8], slots.at[slot_x, 0:8], ALONG_Y),
        small_copy(3, slots.at[slot_y, 8:16], slots.at[slot_y, 8:16], ALONG_X),
    ]

    def conv_put(start, size):
        return lambda at, n: conv_full.at[rows_at(at, n), start : start + size]

    def gate_put(start, size):
        return lambda at, n: wg_full.at[rows_at(at, n), start : start + size]

    def out_put(start, size):
        return lambda at, n: wo_full.at[rows_at(at, n), start : start + size]

    sems = (sends, recvs)
    pieces = []
    for start, size in ((0, 768), (768, 768), (1536, 896)):
        pieces.append(weight_piece(
            stage_in, slice(D_INNER + start, D_INNER + start + size), conv_put(start, size), sems, len(pieces), rows_in))
    for start, size in ((0, 1024), (1024, 1024)):
        pieces.append(weight_piece(stage_in, slice(start, start + size), gate_put(start, size), sems, len(pieces), rows_in))
    for start, size in ((0, 512), (512, 512)):
        pieces.append(weight_piece(stage_out, slice(start, start + size), out_put(start, size), sems, len(pieces), rows_out))
    OWN, PASS, CORNER, ARRIVE, FINISH = range(5)

    def turn(start, count):
        def body(i, _):
            at = pl.ds(pl.multiple_of(start + i * LANES, LANES), LANES)
            stage_in[:, at] = wt_f32[at, :].T.astype(BF16)
            return 0

        lax.fori_loop(0, count, body, 0)

    @pl.when(j == 0)
    def _():
        load_conv.start()
        load_gate.start()
        load_out.start()
        wt_f32[STEP_AT + H : ALL] = jnp.zeros((LANES - H, wt_f32.shape[1]), F32)
        greet((CORE, ALONG_X, ALONG_Y))
        smalls[0].start()
        smalls[1].start()
        load_conv.wait()
        turn(D_INNER, 6)
        pieces[0][OWN]()
        smalls[0].wait_recv()
        smalls[2].start()
        smalls[1].wait_recv()
        smalls[3].start()
        slots[me] = small_ref[...]
        turn(D_INNER + 768, 6)
        pieces[1][OWN]()
        segment_masks(seg_ref, segb_ref, segpad, mask)
        pieces[0][PASS]()
        smalls[2].wait_recv()
        smalls[3].wait_recv()
        unpack_small(slots, taps_ref, vec_ref, hv_ref, skip_ref)
        turn(D_INNER + 1536, 7)
        keep_conv.start()
        pieces[0][CORNER]()
        pieces[2][OWN]()
        pieces[1][PASS]()
        norm_rows(tok_ref, vec_ref[0:1, :D], nrm_ref)
        keep_conv.wait()
        pieces[0][ARRIVE]()

    @pl.when(j == 1)
    def _():
        pieces[1][CORNER]()
        pieces[2][PASS]()
        load_gate.wait()
        turn(0, 16)
        keep_gate.start()
        pieces[3][OWN]()

    @pl.when(j == 3)
    def _():
        pieces[1][ARRIVE]()
        pieces[2][CORNER]()
        load_out.wait()

        def cast(i, _):
            at = pl.ds(pl.multiple_of(i * 32, 32), 32)
            stage_out[at] = wo_f32[at].astype(BF16)
            return 0

        lax.fori_loop(0, rows_out // 32, cast, 0)
        keep_out.start()
        pieces[4][OWN]()

    @pl.when(j == 4)
    def _():
        pieces[3][PASS]()

    @pl.when(j == 6)
    def _():
        pieces[2][ARRIVE]()
        write_conv.start()
        sraw_ref[...] = dot_nn(nrm_ref[...], conv_full[:, CONV_CH:])
        pieces[3][CORNER]()
        pieces[4][PASS]()
        pieces[5][OWN]()

    @pl.when(j == 8)
    def _():
        pieces[4][CORNER]()
        pieces[6][OWN]()

    @pl.when(j < CT)
    def _():
        conv_tile(j, nrm_ref, conv_full, taps_ref, vec_ref, mask, act_ref, dsilu_ref, cin_ref, pad)
        act[:, tile_at(j)] = act_ref[...]

    @pl.when(j == CT)
    def _():
        pieces[5][PASS]()

    @pl.when(j == CT + 1)
    def _():
        pieces[5][CORNER]()
        pieces[6][PASS]()

    @pl.when(j == CT + 2)
    def _():
        pieces[6][CORNER]()

    @pl.when(j >= CT)
    def _():
        scan_forward(j - CT, act, sraw_ref, segb_ref, seg_ref, hv_ref, skip_ref, y_ref, st_ref, scan)

    @pl.when(j == pl.num_programs(0) - 1)
    def _():
        for n in range(3, 7):
            pieces[n][ARRIVE]()
        for piece in pieces:
            piece[FINISH]()
        for one in smalls:
            one.wait_send()
        keep_gate.wait()
        keep_out.wait()
        write_conv.wait()


def plain_project_kernel(
    tok_ref, seg_ref, w_ref, slots,
    act_ref, dsilu_ref, cin_ref, y_ref, st_ref, sraw_ref, nrm_ref, segb_ref, taps_ref, vec_ref, hv_ref, skip_ref,
    pad, segpad, mask, act, *scan,
):
    j = pl.program_id(0)

    @pl.when(j == 0)
    def _():
        segment_masks(seg_ref, segb_ref, segpad, mask)
        unpack_small(slots, taps_ref, vec_ref, hv_ref, skip_ref)
        norm_rows(tok_ref, vec_ref[0:1, :D], nrm_ref)
        sraw_ref[...] = dot_nn(nrm_ref[...], w_ref[:, CONV_CH:])

    @pl.when(j < CT)
    def _():
        conv_tile(j, nrm_ref, w_ref, taps_ref, vec_ref, mask, act_ref, dsilu_ref, cin_ref, pad)
        act[:, tile_at(j)] = act_ref[...]

    @pl.when(j >= CT)
    def _():
        scan_forward(j - CT, act, sraw_ref, segb_ref, seg_ref, hv_ref, skip_ref, y_ref, st_ref, scan)


def project_outputs(length):
    col = lambda j: (0, jnp.minimum(j, CT - 1))
    fixed = lambda j: (0, 0)
    shapes = [((length, CONV_CH), BF16)] * 3 + [((length, D_INNER), F32), ((length // T, NSTATE, D_INNER), BF16)]
    specs = [pl.BlockSpec((length, W), col)] * 3 + [
        pl.BlockSpec((T, D_INNER), lambda j: (jnp.maximum(j - CT, 0), 0)),
        pl.BlockSpec((1, NSTATE, D_INNER), lambda j: (jnp.maximum(j - CT, 0), 0, 0)),
    ]
    for shape, dtype in (
        ((length, LANES), F32), ((length, D), BF16), ((length, LANES), F32), ((8, CONV_CH), F32), ((8, VEC_PAD), F32),
        ((8, LANES), F32), ((8, D_INNER), F32),
    ):
        shapes.append((shape, dtype))
        specs.append(pl.BlockSpec(shape, fixed))
    scratch = [
        pltpu.VMEM((8 + length, W), F32),
        pltpu.VMEM((8 + length, LANES), F32),
        pltpu.VMEM((KERNEL - 1, length, LANES), F32),
        pltpu.VMEM((length, CONV_CH), BF16),
        *scan_scratch(),
    ]
    return [jax.ShapeDtypeStruct(*one) for one in shapes], specs, scratch


def project_call(tok, seg, wt, wo, small):
    length = tok.shape[0]
    shapes, specs, scratch = project_outputs(length)
    hbm = pl.BlockSpec(memory_space=pl.ANY)
    shapes += [jax.ShapeDtypeStruct(shape, BF16) for shape in ((D, D_INNER), (D, CONV_CH + LANES), (D_INNER, D))]
    return pl.pallas_call(
        project_kernel,
        grid=(CT + length // T,),
        in_specs=[whole(tok.shape), whole(seg.shape), hbm, hbm, whole(small.shape)],
        out_specs=specs + [hbm] * 3,
        out_shape=shapes,
        scratch_shapes=[
            pltpu.VMEM((ALL, D // 4), F32),
            pltpu.VMEM((D_INNER // 4, D), F32),
            pltpu.VMEM((D // 4, ALL), BF16),
            pltpu.VMEM((D_INNER // 4, D), BF16),
            pltpu.VMEM((D, CONV_CH + LANES), BF16),
            pltpu.VMEM((4, *small.shape), F32),
            *scratch,
            pltpu.SemaphoreType.DMA((7,)),
            pltpu.SemaphoreType.DMA((7, 8)),
            pltpu.SemaphoreType.DMA((7, 8)),
            pltpu.SemaphoreType.DMA((4,)),
            pltpu.SemaphoreType.DMA((4,)),
        ],
        compiler_params=pltpu.CompilerParams(collective_id=0, has_side_effects=True, vmem_limit_bytes=VMEM_LIMIT),
        cost_estimate=pl.CostEstimate(flops=2 * length * D * CONV_CH, bytes_accessed=40 << 20, transcendentals=0),
    )(tok, seg, wt, wo, small)


def plain_project_call(tok, seg, w_conv, slots):
    length = tok.shape[0]
    shapes, specs, scratch = project_outputs(length)
    return pl.pallas_call(
        plain_project_kernel,
        grid=(CT + length // T,),
        in_specs=[whole(tok.shape), whole(seg.shape), whole(w_conv.shape), whole(slots.shape)],
        out_specs=specs,
        out_shape=shapes,
        scratch_shapes=scratch,
        compiler_params=pltpu.CompilerParams(vmem_limit_bytes=VMEM_LIMIT),
        cost_estimate=pl.CostEstimate(flops=2 * length * D * CONV_CH, bytes_accessed=20 << 20, transcendentals=0),
    )(tok, seg, w_conv, slots)


def fwd_kernel(
    xs_ref, y_ref, nrm_ref, tok_ref, cot_ref, wg_ref, wo_ref, vec_ref, skip_ref,
    out_ref, mixed_ref, gy_ref, gg_ref, rsum_ref, dgain_ref, dskip_ref,
    silu_scr, sig_scr, gated_scr, gm_scr, sums, rho_b, high, low, pick,
):
    block = pl.program_id(0)

    @pl.when(block == 0)
    def _():
        dgain_ref[...] = jnp.zeros_like(dgain_ref)
        dskip_ref[...] = jnp.zeros_like(dskip_ref)
        set_pick(pick)

    sums[...] = jnp.zeros_like(sums)

    def gate_product(i):
        cols = tile_of(i)
        silu_scr[:, cols] = dot_nn(nrm_ref[...], wg_ref[:, cols])

    gate_product(0)
    for i in range(NT):
        if i + 1 < NT:
            gate_product(i + 1)
        cols = tile_of(i)
        for rows in chunks():
            gate = silu_scr[rows, cols]
            sig = sigmoid(gate)
            silu = gate * sig
            sig_scr[rows, cols] = sig
            silu_scr[rows, cols] = silu
            gated = y_ref[rows, cols] * silu
            gated_scr[rows, cols] = gated
            g2 = gated * gated
            sums[rows] += g2[:, :LANES] + g2[:, LANES:]

    def mixed_product(i):
        cols = tile_of(i)
        gm_scr[:, cols] = dot_nt(cot_ref[...], wo_ref[cols, :])

    mixed_product(0)
    mean2 = jnp.sum(sums[...], axis=1, keepdims=True) * (1.0 / D_INNER)
    rho_b[...] = jnp.broadcast_to(lax.rsqrt(mean2 + EPSILON), (T, LANES))
    sums[...] = jnp.zeros_like(sums)

    for i in range(NT):
        if i + 1 < NT:
            mixed_product(i + 1)
        cols = tile_of(i)
        gain = vec_ref[0:1, D + i * W : D + (i + 1) * W]
        total = jnp.zeros((8, W), F32)
        for rows in chunks():
            gated = gated_scr[rows, cols]
            unit = gated * wide(rho_b[rows])
            mixed_ref[rows, cols] = (unit * gain).astype(BF16)
            gm = gm_scr[rows, cols]
            total = total + rows8(gm * unit)
            e = gm * gain
            gm_scr[rows, cols] = e
            eg = e * gated
            sums[rows] += eg[:, :LANES] + eg[:, LANES:]
        dgain_ref[:, cols] += total

    rho = rho_b[...]
    inner = jnp.sum(sums[...], axis=1, keepdims=True) * (1.0 / D_INNER)
    sums[...] = inner * rho * rho * rho
    rsum_ref[...] = jnp.zeros_like(rsum_ref)

    def out_product(j):
        cols = tile_of(j)
        branch = dot_nn(mixed_ref[...], wo_ref[:, cols])
        out_ref[:, cols] = (tok_ref[:, cols].astype(F32) + branch).astype(BF16)

    for i in range(NT):
        if i % 2 == 0:
            out_product(i // 2)
        cols = tile_of(i)
        skip = skip_ref[0:1, cols]
        total = jnp.zeros((8, W), F32)
        p = i % 2
        for rows in chunks():
            sig = sig_scr[rows, cols]
            silu = silu_scr[rows, cols]
            y = y_ref[rows, cols]
            grad_gated = wide(rho_b[rows]) * gm_scr[rows, cols] - gated_scr[rows, cols] * wide(sums[rows])
            gg_ref[rows, cols] = (grad_gated * y * (sig + silu * (1.0 - sig))).astype(BF16)
            gy = (grad_gated * silu).astype(BF16)
            gy_ref[rows, cols] = gy
            gy = gy.astype(F32)
            xs = xs_ref[rows, cols].astype(F32)
            total = total + rows8(gy * xs)
            split_halves(gy * (y - xs * skip), high.at[p], low.at[p], rows)
        dskip_ref[:, cols] += total
        rsum_ref[...] += head_sums(high.at[p], low.at[p], pick[cols, :])


def fwd_call(xs_bc, y, nrm, tok, cot, wg, wo, vec, skip):
    length = nrm.shape[0]
    blocks = length // T
    tokens = lambda b: (b, 0)
    fixed = lambda b: (0, 0)
    wide_block = pl.BlockSpec((T, D_INNER), tokens)
    return pl.pallas_call(
        fwd_kernel,
        grid=(blocks,),
        in_specs=[
            wide_block,
            wide_block,
            pl.BlockSpec((T, D), tokens),
            pl.BlockSpec((T, D), tokens),
            pl.BlockSpec((T, D), tokens),
            whole(wg.shape),
            whole(wo.shape),
            whole(vec.shape),
            whole(skip.shape),
        ],
        out_specs=[
            pl.BlockSpec((T, D), tokens),
            wide_block,
            wide_block,
            wide_block,
            pl.BlockSpec((T, LANES), tokens),
            pl.BlockSpec((8, D_INNER), fixed),
            pl.BlockSpec((8, D_INNER), fixed),
        ],
        out_shape=[
            jax.ShapeDtypeStruct((length, D), BF16),
            jax.ShapeDtypeStruct((length, D_INNER), BF16),
            jax.ShapeDtypeStruct((length, D_INNER), BF16),
            jax.ShapeDtypeStruct((length, D_INNER), BF16),
            jax.ShapeDtypeStruct((length, LANES), F32),
            jax.ShapeDtypeStruct((8, D_INNER), F32),
            jax.ShapeDtypeStruct((8, D_INNER), F32),
        ],
        scratch_shapes=[
            pltpu.VMEM((T, D_INNER), F32),
            pltpu.VMEM((T, D_INNER), F32),
            pltpu.VMEM((T, D_INNER), F32),
            pltpu.VMEM((T, D_INNER), F32),
            pltpu.VMEM((T, LANES), F32),
            pltpu.VMEM((T, LANES), F32),
            pltpu.VMEM((2, T, W), BF16),
            pltpu.VMEM((2, T, W), BF16),
            pltpu.VMEM((D_INNER, LANES), BF16),
        ],
        compiler_params=pltpu.CompilerParams(vmem_limit_bytes=VMEM_LIMIT),
        cost_estimate=pl.CostEstimate(flops=2 * length * D * D_INNER * 3, bytes_accessed=40 << 20, transcendentals=0),
    )(xs_bc, y, nrm, tok, cot, wg, wo, vec, skip)


def bwd_kernel(remote, *refs):
    if remote:
        ticks, ends, refs = gate_out_plan(refs)
        slots = by_slot(ticks)
    (
        xs_ref, bc_ref, sraw_ref, segb_ref, seg_ref, prev_ref, gy_ref, st_ref, rsum_ref, dsilu_ref, cin_ref,
        hv_ref, skip_ref, taps_ref,
        gc_ref, dtaps_ref, dhv_ref,
        gstate, cum_b, fan, wcat, cum_rows, gf, gscore, gyw_scr, xw_scr, back_scr, through, diag_x, diag_y, gw_scr, gx_scr,
        scores, x1_scr, high, low, high_s, pick, segpad, mask, inner_ref, outer_ref, step_f, from_start, to_end,
    ) = refs
    turn = pl.program_id(0)
    last_turn = pl.num_programs(0) - 1

    @pl.when(turn == 0)
    def _():
        gstate[...] = jnp.zeros_like(gstate)
        wcat[...] = jnp.zeros_like(wcat)
        diag_x[...] = jnp.zeros_like(diag_x)
        diag_y[...] = jnp.zeros_like(diag_y)
        dtaps_ref[...] = jnp.zeros_like(dtaps_ref)
        dhv_ref[...] = jnp.zeros_like(dhv_ref)
        gf[T : T + 8] = jnp.zeros((8, CONV_CH), F32)
        segpad[T : T + 8] = jnp.full((8, LANES), -1.0, F32)
        set_pick(pick)
        set_fan(fan)
        if remote:
            greet(range(5))

    @pl.when(turn > 0)
    def _():
        gf[T : T + 8] = gf[0:8]
        segpad[T : T + 8] = segpad[0:8]

    segb = segb_ref[...]
    segpad[0:T] = segb
    for k in range(1, KERNEL):
        mask[k - 1] = jnp.where(segpad[k : k + T] == segb, 1.0, 0.0)
    v, step, rate = head_terms(sraw_ref, hv_ref)
    logdecay = step * rate
    cum = cumulate(logdecay)
    cum_rows[...] = cum.T
    spread(cum, cum_b)
    bmat = bc_ref[:, :NSTATE]
    cmat = bc_ref[:, NSTATE:]
    s_at, t_at = before(T, T)
    same = wide(segb) == seg_ref[...].astype(F32)
    valid = same & (s_at <= t_at)
    scores[...] = jnp.where(valid, dot_nt(bmat, cmat), 0.0).astype(BF16)
    prev = jnp.where(turn == last_turn, -1.0, prev_ref[7:8])
    last_seg = segb[T - 1 : T]
    last = cum[T - 1 : T]
    expand(step, fan, step_f)
    expand(jnp.exp2(cum) * jnp.where(segb == prev, 1.0, 0.0), fan, from_start)
    expand(jnp.exp2(last - cum) * jnp.where(segb == last_seg, 1.0, 0.0), fan, to_end)
    keep = wide(jnp.where(last_seg == prev, 1.0, 0.0))
    c_t = cmat.astype(F32).T.astype(BF16)
    gst_b = gstate[...].astype(BF16)
    back_scr[...] = dot_nn(bmat, gst_b)
    gscore[...] = jnp.zeros_like(gscore)
    inner_ref[...] = jnp.zeros_like(inner_ref)
    outer_ref[...] = jnp.zeros_like(outer_ref)

    def spread_out(i, p):
        cols = tile_at(i)
        for rows in chunks():
            x1 = (xs_ref[rows, cols].astype(F32) * step_f[rows, cols]).astype(BF16)
            x1_scr[p, rows] = x1
            put_diagonal(diag_x.at[p], rows.start, x1)
            gy = gy_ref[rows, cols]
            put_diagonal(diag_y.at[p], rows.start, gy)
            xw_scr[rows, cols] = (x1.astype(F32) * to_end[rows, cols]).astype(BF16)
            gyw_scr[rows, cols] = (gy.astype(F32) * from_start[rows, cols]).astype(BF16)

    def pair_product(i, p):
        gw_scr[p] = dot_nt(diag_x[p], gy_ref[:, tile_at(i)])

    def decays(i, p):
        for rows in chunks():
            start = 0 if rows.start < LANES else LANES
            total = gscore[rows, start:]
            score = scores[rows, start:]
            for k in range(HPT):
                row = cum_rows[pl.ds(HPT * i + k, 1), :]
                colb = cum_b[HPT * i + k, rows]
                colb = colb if start else wide(colb)
                decay = jnp.exp2(jnp.minimum(row[:, start:] - colb, 0.0))
                wcat[p, rows, k * T + start : (k + 1) * T] = score * decay.astype(BF16)
                total = total + gw_scr[p, k * T + rows.start : k * T + rows.stop, start:] * decay
            gscore[rows, start:] = total

    def grad_product(p):
        gx_scr[p] = dot_nn(wcat[p], diag_y[p])

    def collect(i, p):
        cols = tile_at(i)
        skip = skip_ref[0:1, cols]
        for rows in chunks():
            gx1 = gx_scr[p, rows]
            x1 = x1_scr[p, rows].astype(F32)
            from_state = back_scr[rows, cols] * to_end[rows, cols]
            split_halves(x1 * gx1, high.at[p], low.at[p], rows)
            high_s[p, rows] = (x1 * from_state).astype(BF16)
            gx = (gx1 + from_state) * step_f[rows, cols] + gy_ref[rows, cols].astype(F32) * skip
            gf[rows, cols] = gx * dsilu_ref[rows, cols].astype(F32)
        fade = from_start_last(cum_b, i) * keep
        total = jnp.zeros((8, W), F32)
        for rows in chunks(0, NSTATE):
            gst = gstate[rows, cols] * fade
            gstate[rows, cols] = gst
            total = total + rows8(gst * st_ref[0, rows, cols].astype(F32))
        through[:, cols] = total

    def head_product(i, p):
        pick_i = pick[tile_at(i), :]
        inner_ref[...] += head_sums(high.at[p], low.at[p], pick_i)
        outer_ref[...] += dot_nn(high_s[p], pick_i)

    def two_groups(n, _):
        a, b = 2 * n, 2 * n + 1
        spread_out(a, 0)
        pair_product(a, 0)
        spread_out(b, 1)
        pair_product(b, 1)
        decays(a, 0)
        grad_product(0)
        decays(b, 1)
        grad_product(1)
        collect(a, 0)
        head_product(a, 0)
        collect(b, 1)
        head_product(b, 1)
        if remote:
            for slot, actions in sorted(slots.items()):

                @pl.when(turn * NT + a == slot - slot % 2)
                def _():
                    for action in actions:
                        action()

        return 0

    lax.fori_loop(0, NT // 2, two_groups, 0)
    gyw = gyw_scr[...]
    gstate[...] += dot_nn(c_t, gyw)
    gsc = jnp.where(valid, gscore[...], 0.0)
    g_b = dot_nn(gsc.astype(BF16), cmat) + dot_nt(xw_scr[...], gst_b)
    g_c = dot_nn(gsc.T.astype(BF16), bmat) + dot_nt(gyw, st_ref[0])
    tail_cols = slice(D_INNER, CONV_CH)
    gf[0:T, tail_cols] = jnp.concatenate([g_b, g_c], axis=1) * dsilu_ref[:, tail_cols].astype(F32)

    inner_sum, outer_sum = inner_ref[...], outer_ref[...]
    after = jnp.where(valid, 1.0, 0.0)
    ahead = jnp.where(same & (s_at > t_at), 1.0, 0.0)
    flow = through[...]
    flow_high = flow.astype(BF16)
    flow_low = (flow - flow_high.astype(F32)).astype(BF16)
    over = jnp.sum(dot_nn(flow_high, pick[...]) + dot_nn(flow_low, pick[...]), axis=0, keepdims=True)
    gl = jnp.dot(after, rsum_ref[...] - inner_sum, precision=HIGHEST, preferred_element_type=F32)
    gl = gl + jnp.dot(ahead, outer_sum, precision=HIGHEST, preferred_element_type=F32) + over
    grad_step = (inner_sum + outer_sum) / jnp.maximum(step, 1e-37) + gl * rate
    lane = lax.broadcasted_iota(jnp.int32, (T, LANES), 1)
    g_sraw = jnp.where(lane < H, grad_step * sigmoid(v), 0.0)
    gc_ref[:, CONV_CH:] = g_sraw.astype(BF16)
    dhv_ref[0:8] += rows8(g_sraw)
    dhv_ref[8:16] += rows8(gl * logdecay)

    def conv_group(j, _):
        cols = tile_at(j)
        taps = [taps_ref[k : k + 1, cols] for k in range(KERNEL)]
        totals = [jnp.zeros((8, W), F32) for _ in range(KERNEL + 1)]
        for rows in chunks():
            here = gf[rows, cols]
            cin = cin_ref[rows, cols].astype(F32)
            totals[KERNEL] = totals[KERNEL] + rows8(here)
            totals[0] = totals[0] + rows8(cin * here)
            total = here * taps[0]
            for k in range(1, KERNEL):
                u = gf[rows.start + k : rows.stop + k, cols] * wide(mask[k - 1, rows])
                total = total + u * taps[k]
                totals[k] = totals[k] + rows8(cin * u)
            gc_ref[rows, cols] = total.astype(BF16)
        for k in range(KERNEL + 1):
            dtaps_ref[8 * k : 8 * k + 8, cols] += totals[k]
        return 0

    lax.fori_loop(0, CT, conv_group, 0)

    if remote:

        @pl.when(turn == last_turn)
        def _():
            for end in ends:
                end()


OUT_CHUNKS, GATE_CHUNKS = 4, 4
OUT_COLS, GATE_COLS = D // OUT_CHUNKS, D_INNER // GATE_CHUNKS
BWD_PACE = (0, 4, 8, 10, 12, 14, 16, 18, 20)
OUT_SLOTS, GATE_SLOTS = (0, 3, 6, 9), (1, 4, 7, 11)
TOKEN_PACE = (0, 2, 4, 6, 7, 8, 9, 10, 11)


def gate_out_plan(refs):
    ins, outs, scratch = 14, 3, 28
    head, rest = refs[:ins], refs[ins:]
    (grad_out, grad_gate), rest = rest[:2], rest[2:]
    mid, rest = rest[:outs], rest[outs:]
    (out_total, gate_total), rest = rest[:2], rest[2:]
    tail, rest = rest[:scratch], rest[scratch:]
    out_bufs, gate_bufs, sems = rest[:BUFFERS], rest[BUFFERS : 2 * BUFFERS], rest[2 * BUFFERS :]
    out_starts = [OUT_COLS * n for n in range(OUT_CHUNKS)]
    gate_starts = [GATE_COLS * n for n in range(GATE_CHUNKS)]
    out_ticks, out_ends = reduce_plan(
        [grad_out.at[:, :, :, pl.ds(start, OUT_COLS)] for start in out_starts], out_starts, OUT_SLOTS, BWD_PACE, out_bufs,
        out_total, sems, 0, [True] * OUT_CHUNKS,
    )
    gate_ticks, gate_ends = reduce_plan(
        [grad_gate.at[:, :, :, pl.ds(start, GATE_COLS)] for start in gate_starts], gate_starts, GATE_SLOTS, BWD_PACE,
        gate_bufs, gate_total, sems, OUT_CHUNKS, [False] * GATE_CHUNKS,
    )
    return out_ticks + gate_ticks, out_ends + gate_ends, (*head, *mid, *tail)


def reduce_sems(count):
    return [
        pltpu.SemaphoreType.DMA((count,)),
        pltpu.SemaphoreType.DMA((count,)),
        pltpu.SemaphoreType.DMA((count, 8)),
        pltpu.SemaphoreType.DMA((count, 8)),
    ]


def bwd_call(xs_bc, sraw, segb, seg, gy, states, rsum, dsilu, cin, hv, skip, taps, grad_out=None, grad_gate=None):
    remote = grad_out is not None
    hbm = pl.BlockSpec(memory_space=pl.ANY)
    length = gy.shape[0]
    blocks = length // T
    tokens = lambda b: (blocks - 1 - b, 0)
    third = lambda b: (blocks - 1 - b, 0, 0)
    fixed = lambda b: (0, 0)
    return pl.pallas_call(
        functools.partial(bwd_kernel, remote),
        grid=(blocks,),
        in_specs=[
            pl.BlockSpec((T, D_INNER), tokens),
            pl.BlockSpec((T, 2 * NSTATE), lambda b: (blocks - 1 - b, D_INNER // (2 * NSTATE))),
            pl.BlockSpec((T, LANES), tokens),
            pl.BlockSpec((T, LANES), tokens),
            pl.BlockSpec((1, T), lambda b: (0, blocks - 1 - b)),
            pl.BlockSpec((8, LANES), lambda b: (jnp.maximum((blocks - 1 - b) * (T // 8) - 1, 0), 0)),
            pl.BlockSpec((T, D_INNER), tokens),
            pl.BlockSpec((1, NSTATE, D_INNER), third),
            pl.BlockSpec((T, LANES), tokens),
            pl.BlockSpec((T, CONV_CH), tokens),
            pl.BlockSpec((T, CONV_CH), tokens),
            whole(hv.shape),
            whole(skip.shape),
            whole(taps.shape),
            *([hbm] * 2 if remote else []),
        ],
        out_specs=[
            pl.BlockSpec((T, CONV_CH + LANES), tokens),
            pl.BlockSpec((8 * (KERNEL + 1), CONV_CH), fixed),
            pl.BlockSpec((16, LANES), fixed),
            *([hbm] * 2 if remote else []),
        ],
        out_shape=[
            jax.ShapeDtypeStruct((length, CONV_CH + LANES), BF16),
            jax.ShapeDtypeStruct((8 * (KERNEL + 1), CONV_CH), F32),
            jax.ShapeDtypeStruct((16, LANES), F32),
            *([jax.ShapeDtypeStruct(g.shape[2:], BF16) for g in (grad_out, grad_gate)] if remote else []),
        ],
        scratch_shapes=[
            pltpu.VMEM((NSTATE, D_INNER), F32),
            pltpu.VMEM((H, T, LANES), F32),
            pltpu.VMEM((2 * LANES, D_INNER), BF16),
            pltpu.VMEM((2, T, HPT * T), BF16),
            pltpu.VMEM((LANES, T), F32),
            pltpu.VMEM((T + 8, CONV_CH), F32),
            pltpu.VMEM((T, T), F32),
            pltpu.VMEM((T, D_INNER), BF16),
            pltpu.VMEM((T, D_INNER), BF16),
            pltpu.VMEM((T, D_INNER), F32),
            pltpu.VMEM((8, D_INNER), F32),
            pltpu.VMEM((2, HPT * T, W), BF16),
            pltpu.VMEM((2, HPT * T, W), BF16),
            pltpu.VMEM((2, HPT * T, T), F32),
            pltpu.VMEM((2, T, W), F32),
            pltpu.VMEM((T, T), BF16),
            pltpu.VMEM((2, T, W), BF16),
            pltpu.VMEM((2, T, W), BF16),
            pltpu.VMEM((2, T, W), BF16),
            pltpu.VMEM((2, T, W), BF16),
            pltpu.VMEM((D_INNER, LANES), BF16),
            pltpu.VMEM((T + 8, LANES), F32),
            pltpu.VMEM((KERNEL - 1, T, LANES), F32),
            pltpu.VMEM((T, LANES), F32),
            pltpu.VMEM((T, LANES), F32),
            pltpu.VMEM((T, D_INNER), F32),
            pltpu.VMEM((T, D_INNER), F32),
            pltpu.VMEM((T, D_INNER), F32),
            *(
                reduce_buffers(grad_out.shape[2], OUT_COLS, OUT_CHUNKS)
                + reduce_buffers(D // 4, GATE_COLS, GATE_CHUNKS)
                + reduce_sems(OUT_CHUNKS + GATE_CHUNKS)
                if remote
                else []
            ),
        ],
        compiler_params=pltpu.CompilerParams(
            vmem_limit_bytes=VMEM_LIMIT, **(dict(collective_id=1, has_side_effects=True) if remote else {})
        ),
        cost_estimate=pl.CostEstimate(flops=2 * length * D * D_INNER * 4, bytes_accessed=30 << 20, transcendentals=0),
    )(xs_bc, xs_bc, sraw, segb, seg, segb, gy, states, rsum, dsilu, cin, hv, skip, taps, *((grad_out, grad_gate) if remote else ()))


CONV_COLS = 2 * W
CONV_CHUNKS = (CONV_CH + LANES) // CONV_COLS
CONV_DONE = CONV_CHUNKS * CONV_COLS
CONV_LEFT = CONV_CH + LANES - CONV_DONE


def token_kernel(remote, *refs):
    (gg_ref, gc_ref, wg_hbm, wc_hbm, tok_ref, vec_ref, taps_sum, vec_sum), refs = refs[:8], refs[8:]
    if remote:
        (nrm_hbm, gc_hbm), refs = refs[:2], refs[2:]
        (tg_ref, small_total, conv_total), refs = refs[:3], refs[3:]
    else:
        (tg_ref, small_total), refs = refs[:2], refs[2:]
    (wg, wc, grad, dpre, small, load_sems), refs = refs[:6], refs[6:]
    turn = pl.program_id(0)
    last_turn = pl.num_programs(0) - 1
    loads = [
        pltpu.make_async_copy(wg_hbm, wg, load_sems.at[0]),
        pltpu.make_async_copy(wc_hbm, wc, load_sems.at[1]),
    ]
    pieces = D // CONV_COLS
    slots = {}
    if remote:
        conv_bufs, step_bufs, refs = refs[:BUFFERS], refs[BUFFERS : 2 * BUFFERS], refs[2 * BUFFERS :]
        small_bufs, refs = refs[:9], refs[9:]
        sems, small_sems = refs[:9], refs[9:]
        (nrm, turned, gc_all, parts_ref, last_part), sems = sems[:5], sems[5:]
        loads += [
            pltpu.make_async_copy(nrm_hbm, nrm, load_sems.at[2]),
            pltpu.make_async_copy(gc_hbm, gc_all, load_sems.at[3]),
        ]
        starts = [CONV_COLS * n for n in range(CONV_CHUNKS)] + [CONV_DONE]
        chunk_refs = [parts_ref.at[n] for n in range(CONV_CHUNKS)] + [last_part.at[0]]

        def product(n):
            def action():
                cols = slice(starts[n], starts[n] + chunk_refs[n].shape[-1])
                for b in range(4):
                    left = turned[b * (D // 4) : (b + 1) * (D // 4)]
                    chunk_refs[n][b // 2, b % 2] = dot_nn(left, gc_all[:, cols]).astype(BF16)

            return action

        products = [(n, product(n)) for n in range(CONV_CHUNKS + 1)]
        ticks, ends = reduce_plan(
            chunk_refs[:-1], starts, range(CONV_CHUNKS), TOKEN_PACE, conv_bufs, conv_total, sems, 0,
            [n % 2 == 0 for n in range(CONV_CHUNKS)],
        )
        more, more_ends = reduce_plan(
            chunk_refs[-1:], [CONV_DONE], [CONV_CHUNKS], TOKEN_PACE, step_bufs, conv_total, sems, CONV_CHUNKS, [True]
        )
        done = 4 * pieces
        last, last_ends = small_plan(small, small_bufs, small_total, small_sems, done, 1)
        slots = by_slot(products + ticks + more + last)
        ends = ends + more_ends + last_ends

    @pl.when(turn == 0)
    def _():
        for load in reversed(loads):
            load.start()
        dpre[...] = jnp.zeros_like(dpre)
        if remote:
            loads[2].wait()
            for b in range(4):
                at = slice(b * (D // 4), (b + 1) * (D // 4))
                turned[at] = nrm[:, at].T
            loads[3].wait()
            greet(range(5))
            for action in slots.pop(0):
                action()
        for load in loads[:2]:
            load.wait()

    def piece(q, _):
        rows = tile_at(q, CONV_COLS)
        grad[:, rows] = dot_nt(gg_ref[...], wg[rows, :]) + dot_nt(gc_ref[...], wc[rows, :])
        for slot, actions in slots.items():
            if slot < 4 * pieces:

                @pl.when(turn * pieces + q == slot)
                def _():
                    for action in actions:
                        action()

        return 0

    lax.fori_loop(0, pieces, piece, 0)
    gain = vec_ref[0:1, :D]
    total = jnp.zeros((8, D), F32)
    step = 16
    for r in range(0, T, step):
        rows = slice(r, r + step)
        tok = tok_ref[rows].astype(F32)
        rho = lax.rsqrt(jnp.sum(tok * tok, axis=1, keepdims=True) * (1.0 / D) + EPSILON)
        unit = tok * rho
        g = grad[rows]
        total = total + rows8(g * unit)
        e = g * gain
        mean = jnp.sum(e * unit, axis=1, keepdims=True) * (1.0 / D)
        tg_ref[rows] = (rho * (e - unit * mean)).astype(BF16)
    dpre[...] += total

    @pl.when(turn == last_turn)
    def _():
        vec_sum_all = vec_sum[0:1, :]
        pre = jnp.sum(dpre[...], axis=0, keepdims=True)
        vec_all = jnp.concatenate([pre, vec_sum_all[:, D:]], axis=1)
        parts = small.shape[0] * small.shape[1] if remote else small.shape[0]
        n, m = CONV_CH // parts, VEC // parts
        small[...] = jnp.zeros_like(small)
        for p in range(parts):
            at = (p // 2, p % 2) if remote else (p,)
            small[(*at, slice(0, KERNEL), slice(0, n))] = taps_sum[0:KERNEL, n * p : n * (p + 1)]
            small[(*at, slice(KERNEL, KERNEL + 1), slice(0, m))] = vec_all[:, m * p : m * (p + 1)]
        if remote:
            for slot in sorted(slots):
                if slot >= 4 * pieces:
                    for action in slots[slot]:
                        action()
            for end in ends:
                end()
        else:
            small_total[...] = small[...]


def token_call(gg, gc, wg, wc, tok, vec, taps_sum, vec_sum, parts, nrm=None):
    remote = nrm is not None
    length = tok.shape[0]
    tokens = lambda b: (b, 0)
    hbm = pl.BlockSpec(memory_space=pl.ANY)
    small = (2, 2, SMALL_ROWS, SMALL_COLS) if remote else (parts, SMALL_ROWS, SMALL_COLS)
    small_out = small[2:] if remote else small
    zeros = (0,) * len(small_out)
    return pl.pallas_call(
        functools.partial(token_kernel, remote),
        grid=(length // T,),
        in_specs=[
            pl.BlockSpec((T, D_INNER), tokens),
            pl.BlockSpec((T, CONV_CH + LANES), tokens),
            hbm,
            hbm,
            pl.BlockSpec((T, D), tokens),
            whole(vec.shape),
            whole(taps_sum.shape),
            whole(vec_sum.shape),
            *([hbm, hbm] if remote else []),
        ],
        out_specs=[
            pl.BlockSpec((T, D), tokens),
            pl.BlockSpec(small_out, lambda b: zeros),
            *([hbm] if remote else []),
        ],
        out_shape=[
            jax.ShapeDtypeStruct((length, D), BF16),
            jax.ShapeDtypeStruct(small_out, F32),
            *([jax.ShapeDtypeStruct((D // 4, CONV_CH + LANES), BF16)] if remote else []),
        ],
        scratch_shapes=[
            pltpu.VMEM(wg.shape, BF16),
            pltpu.VMEM(wc.shape, BF16),
            pltpu.VMEM((T, D), F32),
            pltpu.VMEM((8, D), F32),
            pltpu.VMEM(small, F32),
            pltpu.SemaphoreType.DMA((4,)),
            *(
                reduce_buffers(D // 4, CONV_COLS, CONV_CHUNKS)
                + reduce_buffers(D // 4, CONV_LEFT, 1)
                + small_buffers(SMALL_ROWS, SMALL_COLS)
                + [
                    pltpu.VMEM(nrm.shape, BF16),
                    pltpu.VMEM((D, length), BF16),
                    pltpu.VMEM(gc.shape, BF16),
                    pltpu.VMEM((CONV_CHUNKS, 2, 2, D // 4, CONV_COLS), BF16),
                    pltpu.VMEM((1, 2, 2, D // 4, CONV_LEFT), BF16),
                ]
                + reduce_sems(CONV_CHUNKS + 1)
                + [pltpu.SemaphoreType.DMA((5,)), pltpu.SemaphoreType.DMA((5,))]
                if remote
                else []
            ),
        ],
        compiler_params=pltpu.CompilerParams(
            vmem_limit_bytes=VMEM_LIMIT, **(dict(collective_id=2, has_side_effects=True) if remote else {})
        ),
        cost_estimate=pl.CostEstimate(flops=2 * length * D * 4480, bytes_accessed=22 << 20, transcendentals=0),
    )(gg, gc, wg, wc, tok, vec, taps_sum, vec_sum, *((nrm, gc) if remote else ()))


FIRST_FIX = 1.0 / (1.0 - BETA_FIRST**STEP)
SECOND_FIX = 1.0 / (1.0 - BETA_SECOND**STEP)


def adam_step(master, first, second, grad, rate):
    first_new = BETA_FIRST * first + (1.0 - BETA_FIRST) * grad
    second_new = BETA_SECOND * second + (1.0 - BETA_SECOND) * grad * grad
    step = (rate * FIRST_FIX) * first_new / (jnp.sqrt(second_new * SECOND_FIX) + ADAM_EPSILON)
    return ((1.0 - rate * WEIGHT_DECAY) * master - step, first_new, second_new)


def adam_rows(rate, grad, refs, at):
    ins, outs = refs
    for ref, value in zip(outs, adam_step(*(r[at] for r in ins), grad, rate)):
        ref[at] = value


def adam_turned_kernel(rate, tiles, first_ref, second_ref, *refs):
    *refs, turned = refs
    j = pl.program_id(0)
    for which, grad_ref in enumerate((first_ref, second_ref)):

        @pl.when((j >= tiles) == bool(which))
        def _():
            for r in range(0, 2 * W, LANES):
                turned[r : r + LANES] = grad_ref[:, r : r + LANES].astype(F32).T

    for r in range(0, 2 * W, CHUNK):
        at = slice(r, r + CHUNK)
        adam_rows(rate, turned[at], (refs[:3], refs[3:]), at)


def adam_kernel(rate, grad_ref, *refs):
    rows, cols = refs[0].shape
    for r in range(0, rows, CHUNK):
        for c in range(0, cols, W):
            at = (slice(r, r + CHUNK), slice(c, c + W))
            adam_rows(rate, grad_ref[at].astype(F32), (refs[:3], refs[3:]), at)


def adam_call(grads, master, first, second, rate):
    rows, cols = master.shape
    if len(grads) == 2:
        tile = 2 * W
        tiles = grads[0].shape[1] // tile
        kernel = functools.partial(adam_turned_kernel, rate, tiles)
        grad_specs = [
            pl.BlockSpec((cols, tile), lambda j: (0, jnp.minimum(j, tiles - 1))),
            pl.BlockSpec((cols, tile), lambda j: (0, jnp.maximum(j - tiles, 0))),
        ]
    else:
        tile = rows // 4
        kernel = functools.partial(adam_kernel, rate)
        grad_specs = [pl.BlockSpec((tile, cols), lambda j: (j, 0))]
    down = pl.BlockSpec((tile, cols), lambda j: (j, 0))
    scratch = [pltpu.VMEM((tile, cols), F32)] if len(grads) == 2 else []
    return pl.pallas_call(
        kernel,
        grid=(-(-rows // tile),),
        in_specs=[*grad_specs, down, down, down],
        out_specs=[down] * 3,
        out_shape=[jax.ShapeDtypeStruct((rows, cols), F32)] * 3,
        scratch_shapes=scratch,
        compiler_params=pltpu.CompilerParams(vmem_limit_bytes=VMEM_LIMIT),
        cost_estimate=pl.CostEstimate(flops=0, bytes_accessed=26 * rows * cols, transcendentals=0),
    )(*grads, master, first, second)


def owners(grad, parts, remote):
    return grad.reshape(*((2, 2) if remote else (parts,)), -1, grad.shape[1])


def row_pass(projected, tok, cot, seg, wg, wc, wo, parts, remote):
    act, dsilu, cin, y, states, sraw, nrm, segb, taps, vec, hv, skip = projected
    block_out, mixed, gy, gg, rsum, dgain, dskip = fwd_call(act, y, nrm, tok, cot, wg, wo, vec, skip)
    grad_out = owners(dot_tn(mixed, cot).astype(BF16), parts, remote)
    grad_gate = owners(dot_tn(nrm, gg).astype(BF16), parts, remote)
    gc, dtaps, dhv, *totals = bwd_call(
        act, sraw, segb, seg, gy, states, rsum, dsilu, cin, hv, skip, taps, *((grad_out, grad_gate) if remote else ())
    )
    dtaps = dtaps.reshape(KERNEL + 1, 8, CONV_CH).sum(1)
    dhv = dhv.reshape(2, 8, LANES).sum(1)
    vec_sum = jnp.concatenate(
        [
            jnp.zeros((D,), F32),
            dgain.sum(0),
            dtaps[KERNEL],
            dhv[0, :H],
            dhv[1, :H],
            dskip.sum(0).reshape(H, P_SIZE).sum(1),
            jnp.zeros((VEC_PAD - VEC,), F32),
        ]
    )[None]
    branch_grad, small, *conv_total = token_call(
        gg, gc, wg, wc, tok, vec, dtaps, vec_sum, parts, *((nrm,) if remote else ())
    )
    token_grad = cot.astype(F32) + branch_grad.astype(F32)
    if remote:
        out_total, gate_total = totals
        return block_out, token_grad, gate_total, conv_total[0], out_total, small
    grad_conv = owners(dot_tn(nrm, gc).astype(BF16), parts, remote)
    return block_out, token_grad, grad_gate, grad_conv, grad_out, small


def local(
    tokens, cotangent, segment_ids, in_weight, out_weight, filter_weight, vectors,
    in_first, out_first, filter_first, vector_first, in_second, out_second, filter_second, vector_second,
):
    remote = lax.axis_size("grp") == 4 and lax.axis_size("dp") == 8
    parts = D // in_weight.shape[0]
    vec_size = vectors.size
    in_turned = in_weight.T
    small = jnp.pad(filter_weight, ((0, 12), (0, SMALL_COLS - filter_weight.shape[1])))
    small = small.at[8, :vec_size].set(vectors)
    tok, cot = tokens[0], cotangent[0]
    if remote:
        *projected, wg, wc, wo = project_call(tok, segment_ids, in_turned, out_weight, small)
    else:
        in_full = lax.all_gather(in_weight.astype(BF16), "grp", axis=0, tiled=True)
        wo = lax.all_gather(out_weight.astype(BF16), "grp", axis=0, tiled=True)
        slots = lax.all_gather(small, "grp")
        wg = in_full[:, :D_INNER]
        wc = jnp.pad(in_full[:, D_INNER:], ((0, 0), (0, LANES - H)))
        projected = plain_project_call(tok, segment_ids, wc, slots)
    block_out, token_grad, *grads = row_pass(projected, tok, cot, segment_ids, wg, wc, wo, parts, remote)
    if not remote:
        grads = [lax.psum(lax.psum_scatter(g, "grp", scatter_dimension=0, tiled=False), "dp") for g in grads]
    gate_total, conv_total, out_total, small_total = grads
    in_new = [a.T for a in adam_call((gate_total, conv_total), in_turned, in_first.T, in_second.T, 0.03)]
    out_new = adam_call((out_total,), out_weight, out_first, out_second, 0.02)
    filter_new = adam_step(
        filter_weight, filter_first, filter_second, small_total[:KERNEL, : filter_weight.shape[1]], 0.3
    )
    vector_new = adam_step(vectors, vector_first, vector_second, small_total[KERNEL, :vec_size], 0.3)
    results = (in_new, out_new, filter_new, vector_new)
    return (block_out[None], token_grad[None], *(r[n] for n in range(3) for r in results))


def solution(mesh):
    rows = P(("grp", "dp"), None, None)
    shards = (P("grp", None), P("grp", None), P(None, "grp"), P("grp"))
    in_specs = (rows, rows, P(("grp", "dp"), None)) + shards * 3
    out_specs = (rows, rows) + shards * 3
    return jax.shard_map(local, mesh=mesh, in_specs=in_specs, out_specs=out_specs, check_vma=False)
```
